32 devices in a mesh: leaf: 8 (over z, core), list: 4 (over y, x).
Axes of the slice: x: 2, y: 2, z: 4, core: 2. Of those that a mesh axis runs over, the one named last changes fastest.
Arguments:
- panel_charges: bfloat16 [512, 64, 256], P(('leaf', 'list')), may hold values from -6 to 6
- leaf_basis: bfloat16 [512, 64, 256], P(('leaf', 'list')), may hold values from -0.375 to 0.375
- near_blocks: bfloat16 [512, 4, 256, 256], P(('leaf', 'list')), may hold values from -0.1875 to 0.1875
- near_list: int32 [512, 4], P(('leaf', 'list')), may hold values from 0 to 15, as said below
- far_list: int32 [512, 8], P(('leaf', 'list')), may hold values from 0 to 63, as said below
- far_count: int32 [512], P(('leaf', 'list')), may hold values from 1 to 8, as said below
- far_coupling: bfloat16 [512, 8, 64, 64], P(('leaf', 'list')), may hold values from -0.25 to 0.25
- leaf_transfer: float32 [512, 64, 64], P(('leaf', 'list')), may hold values from -0.4375 to 0.4375
- device_transfer: float32 [8, 4, 64, 64], P('leaf', 'list'), may hold values from -0.375 to 0.375
- tree_transfer: float32 [8, 64, 64], replicated, may hold values from -0.75 to 0.75
- level_coupling: float32 [12, 4, 64, 64], replicated, may hold values from -0.4375 to 0.4375
Outputs:
- potential: bfloat16 [512, 64, 256], P(('leaf', 'list'))
The draws below stay inside these ranges and needn't reach their ends.
Inputs may be any that keep to these rules, and one draw needn't show every extreme that they name: `far_list`: each row names 8 different leaves of the leaf's group subtree, none on the leaf's own device; the 16 leaves of one device name, over all their slots, exactly 8 different leaves of each other device of the group. Slots at and after far_count[c] are unused. `near_list`: each row names 4 different leaves of the leaf's own device, the first being the leaf itself.
All inputs are finite; a program needn't handle non-finite values.
Results may differ from the reference program's by a relative error of at most 0.0053.
Values may be sent and summed in bfloat16 or wider, within the bound.
No kernel may reach another device: no remote copies, remote signals or barrier semaphores. Data moves between devices by JAX's collectives and lax.ppermute only.
A program may use at most 64 MiB of HBM per device.

```python
import jax
import jax.numpy as jnp
from jax import lax

M = 256
K = 64
R = 64
LEAF_DEV = 16
NFAR = 8
NNEAR = 4
LEAVES = 512
GROUP = 64
PEER_MOST = 8
TREE_NODES = 8
LEVEL_NODES = 12
N_LEAF = 8
N_LIST = 4


def draw_far_list(key, part):
    block_count = LEAVES // LEAF_DEV
    peer_total = N_LIST - 1
    choose = PEER_MOST
    candidates_count = peer_total * choose
    key_subset = jax.random.fold_in(key, 21)
    key_order = jax.random.fold_in(key, 22)
    column = jnp.arange(LEAF_DEV, dtype=jnp.int32)
    scores = jax.random.randint(key_subset, (block_count, peer_total, LEAF_DEV), 0, 1 << 20, dtype=jnp.int32) * LEAF_DEV + column[None, None, :]
    subset = lax.top_k(scores, choose)[1].astype(jnp.int32)
    own_device = jnp.arange(block_count, dtype=jnp.int32) % N_LIST
    step_ids = jnp.arange(peer_total, dtype=jnp.int32)
    peers = (own_device[:, None] + 1 + step_ids[None, :]) % N_LIST
    candidates = (peers[:, :, None] * LEAF_DEV + subset).reshape(block_count, candidates_count)
    order_scores = jax.random.randint(key_order, (block_count, candidates_count), 0, 1 << 20, dtype=jnp.int32) * candidates_count + jnp.arange(candidates_count, dtype=jnp.int32)[None, :]
    order = jnp.argsort(order_scores, axis=1, stable=True).astype(jnp.int32)
    places = ((jnp.arange(LEAF_DEV, dtype=jnp.int32)[:, None] * NFAR + jnp.arange(NFAR, dtype=jnp.int32)[None, :]) % candidates_count).reshape(-1)
    picked_order = jnp.take(order, places, axis=1)
    result = jnp.take_along_axis(candidates, picked_order, axis=1)
    return result.reshape(LEAVES, NFAR).astype(jnp.int32)


def draw_far_count(key, part):
    block_count = LEAVES // LEAF_DEV
    key_cap = jax.random.fold_in(key, 11)
    key_pick = jax.random.fold_in(key, 12)
    key_each = jax.random.fold_in(key, 13)
    key_spot = jax.random.fold_in(key, 14)
    lowest = max(1, NFAR // 4)
    ceiling = jax.random.randint(key_cap, (block_count,), lowest, NFAR + 1, dtype=jnp.int32)
    chosen = jax.random.randint(key_pick, (), 0, block_count, dtype=jnp.int32)
    ceiling = jnp.where(jnp.arange(block_count, dtype=jnp.int32) == chosen, NFAR, ceiling)
    counts = jax.random.randint(key_each, (block_count, LEAF_DEV), 0, 1 << 20, dtype=jnp.int32) % ceiling[:, None] + 1
    position = jax.random.randint(key_spot, (block_count,), 0, LEAF_DEV, dtype=jnp.int32)
    counts = jnp.where(jnp.arange(LEAF_DEV, dtype=jnp.int32)[None, :] == position[:, None], ceiling[:, None], counts)
    return counts.reshape(LEAVES).astype(jnp.int32)


def draw_near_list(key, part):
    column = jnp.arange(LEAF_DEV, dtype=jnp.int32)
    local_ids = jnp.arange(LEAVES, dtype=jnp.int32) % LEAF_DEV
    scores = jax.random.randint(key, (LEAVES, LEAF_DEV), 0, 1 << 20, dtype=jnp.int32) * LEAF_DEV + column[None, :]
    scores = jnp.where(column[None, :] == local_ids[:, None], 1 << 30, scores)
    return lax.top_k(scores, NNEAR)[1].astype(jnp.int32)


def block_scale(rng, extent, cuts, low, top_value):
    def one(dim, shards_of):
        heights = jax.random.uniform(jax.random.fold_in(jax.random.fold_in(rng, 6), dim), (shards_of,), jnp.float32, low / len(cuts), top_value / len(cuts))
        return jnp.repeat(jnp.exp(heights), extent[dim] // shards_of).reshape((-1,) + (1,) * (len(extent) - dim - 1))

    gain = one(*cuts[0])
    for cut in cuts[1:]:
        gain = gain * one(*cut)
    return gain


def centred(rng, dims, width, most, cuts=(), kind=jnp.bfloat16):
    values = width * jax.random.normal(rng, dims, jnp.float32)
    if cuts:
        values = values * block_scale(rng, dims, cuts, -0.22, 0.18)
    return jnp.clip(values, -most, most).astype(kind)


def setup_inputs(seed: int = 0) -> dict:
    key_list = jax.random.split(jax.random.key(seed), 12)
    panel_charges = centred(key_list[0], (LEAVES, R, M), 1.0, 6.0, ((0, 32),))
    leaf_basis = centred(key_list[1], (LEAVES, K, M), M ** -0.5, 0.375, ((0, 32),))
    near_blocks = centred(key_list[2], (LEAVES, NNEAR, M, M), (M * NNEAR) ** -0.5, 0.1875, ((0, 32),))
    near_list = draw_near_list(jax.random.fold_in(key_list[11], 71), 0)
    far_list = draw_far_list(jax.random.fold_in(key_list[11], 71), 0)
    far_count = draw_far_count(jax.random.fold_in(key_list[11], 71), 0)
    far_coupling = centred(key_list[6], (LEAVES, NFAR, K, K), (K * NFAR) ** -0.5, 0.25, ((0, 32),))
    leaf_transfer = centred(key_list[7], (LEAVES, K, K), (3 * K) ** -0.5, 0.4375, ((0, 32),), jnp.float32)
    device_transfer = centred(key_list[8], (N_LEAF, N_LIST, K, K), (4 * K) ** -0.5, 0.375, ((0, 8), (1, 4)), jnp.float32)
    tree_transfer = centred(key_list[9], (TREE_NODES, K, K), K ** -0.5, 0.75, (), jnp.float32)
    level_coupling = centred(key_list[10], (LEVEL_NODES, 4, K, K), (3 * K) ** -0.5, 0.4375, (), jnp.float32)
    return dict(panel_charges=panel_charges, leaf_basis=leaf_basis, near_blocks=near_blocks, near_list=near_list, far_list=far_list, far_count=far_count, far_coupling=far_coupling, leaf_transfer=leaf_transfer, device_transfer=device_transfer, tree_transfer=tree_transfer, level_coupling=level_coupling)


highest = lax.Precision.HIGHEST
offsets = (-3, -2, 2, 3)


def upper_tree(group_nodes, tree_transfer, level_coupling):
    depth = N_LEAF.bit_length() - 2
    nodes = [group_nodes]
    for height in range(depth - 1):
        current = nodes[-1]
        members = current.shape[0]
        begin_row = 2 * N_LEAF - 2 * members
        product = jnp.einsum('qrb,qba->qra', current, tree_transfer[begin_row:begin_row + members], precision=highest)
        nodes.append(product[0::2] + product[1::2])
    coupled = []
    for height in range(depth):
        current = nodes[height]
        members = current.shape[0]
        begin_row = 2 * N_LEAF - 2 * members
        matrices = level_coupling[begin_row:begin_row + members]
        padded = jnp.pad(current, ((3, 3), (0, 0), (0, 0)))
        parity = jnp.arange(members) % 2
        summed = jnp.zeros_like(current)
        for slot_index, offset in enumerate(offsets):
            source = padded[3 + offset:3 + offset + members]
            contribution = jnp.einsum('qrb,qab->qra', source, matrices[:, slot_index], precision=highest)
            if offset == 3:
                usable = parity == 0
            elif offset == -3:
                usable = parity == 1
            else:
                usable = parity >= 0
            summed = summed + jnp.where(usable[:, None, None], contribution, jnp.zeros((), jnp.float32))
        coupled.append(summed)
    result = coupled[-1]
    for height in reversed(range(depth - 1)):
        members = coupled[height].shape[0]
        begin_row = 2 * N_LEAF - 2 * members
        parent = jnp.repeat(result, 2, axis=0)
        result = coupled[height] + jnp.einsum('qrp,qcp->qrc', parent, tree_transfer[begin_row:begin_row + members], precision=highest)
    return result


def reference(panel_charges, leaf_basis, near_blocks, near_list, far_list, far_count, far_coupling, leaf_transfer, device_transfer, tree_transfer, level_coupling):
    skeleton = jnp.einsum('crm,ckm->crk', panel_charges.astype(jnp.float32), leaf_basis.astype(jnp.float32)).astype(jnp.bfloat16)
    shaped = skeleton.astype(jnp.float32).reshape(N_LEAF, N_LIST, LEAF_DEV, R, K)
    transfer = leaf_transfer.reshape(N_LEAF, N_LIST, LEAF_DEV, K, K)
    device_nodes = jnp.einsum('ljirb,ljiba->ljra', shaped, transfer, precision=highest)
    group_nodes = jnp.einsum('ljrb,ljba->lra', device_nodes, device_transfer, precision=highest)
    top_down = upper_tree(group_nodes, tree_transfer, level_coupling)
    device_down = jnp.einsum('lrp,ljdp->ljrd', top_down, device_transfer, precision=highest)
    from_above = jnp.einsum('ljrd,ljiad->ljira', device_down, transfer, precision=highest).reshape(LEAVES, R, K)
    leaf_ids = jnp.arange(LEAVES, dtype=jnp.int32)
    sources = (leaf_ids // GROUP * GROUP)[:, None] + far_list.astype(jnp.int32)
    usable = jnp.arange(NFAR, dtype=jnp.int32)[None, :] < far_count[:, None]
    picked = jnp.where(usable[:, :, None, None], skeleton[sources], jnp.zeros((), jnp.bfloat16))
    leaf_coupled = jnp.einsum('ckrb,ckab->cra', picked.astype(jnp.float32), far_coupling.astype(jnp.float32))
    coefficients = (leaf_coupled + from_above).astype(jnp.bfloat16)
    far_field = jnp.einsum('crk,ckm->crm', coefficients.astype(jnp.float32), leaf_basis.astype(jnp.float32))
    block_count = LEAVES // LEAF_DEV

    def near_block(inputs):
        charges, blocks, neighbours = inputs
        gathered = charges[neighbours].astype(jnp.float32)
        return jnp.einsum('ckrm,cknm->crn', gathered, blocks.astype(jnp.float32))

    near_field = lax.map(near_block, (panel_charges.reshape(block_count, LEAF_DEV, R, M), near_blocks.reshape(block_count, LEAF_DEV, NNEAR, M, M), near_list.reshape(block_count, LEAF_DEV, NNEAR))).reshape(LEAVES, R, M)
    return (far_field + near_field).astype(jnp.bfloat16)
```

```python
import functools

import jax
import jax.numpy as jnp
from jax import lax
from jax.experimental import pallas as pl
from jax.experimental.pallas import tpu as pltpu
from jax.sharding import PartitionSpec as P

highest = lax.Precision.HIGHEST
offsets = (-3, -2, 2, 3)
f32 = jnp.float32
bf16 = jnp.bfloat16
whole = pl.BlockSpec(memory_space=pltpu.VMEM)
scalars = pl.BlockSpec(memory_space=pltpu.SMEM)


def params(mebibytes):
    return pltpu.CompilerParams(vmem_limit_bytes=mebibytes << 20)


def times(left, right):
    return lax.dot_general(left, right, (((1,), (0,)), ((), ())), preferred_element_type=f32)


def times_transposed(left, right):
    return lax.dot_general(left, right, (((1,), (1,)), ((), ())), preferred_element_type=f32)


def split(array):
    high = array.astype(bf16)
    return high, (array - high.astype(f32)).astype(bf16)


def exact(product, left, right):
    left_high, left_low = split(left)
    right_high, right_low = split(right)
    return product(left_high, right_high) + (
        product(left_low, right_high) + product(left_high, right_low)
    )


def upward_kernel(charges, basis, transfer, device_transfer, payload):
    pair_count = charges.shape[0] // 2
    rank = basis.shape[1]
    node = jnp.zeros((charges.shape[1], rank), f32)
    for pair in range(pair_count):
        halves = [
            times_transposed(charges[leaf], basis[leaf]).astype(bf16)
            for leaf in (2 * pair, 2 * pair + 1)
        ]
        skeleton = jnp.concatenate(halves, axis=1)
        payload[pair] = skeleton
        matrix = transfer[pl.ds(2 * pair, 2)].reshape(2 * rank, rank)
        high, low = split(matrix)
        node = node + (times(skeleton, high) + times(skeleton, low))
    term = exact(times, node, device_transfer[...])
    payload[pair_count] = jnp.concatenate(split(term), axis=1)


def near_kernel(near_list, charges, blocks, near):
    step = pl.program_id(0)
    leaves, slots = blocks.shape[0], blocks.shape[1]
    for leaf in range(leaves):
        total = None
        for slot in range(slots):
            source = near_list[step * leaves + leaf, slot]
            part = times_transposed(charges[source], blocks[leaf, slot])
            total = part if total is None else total + part
        near[leaf] = total


def sum_kernel(count, *refs):
    payloads, node = refs[:count], refs[count]
    rank = node.shape[1]
    total = None
    for payload in payloads:
        both = payload[payload.shape[0] - 1].astype(f32)
        part = both[:, :rank] + both[:, rank:]
        total = part if total is None else total + part
    node[...] = total


def far_kernel(peer_count, position, far_list, far_count, *refs):
    peers = refs[:peer_count]
    coupling, coupled, table = refs[peer_count:]
    leaves, slots, rank = coupling.shape[0], coupling.shape[1], coupling.shape[2]
    pair_count = leaves // 2
    for peer in range(peer_count):
        for pair in range(pair_count):
            block = peers[peer][pair]
            first, second = block[:, :rank], block[:, rank:]
            table[peer * leaves + 2 * pair] = jnp.concatenate([first, first], axis=1)
            table[peer * leaves + 2 * pair + 1] = jnp.concatenate([second, second], axis=1)
    own = position[1]
    rows = table.shape[1]
    lower = lax.broadcasted_iota(jnp.int32, (rows, 2 * rank), 1) < rank

    def one(leaf):
        used = far_count[leaf]
        total = jnp.zeros((rows, rank), f32)
        for slot in range(0, slots, 2):
            picked = []
            for each in (slot, slot + 1):
                source = far_list[leaf, each]
                device = source // leaves
                entry = ((device ^ own) - 1) * leaves + (source - device * leaves)
                block = table[entry]
                picked.append(jnp.where(each < used, block, jnp.zeros_like(block)))
            left = jnp.where(lower, picked[0], picked[1])
            right = jnp.concatenate([coupling[leaf, slot], coupling[leaf, slot + 1]], axis=1)
            total = total + times_transposed(left, right)
        return total

    @pl.loop(0, pair_count)
    def _(pair):
        coupled[pair] = jnp.concatenate([one(2 * pair), one(2 * pair + 1)], axis=1)


def down_kernel(chip_count, position, *refs):
    own_nodes, other_nodes = refs[:chip_count], refs[chip_count : 2 * chip_count]
    tree, couplings, device_transfer, transfer, basis, coupled, near, out, pairs = refs[
        2 * chip_count :
    ]
    rank = device_transfer.shape[0]
    leaf_count = 2 * chip_count
    depth = leaf_count.bit_length() - 2
    place = position[0]
    chip, core = place // 2, place % 2
    for distance in range(chip_count):
        own, other = own_nodes[distance][...], other_nodes[distance][...]
        pairs[chip ^ distance] = jnp.where(
            core == 0,
            jnp.concatenate([own, other], axis=1),
            jnp.concatenate([other, own], axis=1),
        )
    begin, stored = 0, 0
    summed = []
    for height in range(depth):
        members = leaf_count >> height
        spot = place >> height
        if 0 < height < depth - 1:
            below = stored
            stored += members
            for pair in range(members // 2):
                halves = [
                    exact(
                        times,
                        pairs[below + each],
                        tree[pl.ds(begin - 2 * members + 2 * each, 2)].reshape(2 * rank, rank),
                    )
                    for each in (2 * pair, 2 * pair + 1)
                ]
                pairs[stored + pair] = jnp.concatenate(halves, axis=1)
        total = jnp.zeros((pairs.shape[1], rank), f32)
        for slot, offset in enumerate(offsets):
            source = spot + offset
            usable = jnp.logical_and(source >= 0, source < members)
            if abs(offset) == 3:
                usable = jnp.logical_and(usable, spot % 2 == (0 if offset > 0 else 1))
            source = jnp.clip(source, 0, members - 1)
            if 0 < height == depth - 1:
                matrix = tree[pl.ds(begin - 2 * members + 2 * source, 2)]
                node = exact(times, pairs[stored + source], matrix.reshape(2 * rank, rank))
            else:
                both = pairs[stored + source // 2]
                node = jnp.where(source % 2 == 0, both[:, :rank], both[:, rank:])
            part = exact(times_transposed, node, couplings[begin + spot, slot])
            total = total + jnp.where(usable, part, jnp.zeros_like(part))
        summed.append(total)
        begin += members
    result = summed[-1]
    for height in reversed(range(depth - 1)):
        begin_row = 2 * leaf_count - 2 * (leaf_count >> height)
        matrix = tree[begin_row + (place >> height)]
        result = summed[height] + exact(times_transposed, result, matrix)
    down = exact(times_transposed, result, device_transfer[...])
    down_high, down_low = split(down)
    for pair in range(coupled.shape[0]):
        matrix = transfer[pl.ds(2 * pair, 2)].reshape(2 * rank, rank)
        high, low = split(matrix)
        above = times_transposed(down_high, high) + (
            times_transposed(down_low, high) + times_transposed(down_high, low)
        )
        coefficients = (coupled[pair] + above).astype(bf16)
        for half in range(2):
            leaf = 2 * pair + half
            far = times(coefficients[:, half * rank : (half + 1) * rank], basis[leaf])
            out[leaf] = (far + near[leaf]).astype(bf16)


def on_device(
    panel_charges,
    leaf_basis,
    near_blocks,
    near_list,
    far_list,
    far_count,
    far_coupling,
    leaf_transfer,
    device_transfer,
    tree_transfer,
    level_coupling,
):
    leaves, rows, panels = panel_charges.shape
    rank = leaf_basis.shape[1]
    list_count, leaf_count = lax.axis_size("list"), lax.axis_size("leaf")
    chip_count = leaf_count // 2
    position = jnp.stack([lax.axis_index("leaf"), lax.axis_index("list")]).astype(jnp.int32)
    device_matrix = device_transfer[0, 0]

    payload = pl.pallas_call(
        upward_kernel,
        out_shape=jax.ShapeDtypeStruct((leaves // 2 + 1, rows, 2 * rank), bf16),
        in_specs=[whole] * 4,
        out_specs=whole,
        compiler_params=params(16),
        name="upward",
    )(panel_charges, leaf_basis, leaf_transfer, device_matrix)

    peers = [
        lax.ppermute(payload, "list", [(i, i ^ distance) for i in range(list_count)])
        for distance in range(1, list_count)
    ]

    group = 2
    near = pl.pallas_call(
        near_kernel,
        grid_spec=pltpu.PrefetchScalarGridSpec(
            num_scalar_prefetch=1,
            grid=(leaves // group,),
            in_specs=[
                pl.BlockSpec((leaves, rows, panels), lambda i, _: (0, 0, 0)),
                pl.BlockSpec((group,) + near_blocks.shape[1:], lambda i, _: (i, 0, 0, 0)),
            ],
            out_specs=pl.BlockSpec((group, rows, panels), lambda i, _: (i, 0, 0)),
        ),
        out_shape=jax.ShapeDtypeStruct((leaves, rows, panels), f32),
        compiler_params=params(16),
        cost_estimate=pl.CostEstimate(
            flops=2 * near_blocks.size * rows, bytes_accessed=2 * near_blocks.size, transcendentals=0
        ),
        name="near",
    )(near_list, panel_charges, near_blocks)

    own_node = pl.pallas_call(
        functools.partial(sum_kernel, list_count),
        out_shape=jax.ShapeDtypeStruct((rows, rank), f32),
        in_specs=[whole] * list_count,
        out_specs=whole,
        name="group_sum",
    )(payload, *peers)

    own_nodes = [own_node] + [
        lax.ppermute(own_node, "leaf", [(i, i ^ 2 * distance) for i in range(leaf_count)])
        for distance in range(1, chip_count)
    ]
    other_nodes = [
        lax.ppermute(node, "leaf", [(i, i ^ 1) for i in range(leaf_count)]) for node in own_nodes
    ]

    coupled = pl.pallas_call(
        functools.partial(far_kernel, list_count - 1),
        out_shape=jax.ShapeDtypeStruct((leaves // 2, rows, 2 * rank), f32),
        in_specs=[scalars] * 3 + [whole] * list_count,
        out_specs=whole,
        scratch_shapes=[pltpu.VMEM(((list_count - 1) * leaves, rows, 2 * rank), bf16)],
        compiler_params=params(24),
        cost_estimate=pl.CostEstimate(
            flops=2 * far_coupling.size * rows * 4,
            bytes_accessed=4 * far_coupling.size,
            transcendentals=0,
        ),
        name="far",
    )(position, far_list, far_count, *peers, far_coupling)

    return pl.pallas_call(
        functools.partial(down_kernel, chip_count),
        out_shape=jax.ShapeDtypeStruct((leaves, rows, panels), bf16),
        in_specs=[scalars] + [whole] * (2 * chip_count + 7),
        out_specs=whole,
        scratch_shapes=[pltpu.VMEM((leaf_count, rows, 2 * rank), f32)],
        compiler_params=params(32),
        name="down",
    )(
        position,
        *own_nodes,
        *other_nodes,
        tree_transfer,
        level_coupling,
        device_matrix,
        leaf_transfer,
        leaf_basis,
        coupled,
        near,
    )


def solution(mesh):
    in_specs = (
        P(("leaf", "list"), None, None),
        P(("leaf", "list"), None, None),
        P(("leaf", "list"), None, None, None),
        P(("leaf", "list"), None),
        P(("leaf", "list"), None),
        P(("leaf", "list")),
        P(("leaf", "list"), None, None, None),
        P(("leaf", "list"), None, None),
        P("leaf", "list", None, None),
        P(),
        P(),
    )
    out_specs = P(("leaf", "list"), None, None)
    return jax.shard_map(
        on_device, mesh=mesh, in_specs=in_specs, out_specs=out_specs, check_vma=False
    )
```

```python
import functools

import jax
import jax.numpy as jnp
from jax import lax
from jax.experimental import pallas as pl
from jax.experimental.pallas import tpu as pltpu
from jax.sharding import PartitionSpec as P

offsets = (-3, -2, 2, 3)
f32 = jnp.float32
bf16 = jnp.bfloat16
whole = pl.BlockSpec(memory_space=pltpu.VMEM)
scalars = pl.BlockSpec(memory_space=pltpu.SMEM)
anywhere = pl.BlockSpec(memory_space=pl.ANY)


def params(mebibytes):
    return pltpu.CompilerParams(vmem_limit_bytes=mebibytes << 20)


def times(left, right):
    return lax.dot_general(left, right, (((1,), (0,)), ((), ())), preferred_element_type=f32)


def times_transposed(left, right):
    return lax.dot_general(left, right, (((1,), (1,)), ((), ())), preferred_element_type=f32)


def split(array):
    high = array.astype(bf16)
    return high, (array - high.astype(f32)).astype(bf16)


def exact(product, left, right):
    left_high, left_low = split(left)
    right_high, right_low = split(right)
    return product(left_high, right_high) + (
        product(left_low, right_high) + product(left_high, right_low)
    )


def upward_kernel(count, *refs):
    sources, blocks_in = refs[:count], refs[count]
    payload, term_parts = refs[count + 1 : count + 3]
    kept, blocks = refs[count + 3 : count + 7], refs[count + 7]
    basis, transfer, matrix, sem = refs[count + 8 :]
    charges = kept[0]
    targets = (charges, basis, transfer, matrix) + kept[1:]
    copies = [
        pltpu.make_async_copy(source, target, sem.at[i])
        for i, (source, target) in enumerate(zip(sources, targets))
    ]
    for copy in copies:
        copy.start()
    ahead = pltpu.make_async_copy(blocks_in.at[pl.ds(0, blocks.shape[0])], blocks, sem.at[count])
    ahead.start()
    for copy in copies:
        copy.wait()
    pair_count = charges.shape[0] // 2
    rank = basis.shape[1]
    node = jnp.zeros((charges.shape[1], rank), f32)
    for pair in range(pair_count):
        halves = [
            times_transposed(charges[leaf], basis[leaf]).astype(bf16)
            for leaf in (2 * pair, 2 * pair + 1)
        ]
        skeleton = jnp.concatenate(halves, axis=1)
        payload[pair] = skeleton
        block = transfer[pl.ds(2 * pair, 2)].reshape(2 * rank, rank)
        high, low = split(block)
        node = node + (times(skeleton, high) + times(skeleton, low))
    term = exact(times, node, matrix[...])
    both = jnp.concatenate(split(term), axis=1)
    term_parts[...] = both
    payload[pair_count] = both
    ahead.wait()


def near_leaf(near_list, charges, blocks, row, leaf):
    total = None
    for slot in range(blocks.shape[1]):
        part = times_transposed(charges[near_list[slot, leaf]], blocks[row, slot])
        total = part if total is None else total + part
    return total


def near_begin_kernel(near_list, charges, blocks, near):
    for leaf in range(near.shape[0]):
        near[leaf] = near_leaf(near_list, charges, blocks, leaf, leaf)


def near_rest_kernel(sizes, near_list, charges, blocks_in, near, buffer, sem):
    count = near.shape[0]
    first = charges.shape[0] - count
    begins = [sum(sizes[:i]) for i in range(len(sizes))]
    copies = [
        pltpu.make_async_copy(
            blocks_in.at[pl.ds(first + begin, size)], buffer.at[pl.ds(begin, size)], sem.at[i]
        )
        for i, (begin, size) in enumerate(zip(begins, sizes))
    ]
    for copy in copies:
        copy.start()
    for copy, begin, size in zip(copies, begins, sizes):
        copy.wait()
        for row in range(begin, begin + size):
            near[row] = near_leaf(near_list, charges, buffer, row, first + row)


def pack_kernel(term_parts, near, payload_in, payload, terms):
    place = payload.shape[0] - 1
    payload[place] = term_parts[...]
    terms[0] = payload_in[place - 1]
    terms[1] = term_parts[...]


def sum_kernel(count, bases, *refs):
    arrays, (pair, *copies) = refs[:count], refs[count + 1 :]
    rank = pair.shape[1] // 2
    totals = [None, None]
    for array in arrays:
        for side in range(2):
            both = array[array.shape[0] - 2 + side].astype(f32)
            part = both[:, :rank] + both[:, rank:]
            totals[side] = part if totals[side] is None else totals[side] + part
    pair[...] = jnp.concatenate(totals, axis=1)
    for base, copy in zip(bases, copies):
        copy[...] = arrays[base][pl.ds(0, copy.shape[0])]


def tree_kernel(
    leaf_count,
    position,
    tree_in,
    couplings_in,
    matrix_in,
    transfer_in,
    basis_in,
    near,
    down_high,
    down_low,
    above,
    basis,
    tree,
    couplings,
    matrix,
    transfer,
    down,
    sem,
):
    rank = matrix.shape[0]
    depth = leaf_count.bit_length() - 2
    place = position[0]
    begins = [2 * leaf_count - 2 * (leaf_count >> height) for height in range(depth)]
    copies = [
        pltpu.make_async_copy(source, target, sem.at[i])
        for i, (source, target) in enumerate(
            [(matrix_in, matrix), (tree_in, tree)]
            + [
                (couplings_in.at[begins[height] + (place >> height)], couplings.at[height])
                for height in range(depth)
            ]
            + [(transfer_in, transfer), (basis_in, basis)]
        )
    ]
    for copy in copies:
        copy.start()
    down[...] = jnp.zeros_like(down)
    for copy in copies[:-2]:
        copy.wait()
    back = matrix[...]
    for height in range(depth):
        members = leaf_count >> height
        spot = place >> height
        for slot, offset in enumerate(offsets):
            source = spot + offset
            usable = jnp.logical_and(source >= 0, source < members)
            if abs(offset) == 3:
                usable = jnp.logical_and(usable, spot % 2 == (0 if offset > 0 else 1))
            entry = begins[height] + jnp.clip(source, 0, members - 1)
            part = exact(times, back, couplings[height, slot])
            down[entry] += jnp.where(usable, part, jnp.zeros_like(part))
        if height < depth - 1:
            back = exact(times, back, tree[begins[height] + spot])
    for height in reversed(range(depth - 1)):
        for parent in range(leaf_count >> (height + 1)):
            for child in (2 * parent, 2 * parent + 1):
                down[begins[height] + child] += exact(
                    times_transposed, down[begins[height + 1] + parent], tree[begins[height] + child]
                )
    for node in range(leaf_count):
        high, low = split(down[node])
        down_high[node] = high
        down_low[node] = low
    copies[-2].wait()
    for leaf in range(transfer.shape[0]):
        high, low = split(transfer[leaf])
        above[leaf] = jnp.concatenate([high, high, low], axis=1)
    copies[-1].wait()


def relay_kernel(count, *refs):
    out = refs[count + 1]
    for i in range(count):
        out[i] = refs[i][...]


def far_kernel(peer_count, position, far_list, far_count, *refs):
    peers = refs[:peer_count]
    coupling, coupled, table = refs[peer_count:]
    leaves, slots, rank = coupling.shape[0], coupling.shape[1], coupling.shape[2]
    rows = table.shape[1]
    pair_count = leaves // 2
    empty = peer_count * leaves
    table[empty] = jnp.zeros(table.shape[1:], bf16)
    for peer in range(peer_count):
        for pair in range(pair_count):
            block = peers[peer][pair]
            first, second = block[:, :rank], block[:, rank:]
            table[peer * leaves + 2 * pair] = jnp.concatenate([first, first], axis=1)
            table[peer * leaves + 2 * pair + 1] = jnp.concatenate([second, second], axis=1)
    own = position[1]
    lower = lax.broadcasted_iota(jnp.int32, (rows, 2 * rank), 1) < rank

    def entry(leaf, slot):
        source = far_list[slot, leaf]
        device = source // leaves
        place = ((device ^ own) - 1) * leaves + (source - device * leaves)
        return jnp.where(slot < far_count[0, leaf], place, empty)

    def one(leaf):
        lefts, rights = [], []
        for slot in range(0, slots, 2):
            lefts.append(
                jnp.where(lower, table[entry(leaf, slot)], table[entry(leaf, slot + 1)])
            )
            rights.append(
                jnp.concatenate([coupling[leaf, slot], coupling[leaf, slot + 1]], axis=1)
            )
        return times_transposed(
            jnp.concatenate(lefts, axis=1), jnp.concatenate(rights, axis=1)
        )

    for pair in range(pair_count):
        coupled[pair] = jnp.concatenate([one(2 * pair), one(2 * pair + 1)], axis=1)


def down_kernel(distances, position, *refs):
    steps = len(distances[0])
    own_pair, received, swapped = refs[0], refs[1 : 1 + steps], refs[1 + steps]
    down_high, down_low, above, basis, coupled, near_begin, near_rest, out, buffer, sem = refs[
        2 + steps :
    ]
    rank = basis.shape[1]
    place = position[0]
    chip, core = place // 2, place % 2

    def product(both, chip_at, flipped):
        first = 2 * chip_at + (core ^ flipped)
        second = 2 * chip_at + (1 - (core ^ flipped))
        high = jnp.concatenate([down_high[first], down_high[second]], axis=1)
        low = jnp.concatenate([down_low[first], down_low[second]], axis=1)
        both_high, both_low = split(both)
        return times_transposed(
            jnp.concatenate([both_high, both_low, both_high], axis=1),
            jnp.concatenate([high, high, low], axis=1),
        )

    total = product(own_pair[...], chip, 0)
    for step in range(steps):
        for flipped in range(2):
            both = swapped[step] if flipped else received[step][...]
            apart = [distances[core_at ^ flipped] for core_at in range(2)]
            fresh = [apart[core_at].index(apart[core_at][step]) == step for core_at in range(2)]
            if not all(fresh):
                usable = core == fresh.index(True)
                both = jnp.where(usable, both, jnp.zeros_like(both))
            at = chip ^ jnp.where(core == 0, apart[0][step], apart[1][step])
            total = total + product(both, at, flipped)
    high, low = split(total)
    wide = jnp.concatenate([high, low, high], axis=1)
    copies = []
    group = 4
    for begin in range(0, basis.shape[0], group):
        for pair in range(begin // 2, (begin + group) // 2):
            matrix = above[pl.ds(2 * pair, 2)].reshape(2 * rank, 3 * rank)
            coefficients = (coupled[pair] + times_transposed(wide, matrix)).astype(bf16)
            for half in range(2):
                leaf = 2 * pair + half
                count = near_begin.shape[0]
                near = near_begin[leaf] if leaf < count else near_rest[leaf - count]
                far = times(coefficients[:, half * rank : (half + 1) * rank], basis[leaf])
                buffer[leaf] = (far + near).astype(bf16)
        rows = pl.ds(begin, group)
        copy = pltpu.make_async_copy(buffer.at[rows], out.at[rows], sem.at[begin // group])
        copy.start()
        copies.append(copy)
    for copy in copies:
        copy.wait()


def on_device(
    panel_charges,
    leaf_basis,
    near_blocks,
    near_list,
    far_list,
    far_count,
    far_coupling,
    leaf_transfer,
    device_transfer,
    tree_transfer,
    level_coupling,
):
    leaves, rows, panels = panel_charges.shape
    rank = leaf_basis.shape[1]
    list_count, leaf_count = lax.axis_size("list"), lax.axis_size("leaf")
    chip_count = leaf_count // 2
    position = jnp.stack([lax.axis_index("leaf"), lax.axis_index("list")]).astype(jnp.int32)

    def like(array, dtype=None):
        return jax.ShapeDtypeStruct(array.shape, dtype or array.dtype)

    def shape(*dims, dtype=bf16):
        return jax.ShapeDtypeStruct(dims, dtype)

    def stay(array):
        return pltpu.with_memory_space_constraint(array, pltpu.HBM)

    def exchange(array, axis, distance):
        pairs = [(i, i ^ distance) for i in range(lax.axis_size(axis))]
        return lax.ppermute(array, axis, pairs)

    ahead = leaves // 8
    inputs = [stay(panel_charges), stay(leaf_basis), stay(leaf_transfer)]
    inputs += [stay(device_transfer[0, 0]), near_list.T, far_list.T, far_count[None]]
    blocks_in = stay(near_blocks)
    count = len(inputs)
    payload, term_parts, charges, near_list, far_list, far_count, blocks_ahead = pl.pallas_call(
        functools.partial(upward_kernel, count),
        out_shape=[
            shape(leaves // 2 + 2, rows, 2 * rank),
            shape(rows, 2 * rank),
            like(panel_charges),
            *[like(array) for array in inputs[4:]],
            shape(ahead, *near_blocks.shape[1:]),
        ],
        in_specs=[anywhere] * (count + 1),
        out_specs=[whole] * 7,
        scratch_shapes=[
            pltpu.VMEM(leaf_basis.shape, bf16),
            pltpu.VMEM(leaf_transfer.shape, f32),
            pltpu.VMEM((rank, rank), f32),
            pltpu.SemaphoreType.DMA((count + 1,)),
        ],
        compiler_params=params(8),
        name="upward",
    )(*inputs[:4], *[stay(array) for array in inputs[4:]], blocks_in)

    other_parts = exchange(term_parts, "leaf", 1)

    near_begin = pl.pallas_call(
        near_begin_kernel,
        out_shape=shape(ahead, rows, panels, dtype=f32),
        in_specs=[scalars, whole, whole],
        out_specs=whole,
        compiler_params=params(4),
        name="near_begin",
    )(near_list, charges, blocks_ahead)

    payload, terms = pl.pallas_call(
        pack_kernel,
        out_shape=[like(payload), shape(2, rows, 2 * rank)],
        in_specs=[whole, anywhere, whole],
        out_specs=[whole, whole],
        input_output_aliases={2: 0},
        compiler_params=params(2),
        name="pack",
    )(other_parts, near_begin, payload)

    direct = [distance for distance in range(1, list_count) if distance & (distance - 1) == 0]
    arrived = {
        distance: exchange(payload if distance in direct else terms, "list", distance)
        for distance in range(1, list_count)
    }

    sizes = (2, 4, 4, 4)
    near_rest = pl.pallas_call(
        functools.partial(near_rest_kernel, sizes),
        out_shape=shape(leaves - ahead, rows, panels, dtype=f32),
        in_specs=[scalars, whole, anywhere],
        out_specs=whole,
        scratch_shapes=[
            pltpu.VMEM((leaves - ahead,) + near_blocks.shape[1:], bf16),
            pltpu.SemaphoreType.DMA((len(sizes),)),
        ],
        compiler_params=params(12),
        cost_estimate=pl.CostEstimate(
            flops=2 * near_blocks.size * rows,
            bytes_accessed=2 * near_blocks.size,
            transcendentals=0,
        ),
        name="near_rest",
    )(near_list, charges, blocks_in)

    bases = direct[:-1]
    own_pair, *copied = pl.pallas_call(
        functools.partial(sum_kernel, list_count, bases),
        out_shape=[shape(rows, 2 * rank, dtype=f32)]
        + [shape(leaves // 2, rows, 2 * rank) for _ in bases],
        in_specs=[whole] * list_count + [anywhere],
        out_specs=[whole] * (1 + len(bases)),
        compiler_params=params(4),
        name="group_sum",
    )(payload, *[arrived[distance] for distance in range(1, list_count)], near_rest)

    steps = chip_count // 2
    apart = list(range(1, chip_count))
    near_chips, far_chips = apart[: chip_count - 1 - steps], apart[chip_count - 1 - steps :]
    distances = (near_chips + near_chips[: steps - len(near_chips)], far_chips)
    received = [
        lax.ppermute(
            own_pair, "leaf", [(i, i ^ 2 * distances[i % 2][step]) for i in range(leaf_count)]
        )
        for step in range(steps)
    ]

    skeletons = {distance: arrived[distance] for distance in direct}
    forward = dict(zip(bases, copied))
    for distance in range(1, list_count):
        if distance not in direct:
            top = 1 << (distance.bit_length() - 1)
            forward[distance] = exchange(forward[distance ^ top], "list", top)
            skeletons[distance] = forward[distance]

    depth = leaf_count.bit_length() - 2
    down_high, down_low, above, basis = pl.pallas_call(
        functools.partial(tree_kernel, leaf_count),
        out_shape=[
            shape(leaf_count, rank, rank),
            shape(leaf_count, rank, rank),
            shape(leaves, rank, 3 * rank),
            like(leaf_basis),
        ],
        in_specs=[scalars] + [anywhere] * 6,
        out_specs=[whole] * 4,
        scratch_shapes=[
            pltpu.VMEM(tree_transfer.shape, f32),
            pltpu.VMEM((depth,) + level_coupling.shape[1:], f32),
            pltpu.VMEM((rank, rank), f32),
            pltpu.VMEM(leaf_transfer.shape, f32),
            pltpu.VMEM((2 * leaf_count, rank, rank), f32),
            pltpu.SemaphoreType.DMA((depth + 4,)),
        ],
        compiler_params=params(8),
        cost_estimate=pl.CostEstimate(
            flops=near_blocks.size * rows, bytes_accessed=near_blocks.size, transcendentals=0
        ),
        name="tree",
    )(
        position,
        stay(tree_transfer),
        stay(level_coupling),
        stay(device_transfer[0, 0]),
        stay(leaf_transfer),
        stay(leaf_basis),
        own_pair,
    )

    relayed = pl.pallas_call(
        functools.partial(relay_kernel, steps),
        out_shape=shape(steps, rows, 2 * rank, dtype=f32),
        in_specs=[whole] * steps + [anywhere],
        out_specs=whole,
        compiler_params=params(2),
        name="relay",
    )(*received, down_high)
    swapped = exchange(relayed, "leaf", 1)

    coupled = pl.pallas_call(
        functools.partial(far_kernel, list_count - 1),
        out_shape=shape(leaves // 2, rows, 2 * rank, dtype=f32),
        in_specs=[scalars] * 3 + [whole] * list_count,
        out_specs=whole,
        scratch_shapes=[pltpu.VMEM(((list_count - 1) * leaves + 1, rows, 2 * rank), bf16)],
        compiler_params=params(8),
        cost_estimate=pl.CostEstimate(
            flops=2 * far_coupling.size * rows * 4,
            bytes_accessed=4 * far_coupling.size,
            transcendentals=0,
        ),
        name="far",
    )(
        position,
        far_list,
        far_count,
        *[skeletons[distance] for distance in range(1, list_count)],
        far_coupling,
    )

    return pl.pallas_call(
        functools.partial(down_kernel, distances),
        out_shape=shape(leaves, rows, panels),
        in_specs=[scalars] + [whole] * (steps + 9),
        out_specs=anywhere,
        scratch_shapes=[
            pltpu.VMEM((leaves, rows, panels), bf16),
            pltpu.SemaphoreType.DMA((leaves // 4,)),
        ],
        compiler_params=params(4),
        name="down",
    )(
        position,
        own_pair,
        *received,
        swapped,
        down_high,
        down_low,
        above,
        basis,
        coupled,
        near_begin,
        near_rest,
    )


def solution(mesh):
    in_specs = (
        P(("leaf", "list"), None, None),
        P(("leaf", "list"), None, None),
        P(("leaf", "list"), None, None, None),
        P(("leaf", "list"), None),
        P(("leaf", "list"), None),
        P(("leaf", "list")),
        P(("leaf", "list"), None, None, None),
        P(("leaf", "list"), None, None),
        P("leaf", "list", None, None),
        P(),
        P(),
    )
    out_specs = P(("leaf", "list"), None, None)
    return jax.shard_map(
        on_device, mesh=mesh, in_specs=in_specs, out_specs=out_specs, check_vma=False
    )
```

```python
import functools

import jax
import jax.numpy as jnp
from jax import lax
from jax.experimental import pallas as pl
from jax.experimental.pallas import tpu as pltpu
from jax.sharding import PartitionSpec as P

offsets = (-3, -2, 2, 3)
f32 = jnp.float32
bf16 = jnp.bfloat16
whole = pl.BlockSpec(memory_space=pltpu.VMEM)
anywhere = pl.BlockSpec(memory_space=pl.ANY)


def params(mebibytes):
    return pltpu.CompilerParams(vmem_limit_bytes=mebibytes << 20)


def times(left, right):
    return lax.dot_general(left, right, (((1,), (0,)), ((), ())), preferred_element_type=f32)


def times_transposed(left, right):
    return lax.dot_general(left, right, (((1,), (1,)), ((), ())), preferred_element_type=f32)


def split(array):
    high = array.astype(bf16)
    return high, (array - high.astype(f32)).astype(bf16)


def exact(product, left, right):
    left_high, left_low = split(left)
    right_high, right_low = split(right)
    return product(left_high, right_high) + (
        product(left_low, right_high) + product(left_high, right_low)
    )


def upward_kernel(count, *refs):
    sources = refs[:count]
    payload, terms = refs[count : count + 2]
    kept = refs[count + 2 : count + 6]
    basis, transfer, matrix, sem = refs[count + 6 :]
    charges = kept[0]
    targets = (charges, basis, transfer, matrix) + kept[1:]
    copies = [
        pltpu.make_async_copy(source, target, sem.at[i])
        for i, (source, target) in enumerate(zip(sources, targets))
    ]
    for copy in copies:
        copy.start()
    for copy in copies:
        copy.wait()
    pair_count = charges.shape[0] // 2
    rank = basis.shape[1]
    node = jnp.zeros((charges.shape[1], rank), f32)
    for pair in range(pair_count):
        halves = [
            times_transposed(charges[leaf], basis[leaf]).astype(bf16)
            for leaf in (2 * pair, 2 * pair + 1)
        ]
        skeleton = jnp.concatenate(halves, axis=1)
        payload[pair] = skeleton
        block = transfer[pl.ds(2 * pair, 2)].reshape(2 * rank, rank)
        high, low = split(block)
        node = node + (times(skeleton, high) + times(skeleton, low))
    term = exact(times, node, matrix[...])
    both = jnp.concatenate(split(term), axis=1)
    terms[0] = both
    payload[pair_count] = both


def near_leaf(near_list, charges, blocks, row, leaf):
    total = None
    for slot in range(blocks.shape[1]):
        part = times_transposed(charges[near_list[slot, leaf]], blocks[row, slot])
        total = part if total is None else total + part
    return total


def near_kernel(first, list_in, charges, blocks, after, near, near_list, sem):
    listed = pltpu.make_async_copy(list_in, near_list, sem)
    listed.start()
    listed.wait()
    for row in range(near.shape[0]):
        near[row] = near_leaf(near_list, charges, blocks, first + row, first + row)


def pair_kernel(own, other, after, pair):
    pair[...] = jnp.concatenate([own[...], other[...]], axis=1)


def forward_kernel(payload, near, terms, copy):
    copy[...] = payload[pl.ds(0, copy.shape[0])]


def sum_kernel(count, *refs):
    arrays, node = refs[:count], refs[-1]
    rank = node.shape[1]
    total = None
    for array in arrays:
        both = array[array.shape[0] - 1].astype(f32)
        part = both[:, :rank] + both[:, rank:]
        total = part if total is None else total + part
    node[...] = total


def tree_kernel(
    leaf_count, tree, couplings, matrix, own_node, down_high, down_low, down
):
    rank = matrix.shape[0]
    depth = leaf_count.bit_length() - 2
    place = lax.axis_index("leaf")
    begins = [2 * leaf_count - 2 * (leaf_count >> height) for height in range(depth)]
    down[...] = jnp.zeros_like(down)
    back = matrix[...]
    for height in range(depth):
        members = leaf_count >> height
        spot = place >> height
        for slot, offset in enumerate(offsets):
            source = spot + offset
            usable = jnp.logical_and(source >= 0, source < members)
            if abs(offset) == 3:
                usable = jnp.logical_and(usable, spot % 2 == (0 if offset > 0 else 1))
            entry = begins[height] + jnp.clip(source, 0, members - 1)
            part = exact(times, back, couplings[begins[height] + spot, slot])
            down[entry] += jnp.where(usable, part, jnp.zeros_like(part))
        if height < depth - 1:
            back = exact(times, back, tree[begins[height] + spot])
    for height in reversed(range(depth - 1)):
        for parent in range(leaf_count >> (height + 1)):
            for child in (2 * parent, 2 * parent + 1):
                down[begins[height] + child] += exact(
                    times_transposed, down[begins[height + 1] + parent], tree[begins[height] + child]
                )
    for node in range(leaf_count):
        high, low = split(down[node])
        down_high[node] = high
        down_low[node] = low


def weights_kernel(transfer, basis, after, weights):
    for leaf in range(transfer.shape[0]):
        high, low = split(transfer[leaf])
        full = times(high.T, basis[leaf]) + times(low.T, basis[leaf])
        full_high, full_low = split(full)
        weights[leaf] = jnp.concatenate([full_high, full_high, full_low], axis=0)


def base_kernel(coupled, basis, near, base):
    rank = basis.shape[1]
    for pair in range(coupled.shape[0]):
        both = coupled[pair].astype(bf16)
        for half in range(2):
            leaf = 2 * pair + half
            far = times(both[:, half * rank : (half + 1) * rank], basis[leaf])
            base[leaf] = far + near[leaf]


def relay_kernel(count, *refs):
    out = refs[-1]
    for i in range(count):
        out[i] = refs[i][...]


def far_kernel(peer_count, list_in, count_in, *refs):
    peers = refs[:peer_count]
    coupling, after, coupled, table, far_list, far_count, sem = refs[peer_count:]
    copies = [
        pltpu.make_async_copy(list_in, far_list, sem.at[0]),
        pltpu.make_async_copy(count_in, far_count, sem.at[1]),
    ]
    for copy in copies:
        copy.start()
    leaves, slots, rank = coupling.shape[0], coupling.shape[1], coupling.shape[2]
    rows = table.shape[1]
    pair_count = leaves // 2
    empty = peer_count * leaves
    table[empty] = jnp.zeros(table.shape[1:], bf16)
    for peer in range(peer_count):
        for pair in range(pair_count):
            block = peers[peer][pair]
            first, second = block[:, :rank], block[:, rank:]
            table[peer * leaves + 2 * pair] = jnp.concatenate([first, first], axis=1)
            table[peer * leaves + 2 * pair + 1] = jnp.concatenate([second, second], axis=1)
    for copy in copies:
        copy.wait()
    own = lax.axis_index("list")
    lower = lax.broadcasted_iota(jnp.int32, (rows, 2 * rank), 1) < rank

    def entry(leaf, slot):
        source = far_list[slot, leaf]
        device = source // leaves
        place = ((device ^ own) - 1) * leaves + (source - device * leaves)
        return jnp.where(slot < far_count[0, leaf], place, empty)

    def one(leaf):
        lefts, rights = [], []
        for slot in range(0, slots, 2):
            lefts.append(
                jnp.where(lower, table[entry(leaf, slot)], table[entry(leaf, slot + 1)])
            )
            rights.append(
                jnp.concatenate([coupling[leaf, slot], coupling[leaf, slot + 1]], axis=1)
            )
        return times_transposed(
            jnp.concatenate(lefts, axis=1), jnp.concatenate(rights, axis=1)
        )

    for pair in range(pair_count):
        coupled[pair] = jnp.concatenate([one(2 * pair), one(2 * pair + 1)], axis=1)


def down_kernel(distances, *refs):
    steps = len(distances[0])
    own_pair, received, swapped = refs[0], refs[1 : 1 + steps], refs[1 + steps]
    down_high, down_low, weights, base, out, buffer, sem = refs[2 + steps :]
    place = lax.axis_index("leaf")
    chip, core = place // 2, place % 2

    def product(both, chip_at, flipped):
        first = 2 * chip_at + (core ^ flipped)
        second = 2 * chip_at + (1 - (core ^ flipped))
        high = jnp.concatenate([down_high[first], down_high[second]], axis=1)
        low = jnp.concatenate([down_low[first], down_low[second]], axis=1)
        both_high, both_low = split(both)
        return times_transposed(
            jnp.concatenate([both_high, both_low, both_high], axis=1),
            jnp.concatenate([high, high, low], axis=1),
        )

    total = product(own_pair[...], chip, 0)
    for step in range(steps):
        for flipped in range(2):
            both = swapped[step] if flipped else received[step][...]
            apart = [distances[core_at ^ flipped] for core_at in range(2)]
            fresh = [apart[core_at].index(apart[core_at][step]) == step for core_at in range(2)]
            if not all(fresh):
                usable = core == fresh.index(True)
                both = jnp.where(usable, both, jnp.zeros_like(both))
            at = chip ^ jnp.where(core == 0, apart[0][step], apart[1][step])
            total = total + product(both, at, flipped)
    high, low = split(total)
    wide = jnp.concatenate([high, low, high], axis=1)
    copies = []
    group = 4
    for begin in range(0, base.shape[0], group):
        for leaf in range(begin, begin + group):
            buffer[leaf] = (base[leaf] + times(wide, weights[leaf])).astype(bf16)
        rows = pl.ds(begin, group)
        copy = pltpu.make_async_copy(buffer.at[rows], out.at[rows], sem.at[begin // group])
        copy.start()
        copies.append(copy)
    for copy in copies:
        copy.wait()


def on_device(
    panel_charges,
    leaf_basis,
    near_blocks,
    near_list,
    far_list,
    far_count,
    far_coupling,
    leaf_transfer,
    device_transfer,
    tree_transfer,
    level_coupling,
):
    leaves, rows, panels = panel_charges.shape
    rank = leaf_basis.shape[1]
    list_count, leaf_count = lax.axis_size("list"), lax.axis_size("leaf")
    chip_count = leaf_count // 2

    def like(array, dtype=None):
        return jax.ShapeDtypeStruct(array.shape, dtype or array.dtype)

    def shape(*dims, dtype=bf16):
        return jax.ShapeDtypeStruct(dims, dtype)

    def stay(array):
        return pltpu.with_memory_space_constraint(array, pltpu.HBM)

    def exchange(array, axis, distance):
        pairs = [(i, i ^ distance) for i in range(lax.axis_size(axis))]
        return lax.ppermute(array, axis, pairs)

    inputs = [stay(panel_charges), stay(leaf_basis), stay(leaf_transfer)]
    inputs += [stay(device_transfer[0, 0]), near_list.T, far_list.T, far_count[None]]
    count = len(inputs)
    payload, terms, charges, near_list, far_list, far_count = pl.pallas_call(
        functools.partial(upward_kernel, count),
        out_shape=[
            shape(leaves // 2 + 1, rows, 2 * rank),
            shape(1, rows, 2 * rank),
            like(panel_charges),
            *[like(array) for array in inputs[4:]],
        ],
        in_specs=[anywhere] * count,
        out_specs=[whole] * 6,
        scratch_shapes=[
            pltpu.VMEM(leaf_basis.shape, bf16),
            pltpu.VMEM(leaf_transfer.shape, f32),
            pltpu.VMEM((rank, rank), f32),
            pltpu.SemaphoreType.DMA((count,)),
        ],
        compiler_params=params(4),
        cost_estimate=pl.CostEstimate(
            flops=64 * near_blocks.size * rows,
            bytes_accessed=64 * near_blocks.size,
            transcendentals=0,
        ),
        name="upward",
    )(*inputs[:4], *[stay(array) for array in inputs[4:]])

    direct = [distance for distance in range(1, list_count) if distance & (distance - 1) == 0]
    arrived = {
        distance: exchange(payload if distance in direct else terms, "list", distance)
        for distance in range(1, list_count)
    }

    def near_part(first, count, after):
        return pl.pallas_call(
            functools.partial(near_kernel, first),
            out_shape=shape(count, rows, panels, dtype=f32),
            in_specs=[anywhere, whole, whole, anywhere],
            out_specs=whole,
            scratch_shapes=[pltpu.SMEM(near_list.shape, jnp.int32), pltpu.SemaphoreType.DMA],
            compiler_params=params(4),
            cost_estimate=pl.CostEstimate(
                flops=2 * near_blocks.size * rows,
                bytes_accessed=2 * near_blocks.size,
                transcendentals=0,
            ),
            name="near",
        )(near_list, charges, near_blocks, after)

    near = near_part(0, leaves, terms)

    bases = direct[:-1]
    forward = {}
    for base in bases:
        forward[base] = pl.pallas_call(
            forward_kernel,
            out_shape=shape(leaves // 2, rows, 2 * rank),
            in_specs=[whole, anywhere, anywhere],
            out_specs=whole,
            compiler_params=params(2),
            name="forward",
        )(arrived[base], near, arrived[list_count - 1])

    own_node = pl.pallas_call(
        functools.partial(sum_kernel, list_count),
        out_shape=shape(rows, rank, dtype=f32),
        in_specs=[whole] * list_count + [anywhere],
        out_specs=whole,
        compiler_params=params(4),
        name="group_sum",
    )(payload, *[arrived[distance] for distance in range(1, list_count)], near)
    other_node = exchange(own_node, "leaf", 1)

    down_high, down_low = pl.pallas_call(
        functools.partial(tree_kernel, leaf_count),
        out_shape=[
            shape(leaf_count, rank, rank),
            shape(leaf_count, rank, rank),
        ],
        in_specs=[whole] * 3 + [anywhere],
        out_specs=[whole] * 2,
        scratch_shapes=[pltpu.VMEM((2 * leaf_count, rank, rank), f32)],
        compiler_params=params(4),
        name="tree",
    )(tree_transfer, level_coupling, device_transfer[0, 0], own_node)

    own_pair = pl.pallas_call(
        pair_kernel,
        out_shape=shape(rows, 2 * rank, dtype=f32),
        in_specs=[whole] * 2 + [anywhere],
        out_specs=whole,
        compiler_params=params(2),
        name="pair",
    )(own_node, other_node, down_high)

    steps = chip_count // 2
    apart = list(range(1, chip_count))
    near_chips, far_chips = apart[: chip_count - 1 - steps], apart[chip_count - 1 - steps :]
    distances = (near_chips + near_chips[: steps - len(near_chips)], far_chips)
    received = [
        lax.ppermute(
            own_pair, "leaf", [(i, i ^ 2 * distances[i % 2][step]) for i in range(leaf_count)]
        )
        for step in range(steps)
    ]

    skeletons = {distance: arrived[distance] for distance in direct}
    for distance in range(1, list_count):
        if distance not in direct:
            top = 1 << (distance.bit_length() - 1)
            forward[distance] = exchange(forward[distance ^ top], "list", top)
            skeletons[distance] = forward[distance]

    coupled = pl.pallas_call(
        functools.partial(far_kernel, list_count - 1),
        out_shape=shape(leaves // 2, rows, 2 * rank, dtype=f32),
        in_specs=[anywhere] * 2 + [whole] * list_count + [anywhere],
        out_specs=whole,
        scratch_shapes=[
            pltpu.VMEM(((list_count - 1) * leaves + 1, rows, 2 * rank), bf16),
            pltpu.SMEM(far_list.shape, jnp.int32),
            pltpu.SMEM(far_count.shape, jnp.int32),
            pltpu.SemaphoreType.DMA((2,)),
        ],
        compiler_params=params(8),
        cost_estimate=pl.CostEstimate(
            flops=2 * far_coupling.size * rows * 4,
            bytes_accessed=4 * far_coupling.size,
            transcendentals=0,
        ),
        name="far",
    )(
        far_list,
        far_count,
        *[skeletons[distance] for distance in range(1, list_count)],
        far_coupling,
        own_pair,
    )

    weights = pl.pallas_call(
        weights_kernel,
        out_shape=shape(leaves, 3 * rank, panels),
        in_specs=[whole] * 2 + [anywhere],
        out_specs=whole,
        compiler_params=params(4),
        name="weights",
    )(leaf_transfer, leaf_basis, own_pair)

    relayed = pl.pallas_call(
        functools.partial(relay_kernel, steps),
        out_shape=shape(steps, rows, 2 * rank, dtype=f32),
        in_specs=[whole] * steps + [anywhere] * 2,
        out_specs=whole,
        compiler_params=params(2),
        name="relay",
    )(*received, coupled, weights)
    swapped = exchange(relayed, "leaf", 1)

    base = pl.pallas_call(
        base_kernel,
        out_shape=shape(leaves, rows, panels, dtype=f32),
        in_specs=[whole] * 3,
        out_specs=whole,
        compiler_params=params(4),
        name="base",
    )(coupled, leaf_basis, near)

    return pl.pallas_call(
        functools.partial(down_kernel, distances),
        out_shape=shape(leaves, rows, panels),
        in_specs=[whole] * (steps + 6),
        out_specs=anywhere,
        scratch_shapes=[
            pltpu.VMEM((leaves, rows, panels), bf16),
            pltpu.SemaphoreType.DMA((leaves // 4,)),
        ],
        compiler_params=params(4),
        name="down",
    )(
        own_pair,
        *received,
        swapped,
        down_high,
        down_low,
        weights,
        base,
    )


def solution(mesh):
    in_specs = (
        P(("leaf", "list"), None, None),
        P(("leaf", "list"), None, None),
        P(("leaf", "list"), None, None, None),
        P(("leaf", "list"), None),
        P(("leaf", "list"), None),
        P(("leaf", "list")),
        P(("leaf", "list"), None, None, None),
        P(("leaf", "list"), None, None),
        P("leaf", "list", None, None),
        P(),
        P(),
    )
    out_specs = P(("leaf", "list"), None, None)
    return jax.shard_map(
        on_device, mesh=mesh, in_specs=in_specs, out_specs=out_specs, check_vma=False
    )
```

```python
import functools

import jax
import jax.numpy as jnp
from jax import lax
from jax.experimental import pallas as pl
from jax.experimental.pallas import tpu as pltpu
from jax.sharding import PartitionSpec as P

offsets = (-3, -2, 2, 3)
f32 = jnp.float32
bf16 = jnp.bfloat16
whole = pl.BlockSpec(memory_space=pltpu.VMEM)
anywhere = pl.BlockSpec(memory_space=pl.ANY)


def params(mebibytes):
    return pltpu.CompilerParams(vmem_limit_bytes=mebibytes << 20)


def times(left, right):
    return lax.dot_general(left, right, (((1,), (0,)), ((), ())), preferred_element_type=f32)


def times_transposed(left, right):
    return lax.dot_general(left, right, (((1,), (1,)), ((), ())), preferred_element_type=f32)


def split(array):
    high = array.astype(bf16)
    return high, (array - high.astype(f32)).astype(bf16)


def exact(product, left, right):
    left_high, left_low = split(left)
    right_high, right_low = split(right)
    return product(left_high, right_high) + (
        product(left_low, right_high) + product(left_high, right_low)
    )


def upward_kernel(count, *refs):
    sources = refs[:count]
    payload = refs[count]
    kept = refs[count + 1 : count + 5]
    basis, transfer, matrix, sem = refs[count + 5 :]
    charges = kept[0]
    targets = (charges, basis, transfer, matrix) + kept[1:]
    copies = [
        pltpu.make_async_copy(source, target, sem.at[i])
        for i, (source, target) in enumerate(zip(sources, targets))
    ]
    for copy in copies:
        copy.start()
    for copy in copies:
        copy.wait()
    pair_count = charges.shape[0] // 2
    rank = basis.shape[1]
    skeletons = []
    for pair in range(pair_count):
        halves = [
            times_transposed(charges[leaf], basis[leaf]).astype(bf16)
            for leaf in (2 * pair, 2 * pair + 1)
        ]
        skeletons.append(jnp.concatenate(halves, axis=1))
        payload[pair] = skeletons[pair]
    high, low = split(transfer[...].reshape(2 * pair_count * rank, rank))
    row = jnp.concatenate(skeletons, axis=1)
    node = times(row, high) + times(row, low)
    term = exact(times, node, matrix[...])
    payload[pair_count] = jnp.concatenate(split(term), axis=1)


def mark_kernel(*refs):
    pass


def near_leaf(near_list, charges, blocks, row, leaf):
    total = None
    for slot in range(blocks.shape[1]):
        part = times_transposed(charges[near_list[slot, leaf]], blocks[row, slot])
        total = part if total is None else total + part
    return total


def near_rest_kernel(first, list_in, charges, blocks, after, near, near_list, sem):
    listed = pltpu.make_async_copy(list_in, near_list, sem)
    listed.start()
    listed.wait()
    for row in range(near.shape[0]):
        near[row] = near_leaf(near_list, charges, blocks, first + row, first + row)


def near_kernel(leaf_count, list_in, charges, blocks, after, *refs):
    sources, couplings_in = refs[:5], refs[5]
    near, targets, couplings = refs[6], refs[7:12], refs[12]
    near_list, sem = refs[13:]
    listed = pltpu.make_async_copy(list_in, near_list, sem.at[0])
    listed.start()
    place = lax.axis_index("leaf")
    moves = list(zip(sources, targets))
    for height in range(couplings.shape[0]):
        begin = 2 * leaf_count - 2 * (leaf_count >> height)
        moves.append((couplings_in.at[begin + (place >> height)], couplings.at[height]))
    copies = [
        pltpu.make_async_copy(source, target, sem.at[1 + i])
        for i, (source, target) in enumerate(moves)
    ]
    for copy in copies:
        copy.start()
    listed.wait()
    for leaf in range(near.shape[0]):
        near[leaf] = near_leaf(near_list, charges, blocks, leaf, leaf)
    for copy in copies:
        copy.wait()


def joined(both):
    both = both.astype(f32)
    rank = both.shape[1] // 2
    return both[:, :rank] + both[:, rank:]


def terms_kernel(own, other, terms):
    last = own.shape[0] - 1
    terms[...] = jnp.concatenate([joined(own[last]), joined(other[last])], axis=1)


def pair_kernel(mine, theirs, *refs):
    pair = refs[-1]
    rank = pair.shape[1] // 2
    odd = lax.axis_index("leaf") % 2 == 1
    far = jnp.where(odd, mine[1], theirs[1])
    flipped = jnp.concatenate([far[:, rank:], far[:, :rank]], axis=1)
    near = jnp.concatenate([mine[0][:, :rank], theirs[0][:, :rank]], axis=1)
    pair[...] = near + jnp.where(odd, far, flipped)


def forward_kernel(payload, near, copy):
    copy[...] = payload[pl.ds(0, copy.shape[0])]


def sum_kernel(count, *refs):
    arrays, pairs, sums = refs[:count], refs[count:-2], refs[-1]
    total = None
    for array in arrays:
        part = joined(array[array.shape[0] - 1])
        total = part if total is None else total + part
    sums[0] = jnp.concatenate([total, jnp.zeros_like(total)], axis=1)
    total = jnp.zeros(sums.shape[1:], f32)
    for pair in pairs:
        total = total + pair[...]
    sums[1] = total


def tree_kernel(
    leaf_count, tree, couplings, matrix, sums, down_high, down_low, down
):
    rank = matrix.shape[0]
    depth = leaf_count.bit_length() - 2
    place = lax.axis_index("leaf")
    begins = [2 * leaf_count - 2 * (leaf_count >> height) for height in range(depth)]
    down[...] = jnp.zeros_like(down)
    back = matrix[...]
    for height in range(depth):
        members = leaf_count >> height
        spot = place >> height
        for slot, offset in enumerate(offsets):
            source = spot + offset
            usable = jnp.logical_and(source >= 0, source < members)
            if abs(offset) == 3:
                usable = jnp.logical_and(usable, spot % 2 == (0 if offset > 0 else 1))
            entry = begins[height] + jnp.clip(source, 0, members - 1)
            part = exact(times, back, couplings[height, slot])
            down[entry] += jnp.where(usable, part, jnp.zeros_like(part))
        if height < depth - 1:
            back = exact(times, back, tree[begins[height] + spot])
    for height in reversed(range(depth - 1)):
        for parent in range(leaf_count >> (height + 1)):
            for child in (2 * parent, 2 * parent + 1):
                down[begins[height] + child] += exact(
                    times_transposed, down[begins[height + 1] + parent], tree[begins[height] + child]
                )
    for node in range(leaf_count):
        high, low = split(down[node])
        down_high[node] = high
        down_low[node] = low


def weights_kernel(transfer, basis, after, weights):
    for leaf in range(transfer.shape[0]):
        high, low = split(transfer[leaf])
        full = times(high.T, basis[leaf]) + times(low.T, basis[leaf])
        full_high, full_low = split(full)
        weights[leaf] = jnp.concatenate([full_high, full_high, full_low], axis=0)


def base_kernel(distances, coupled, basis, near, near_rest, down_high, down_low, *refs):
    pairs, base, part = refs[:-2], refs[-2], refs[-1]
    rank = basis.shape[1]
    for pair in range(coupled.shape[0]):
        both = coupled[pair].astype(bf16)
        for half in range(2):
            leaf = 2 * pair + half
            far = times(both[:, half * rank : (half + 1) * rank], basis[leaf])
            count = near.shape[0]
            base[leaf] = far + (near[leaf] if leaf < count else near_rest[leaf - count])
    place = lax.axis_index("leaf")
    chip, core = place // 2, place % 2
    total = down_product(down_high, down_low, pairs[0][...], chip, core)
    for both, at in arrivals(distances, [ref[...] for ref in pairs[1:]], chip, core, 0):
        total = total + down_product(down_high, down_low, both, at, core)
    part[...] = total


def relay_kernel(count, *refs):
    out = refs[-1]
    for i in range(count):
        out[i] = refs[i][...]


def far_kernel(peer_count, list_in, count_in, *refs):
    peers = refs[:peer_count]
    coupling, after, coupled, table, far_list, far_count, sem = refs[peer_count:]
    copies = [
        pltpu.make_async_copy(list_in, far_list, sem.at[0]),
        pltpu.make_async_copy(count_in, far_count, sem.at[1]),
    ]
    for copy in copies:
        copy.start()
    leaves, slots, rank = coupling.shape[0], coupling.shape[1], coupling.shape[2]
    rows = table.shape[1]
    pair_count = leaves // 2
    empty = peer_count * leaves
    table[empty] = jnp.zeros(table.shape[1:], bf16)
    for peer in range(peer_count):
        for pair in range(pair_count):
            block = peers[peer][pair]
            first, second = block[:, :rank], block[:, rank:]
            table[peer * leaves + 2 * pair] = jnp.concatenate([first, first], axis=1)
            table[peer * leaves + 2 * pair + 1] = jnp.concatenate([second, second], axis=1)
    for copy in copies:
        copy.wait()
    own = lax.axis_index("list")
    lower = lax.broadcasted_iota(jnp.int32, (rows, 2 * rank), 1) < rank

    def entry(leaf, slot):
        source = far_list[slot, leaf]
        device = source // leaves
        place = ((device ^ own) - 1) * leaves + (source - device * leaves)
        return jnp.where(slot < far_count[0, leaf], place, empty)

    def one(leaf):
        lefts, rights = [], []
        for slot in range(0, slots, 2):
            lefts.append(
                jnp.where(lower, table[entry(leaf, slot)], table[entry(leaf, slot + 1)])
            )
            rights.append(
                jnp.concatenate([coupling[leaf, slot], coupling[leaf, slot + 1]], axis=1)
            )
        return times_transposed(
            jnp.concatenate(lefts, axis=1), jnp.concatenate(rights, axis=1)
        )

    for pair in range(pair_count):
        coupled[pair] = jnp.concatenate([one(2 * pair), one(2 * pair + 1)], axis=1)


def down_product(down_high, down_low, both, chip_at, core):
    first, second = 2 * chip_at + core, 2 * chip_at + 1 - core
    high = jnp.concatenate([down_high[first], down_high[second]], axis=1)
    low = jnp.concatenate([down_low[first], down_low[second]], axis=1)
    both_high, both_low = split(both)
    return times_transposed(
        jnp.concatenate([both_high, both_low, both_high], axis=1),
        jnp.concatenate([high, high, low], axis=1),
    )


def arrivals(distances, arrays, chip, core, flipped):
    apart = [distances[core_at ^ flipped] for core_at in range(2)]
    result = []
    for step, both in enumerate(arrays):
        fresh = [apart[core_at].index(apart[core_at][step]) == step for core_at in range(2)]
        if not all(fresh):
            both = jnp.where(core == fresh.index(True), both, jnp.zeros_like(both))
        result.append((both, chip ^ jnp.where(core == 0, apart[0][step], apart[1][step])))
    return result


def down_kernel(distances, part, swapped, down_high, down_low, weights, base, out, buffer, sem):
    place = lax.axis_index("leaf")
    chip, core = place // 2, place % 2
    total = part[...]
    arrays = [swapped[step] for step in range(swapped.shape[0])]
    for both, at in arrivals(distances, arrays, chip, core, 1):
        total = total + down_product(down_high, down_low, both, at, 1 - core)
    high, low = split(total)
    wide = jnp.concatenate([high, low, high], axis=1)
    copies = []
    group = 2
    for begin in range(0, base.shape[0], group):
        for leaf in range(begin, begin + group):
            buffer[leaf] = (base[leaf] + times(wide, weights[leaf])).astype(bf16)
        rows = pl.ds(begin, group)
        copy = pltpu.make_async_copy(buffer.at[rows], out.at[rows], sem.at[begin // group])
        copy.start()
        copies.append(copy)
    for copy in copies:
        copy.wait()


def on_device(
    panel_charges,
    leaf_basis,
    near_blocks,
    near_list,
    far_list,
    far_count,
    far_coupling,
    leaf_transfer,
    device_transfer,
    tree_transfer,
    level_coupling,
):
    leaves, rows, panels = panel_charges.shape
    rank = leaf_basis.shape[1]
    list_count, leaf_count = lax.axis_size("list"), lax.axis_size("leaf")
    chip_count = leaf_count // 2

    def like(array, dtype=None):
        return jax.ShapeDtypeStruct(array.shape, dtype or array.dtype)

    def shape(*dims, dtype=bf16):
        return jax.ShapeDtypeStruct(dims, dtype)

    def stay(array):
        return pltpu.with_memory_space_constraint(array, pltpu.HBM)

    def exchange(array, axis, distance):
        pairs = [(i, i ^ distance) for i in range(lax.axis_size(axis))]
        return lax.ppermute(array, axis, pairs)

    inputs = [stay(panel_charges), stay(leaf_basis), stay(leaf_transfer)]
    inputs += [stay(device_transfer[0, 0]), near_list.T, far_list.T, far_count[None]]
    count = len(inputs)
    payload, charges, near_list, far_list, far_count = pl.pallas_call(
        functools.partial(upward_kernel, count),
        out_shape=[
            shape(leaves // 2 + 1, rows, 2 * rank),
            like(panel_charges),
            *[like(array) for array in inputs[4:]],
        ],
        in_specs=[anywhere] * count,
        out_specs=[whole] * 5,
        scratch_shapes=[
            pltpu.VMEM(leaf_basis.shape, bf16),
            pltpu.VMEM(leaf_transfer.shape, f32),
            pltpu.VMEM((rank, rank), f32),
            pltpu.SemaphoreType.DMA((count,)),
        ],
        compiler_params=params(4),
        name="upward",
    )(*inputs[:4], *[stay(array) for array in inputs[4:]])

    payload = pl.pallas_call(
        mark_kernel,
        out_shape=like(payload),
        in_specs=[anywhere],
        out_specs=anywhere,
        input_output_aliases={0: 0},
        compiler_params=params(1),
        cost_estimate=pl.CostEstimate(
            flops=64 * near_blocks.size * rows,
            bytes_accessed=64 * near_blocks.size,
            transcendentals=0,
        ),
        name="mark",
    )(payload)

    other_payload = exchange(payload, "leaf", 1)
    direct = [distance for distance in range(1, list_count) if distance & (distance - 1) == 0]
    arrived = {distance: exchange(payload, "list", distance) for distance in direct}

    terms = pl.pallas_call(
        terms_kernel,
        out_shape=shape(rows, 2 * rank, dtype=f32),
        in_specs=[whole] * 2,
        out_specs=whole,
        compiler_params=params(2),
        name="terms",
    )(payload, other_payload)

    def send_pairs(distance):
        places = [(l, j) for l in range(leaf_count) for j in range(list_count)]
        ends = [l * list_count + (j ^ (distance if l % 2 else direct[0])) for l, j in places]
        return lax.ppermute(terms, ("leaf", "list"), list(enumerate(ends)))

    far_terms = [
        send_pairs(distance) for distance in range(1, list_count) if distance not in direct
    ]

    early = leaves * 14 // 16
    depth = leaf_count.bit_length() - 2
    fetched = [tree_transfer, device_transfer[0, 0], leaf_transfer, leaf_basis, far_coupling]
    near, tree_matrices, device_matrix, transfer, basis, coupling, couplings = pl.pallas_call(
        functools.partial(near_kernel, leaf_count),
        out_shape=[
            shape(early, rows, panels, dtype=f32),
            *[like(array) for array in fetched],
            shape(depth, *level_coupling.shape[1:], dtype=f32),
        ],
        in_specs=[anywhere, whole, whole] + [anywhere] * (2 + len(fetched)),
        out_specs=[whole] * (2 + len(fetched)),
        scratch_shapes=[
            pltpu.SMEM(near_list.shape, jnp.int32),
            pltpu.SemaphoreType.DMA((1 + len(fetched) + depth,)),
        ],
        compiler_params=params(12),
        cost_estimate=pl.CostEstimate(
            flops=2 * near_blocks.size * rows,
            bytes_accessed=2 * near_blocks.size,
            transcendentals=0,
        ),
        name="near",
    )(
        near_list,
        charges,
        near_blocks,
        terms,
        *[stay(array) for array in fetched],
        stay(level_coupling),
    )

    sums = pl.pallas_call(
        functools.partial(sum_kernel, 1 + len(direct)),
        out_shape=shape(2, rows, 2 * rank, dtype=f32),
        in_specs=[whole] * (1 + len(direct) + len(far_terms)) + [anywhere],
        out_specs=whole,
        compiler_params=params(4),
        name="group_sum",
    )(payload, *[arrived[distance] for distance in direct], *far_terms, near)
    other_sums = exchange(sums, "leaf", 1)

    bases = direct[:-1]
    forward = {}
    for base in bases:
        forward[base] = pl.pallas_call(
            forward_kernel,
            out_shape=shape(leaves // 2, rows, 2 * rank),
            in_specs=[whole, anywhere],
            out_specs=whole,
            compiler_params=params(2),
            name="forward",
        )(arrived[base], near)

    down_high, down_low = pl.pallas_call(
        functools.partial(tree_kernel, leaf_count),
        out_shape=[
            shape(leaf_count, rank, rank),
            shape(leaf_count, rank, rank),
        ],
        in_specs=[whole] * 3 + [anywhere],
        out_specs=[whole] * 2,
        scratch_shapes=[pltpu.VMEM((2 * leaf_count, rank, rank), f32)],
        compiler_params=params(4),
        cost_estimate=pl.CostEstimate(
            flops=64 * near_blocks.size * rows,
            bytes_accessed=64 * near_blocks.size,
            transcendentals=0,
        ),
        name="tree",
    )(tree_matrices, couplings, device_matrix, sums)

    own_pair = pl.pallas_call(
        pair_kernel,
        out_shape=shape(rows, 2 * rank, dtype=f32),
        in_specs=[whole] * 2 + [anywhere],
        out_specs=whole,
        compiler_params=params(2),
        name="pair",
    )(sums, other_sums, down_high)

    steps = chip_count // 2
    apart = list(range(1, chip_count))
    near_chips, far_chips = apart[: chip_count - 1 - steps], apart[chip_count - 1 - steps :]
    distances = (near_chips + near_chips[: steps - len(near_chips)], far_chips)
    received = [
        lax.ppermute(
            own_pair, "leaf", [(i, i ^ 2 * distances[i % 2][step]) for i in range(leaf_count)]
        )
        for step in range(steps)
    ]

    near_rest = pl.pallas_call(
        functools.partial(near_rest_kernel, early),
        out_shape=shape(leaves - early, rows, panels, dtype=f32),
        in_specs=[anywhere, whole, whole, anywhere],
        out_specs=whole,
        scratch_shapes=[pltpu.SMEM(near_list.shape, jnp.int32), pltpu.SemaphoreType.DMA],
        compiler_params=params(4),
        name="near_rest",
    )(near_list, charges, near_blocks, own_pair)

    skeletons = {distance: arrived[distance] for distance in direct}
    for distance in range(1, list_count):
        if distance not in direct:
            top = 1 << (distance.bit_length() - 1)
            forward[distance] = exchange(forward[distance ^ top], "list", top)
            skeletons[distance] = forward[distance]

    coupled = pl.pallas_call(
        functools.partial(far_kernel, list_count - 1),
        out_shape=shape(leaves // 2, rows, 2 * rank, dtype=f32),
        in_specs=[anywhere] * 2 + [whole] * list_count + [anywhere],
        out_specs=whole,
        scratch_shapes=[
            pltpu.VMEM(((list_count - 1) * leaves + 1, rows, 2 * rank), bf16),
            pltpu.SMEM(far_list.shape, jnp.int32),
            pltpu.SMEM(far_count.shape, jnp.int32),
            pltpu.SemaphoreType.DMA((2,)),
        ],
        compiler_params=params(8),
        cost_estimate=pl.CostEstimate(
            flops=2 * far_coupling.size * rows * 4,
            bytes_accessed=4 * far_coupling.size,
            transcendentals=0,
        ),
        name="far",
    )(
        far_list,
        far_count,
        *[skeletons[distance] for distance in range(1, list_count)],
        coupling,
        near_rest,
    )

    relayed = pl.pallas_call(
        functools.partial(relay_kernel, steps),
        out_shape=shape(steps, rows, 2 * rank, dtype=f32),
        in_specs=[whole] * steps + [anywhere],
        out_specs=whole,
        compiler_params=params(2),
        name="relay",
    )(*received, coupled)
    swapped = exchange(relayed, "leaf", 1)

    weights = pl.pallas_call(
        weights_kernel,
        out_shape=shape(leaves, 3 * rank, panels),
        in_specs=[whole] * 2 + [anywhere],
        out_specs=whole,
        compiler_params=params(4),
        name="weights",
    )(transfer, basis, relayed)


    base, part = pl.pallas_call(
        functools.partial(base_kernel, distances),
        out_shape=[
            shape(leaves, rows, panels, dtype=f32),
            shape(rows, rank, dtype=f32),
        ],
        in_specs=[whole] * (7 + steps),
        out_specs=[whole] * 2,
        compiler_params=params(4),
        name="base",
    )(coupled, basis, near, near_rest, down_high, down_low, own_pair, *received)

    return pl.pallas_call(
        functools.partial(down_kernel, distances),
        out_shape=shape(leaves, rows, panels),
        in_specs=[whole] * 6,
        out_specs=anywhere,
        scratch_shapes=[
            pltpu.VMEM((leaves, rows, panels), bf16),
            pltpu.SemaphoreType.DMA((leaves // 2,)),
        ],
        compiler_params=params(4),
        name="down",
    )(part, swapped, down_high, down_low, weights, base)


def solution(mesh):
    in_specs = (
        P(("leaf", "list"), None, None),
        P(("leaf", "list"), None, None),
        P(("leaf", "list"), None, None, None),
        P(("leaf", "list"), None),
        P(("leaf", "list"), None),
        P(("leaf", "list")),
        P(("leaf", "list"), None, None, None),
        P(("leaf", "list"), None, None),
        P("leaf", "list", None, None),
        P(),
        P(),
    )
    out_specs = P(("leaf", "list"), None, None)
    return jax.shard_map(
        on_device, mesh=mesh, in_specs=in_specs, out_specs=out_specs, check_vma=False
    )
```

```python
import functools

import jax
import jax.numpy as jnp
from jax import lax
from jax.experimental import pallas as pl
from jax.experimental.pallas import tpu as pltpu
from jax.sharding import PartitionSpec as P

offsets = (-3, -2, 2, 3)
f32 = jnp.float32
bf16 = jnp.bfloat16
whole = pl.BlockSpec(memory_space=pltpu.VMEM)
anywhere = pl.BlockSpec(memory_space=pl.ANY)


def params(mebibytes):
    return pltpu.CompilerParams(vmem_limit_bytes=mebibytes << 20)


def times(left, right):
    return lax.dot_general(left, right, (((1,), (0,)), ((), ())), preferred_element_type=f32)


def times_transposed(left, right):
    return lax.dot_general(left, right, (((1,), (1,)), ((), ())), preferred_element_type=f32)


def split(array):
    high = array.astype(bf16)
    return high, (array - high.astype(f32)).astype(bf16)


def exact(product, left, right):
    left_high, left_low = split(left)
    right_high, right_low = split(right)
    return product(left_high, right_high) + (
        product(left_low, right_high) + product(left_high, right_low)
    )


def mirrored(distance, count):
    bits = count.bit_length() - 1
    return sum(((distance >> i) & 1) << (bits - 1 - i) for i in range(bits))


def upward_kernel(count, *refs):
    sources = refs[:count]
    payload = refs[count]
    charges, basis, transfer, *lists, matrix, sem = refs[count + 1 :]
    targets = [charges, basis, transfer, matrix] + lists
    copies = [
        pltpu.make_async_copy(source, target, sem.at[i])
        for i, (source, target) in enumerate(zip(sources, targets))
    ]
    for copy in copies:
        copy.start()
    for copy in copies:
        copy.wait()
    pair_count = charges.shape[0] // 2
    rank = basis.shape[1]
    skeletons = []
    for pair in range(pair_count):
        halves = [
            times_transposed(charges[leaf], basis[leaf]).astype(bf16)
            for leaf in (2 * pair, 2 * pair + 1)
        ]
        skeletons.append(jnp.concatenate(halves, axis=1))
        payload[pair] = skeletons[pair]
    high, low = split(transfer[...].reshape(2 * pair_count * rank, rank))
    row = jnp.concatenate(skeletons, axis=1)
    node = times(row, high) + times(row, low)
    term = exact(times, node, matrix[...])
    payload[pair_count] = jnp.concatenate(split(term), axis=1)


def mark_kernel(*refs):
    pass


def pause_kernel(after, out):
    out[...] = jnp.zeros_like(out)


def near_leaf(near_list, charges, blocks, row, leaf):
    total = None
    for slot in range(blocks.shape[1]):
        part = times_transposed(charges[near_list[slot, leaf]], blocks[row, slot])
        total = part if total is None else total + part
    return total


def near_kernel(leaf_count, list_in, charges, blocks, after, *refs):
    sources, couplings_in = refs[:4], refs[4]
    near, targets, couplings = refs[5], refs[6:10], refs[10]
    near_list, sem = refs[11:]
    listed = pltpu.make_async_copy(list_in, near_list, sem.at[0])
    listed.start()
    place = lax.axis_index("leaf")
    moves = list(zip(sources, targets))
    for height in range(couplings.shape[0]):
        begin = 2 * leaf_count - 2 * (leaf_count >> height)
        moves.append((couplings_in.at[begin + (place >> height)], couplings.at[height]))
    copies = [
        pltpu.make_async_copy(source, target, sem.at[1 + i])
        for i, (source, target) in enumerate(moves)
    ]
    for copy in copies:
        copy.start()
    listed.wait()
    for leaf in range(near.shape[0]):
        near[leaf] = near_leaf(near_list, charges, blocks, leaf, leaf)
    for copy in copies:
        copy.wait()


def joined(both):
    both = both.astype(f32)
    rank = both.shape[1] // 2
    return both[:, :rank] + both[:, rank:]


def terms_kernel(own, other, terms):
    last = own.shape[0] - 1
    terms[...] = jnp.concatenate([joined(own[last]), joined(other[last])], axis=1)


def pair_kernel(mine, theirs, *refs):
    pair, rounded = refs[-2:]
    rank = pair.shape[1] // 2
    odd = lax.axis_index("leaf") % 2 == 1
    far = jnp.where(odd, mine[1], theirs[1])
    flipped = jnp.concatenate([far[:, rank:], far[:, :rank]], axis=1)
    near = jnp.concatenate([mine[0][:, :rank], theirs[0][:, :rank]], axis=1)
    total = near + jnp.where(odd, far, flipped)
    pair[...] = total
    rounded[...] = total.astype(bf16)


def forward_kernel(payload, near, copy):
    copy[...] = payload[pl.ds(0, copy.shape[0])]


def sum_kernel(count, *refs):
    arrays, pairs, sums = refs[:count], refs[count:-2], refs[-1]
    total = None
    for array in arrays:
        part = joined(array[array.shape[0] - 1])
        total = part if total is None else total + part
    sums[0] = jnp.concatenate([total, jnp.zeros_like(total)], axis=1)
    total = jnp.zeros(sums.shape[1:], f32)
    for pair in pairs:
        total = total + pair[...]
    sums[1] = total


def tree_kernel(
    leaf_count, tree, couplings, matrix, sums, down_high, down_low, down
):
    rank = matrix.shape[0]
    depth = leaf_count.bit_length() - 2
    place = lax.axis_index("leaf")
    begins = [2 * leaf_count - 2 * (leaf_count >> height) for height in range(depth)]
    down[...] = jnp.zeros_like(down)
    back = matrix[...]
    for height in range(depth):
        members = leaf_count >> height
        spot = place >> height
        for slot, offset in enumerate(offsets):
            source = spot + offset
            usable = jnp.logical_and(source >= 0, source < members)
            if abs(offset) == 3:
                usable = jnp.logical_and(usable, spot % 2 == (0 if offset > 0 else 1))
            entry = begins[height] + jnp.clip(source, 0, members - 1)
            part = exact(times, back, couplings[height, slot])
            down[entry] += jnp.where(usable, part, jnp.zeros_like(part))
        if height < depth - 1:
            back = exact(times, back, tree[begins[height] + spot])
    for height in reversed(range(depth - 1)):
        for parent in range(leaf_count >> (height + 1)):
            for child in (2 * parent, 2 * parent + 1):
                down[begins[height] + child] += exact(
                    times_transposed, down[begins[height + 1] + parent], tree[begins[height] + child]
                )
    for node in range(leaf_count):
        high, low = split(down[node])
        down_high[node] = high
        down_low[node] = low


def weights_kernel(transfer, basis, after, weights):
    for leaf in range(transfer.shape[0]):
        high, low = split(transfer[leaf])
        full = times(high.T, basis[leaf]) + times(low.T, basis[leaf])
        full_high, full_low = split(full)
        weights[leaf] = jnp.concatenate([full_high, full_high, full_low], axis=0)


def base_kernel(coupled, basis, near, down_high, down_low, own, beside, *refs):
    pairs, base, part = refs[:-2], refs[-2], refs[-1]
    rank = basis.shape[1]
    for pair in range(coupled.shape[0]):
        both = coupled[pair].astype(bf16)
        for half in range(2):
            leaf = 2 * pair + half
            far = times(both[:, half * rank : (half + 1) * rank], basis[leaf])
            base[leaf] = far + near[leaf]
    place = lax.axis_index("leaf")
    chip, core = place // 2, place % 2
    total = down_product(down_high, down_low, own[...], chip, core)
    total = total + down_product(down_high, down_low, beside[...], chip ^ 1, core)
    for step, pair in enumerate(pairs):
        at = chip ^ (2 + step + len(pairs) * core)
        total = total + down_product(down_high, down_low, pair[...], at, core)
    part[...] = total


def relay_kernel(count, *refs):
    out = refs[-1]
    for i in range(count):
        out[i] = refs[i][...]


def far_kernel(peer_count, list_in, count_in, *refs):
    peers = refs[:peer_count]
    coupling, after, coupled, table, far_list, far_count, sem = refs[peer_count:]
    copies = [
        pltpu.make_async_copy(list_in, far_list, sem.at[0]),
        pltpu.make_async_copy(count_in, far_count, sem.at[1]),
    ]
    for copy in copies:
        copy.start()
    leaves, slots, rank = coupling.shape[0], coupling.shape[1], coupling.shape[2]
    rows = table.shape[1]
    pair_count = leaves // 2
    empty = peer_count * leaves
    table[empty] = jnp.zeros(table.shape[1:], bf16)
    odd = lax.axis_index("leaf") % 2 == 1
    for peer in range(peer_count):
        begin = jnp.where(odd, mirrored(peer + 1, peer_count + 1) - 1, peer) * leaves
        for pair in range(pair_count):
            block = peers[peer][pair]
            first, second = block[:, :rank], block[:, rank:]
            table[begin + 2 * pair] = jnp.concatenate([first, first], axis=1)
            table[begin + 2 * pair + 1] = jnp.concatenate([second, second], axis=1)
    for copy in copies:
        copy.wait()
    own = lax.axis_index("list")
    lower = lax.broadcasted_iota(jnp.int32, (rows, 2 * rank), 1) < rank

    def entry(leaf, slot):
        source = far_list[slot, leaf]
        device = source // leaves
        place = ((device ^ own) - 1) * leaves + (source - device * leaves)
        return jnp.where(slot < far_count[0, leaf], place, empty)

    def one(leaf):
        lefts, rights = [], []
        for slot in range(0, slots, 2):
            lefts.append(
                jnp.where(lower, table[entry(leaf, slot)], table[entry(leaf, slot + 1)])
            )
            rights.append(
                jnp.concatenate([coupling[leaf, slot], coupling[leaf, slot + 1]], axis=1)
            )
        return times_transposed(
            jnp.concatenate(lefts, axis=1), jnp.concatenate(rights, axis=1)
        )

    for pair in range(pair_count):
        coupled[pair] = jnp.concatenate([one(2 * pair), one(2 * pair + 1)], axis=1)


def down_product(down_high, down_low, both, chip_at, core):
    first, second = 2 * chip_at + core, 2 * chip_at + 1 - core
    high = jnp.concatenate([down_high[first], down_high[second]], axis=1)
    low = jnp.concatenate([down_low[first], down_low[second]], axis=1)
    if both.dtype == bf16:
        return times_transposed(
            jnp.concatenate([both, both], axis=1), jnp.concatenate([high, low], axis=1)
        )
    both_high, both_low = split(both)
    return times_transposed(
        jnp.concatenate([both_high, both_low, both_high], axis=1),
        jnp.concatenate([high, high, low], axis=1),
    )


def down_kernel(part, swapped, down_high, down_low, weights, base, out, buffer, sem):
    place = lax.axis_index("leaf")
    chip, other = place // 2, 1 - place % 2
    total = part[...]
    steps = swapped.shape[0]
    for step in range(steps):
        at = chip ^ (2 + step + steps * other)
        total = total + down_product(down_high, down_low, swapped[step], at, other)
    high, low = split(total)
    wide = jnp.concatenate([high, low, high], axis=1)
    copies = []
    group = 2
    for begin in range(0, base.shape[0], group):
        for leaf in range(begin, begin + group):
            buffer[leaf] = (base[leaf] + times(wide, weights[leaf])).astype(bf16)
        rows = pl.ds(begin, group)
        copy = pltpu.make_async_copy(buffer.at[rows], out.at[rows], sem.at[begin // group])
        copy.start()
        copies.append(copy)
    for copy in copies:
        copy.wait()


def on_device(
    panel_charges,
    leaf_basis,
    near_blocks,
    near_list,
    far_list,
    far_count,
    far_coupling,
    leaf_transfer,
    device_transfer,
    tree_transfer,
    level_coupling,
):
    leaves, rows, panels = panel_charges.shape
    rank = leaf_basis.shape[1]
    list_count, leaf_count = lax.axis_size("list"), lax.axis_size("leaf")
    chip_count = leaf_count // 2

    def like(array, dtype=None):
        return jax.ShapeDtypeStruct(array.shape, dtype or array.dtype)

    def shape(*dims, dtype=bf16):
        return jax.ShapeDtypeStruct(dims, dtype)

    def stay(array):
        return pltpu.with_memory_space_constraint(array, pltpu.HBM)

    def exchange(array, axis, distance):
        pairs = [(i, i ^ distance) for i in range(lax.axis_size(axis))]
        return lax.ppermute(array, axis, pairs)

    def spread(array, first, second):
        places = [(l, j) for l in range(leaf_count) for j in range(list_count)]
        ends = [l * list_count + (j ^ (second if l % 2 else first)) for l, j in places]
        return lax.ppermute(array, ("leaf", "list"), list(enumerate(ends)))

    def list_exchange(array, distance):
        return spread(array, distance, mirrored(distance, list_count))

    inputs = [stay(panel_charges), stay(leaf_basis), stay(leaf_transfer)]
    inputs += [stay(device_transfer[0, 0]), near_list.T, far_list.T, far_count[None]]
    count = len(inputs)
    payload, charges, basis, transfer, near_list, far_list, far_count = pl.pallas_call(
        functools.partial(upward_kernel, count),
        out_shape=[
            shape(leaves // 2 + 1, rows, 2 * rank),
            like(panel_charges),
            like(leaf_basis),
            like(leaf_transfer),
            *[like(array) for array in inputs[4:]],
        ],
        in_specs=[anywhere] * count,
        out_specs=[whole] * 7,
        scratch_shapes=[
            pltpu.VMEM((rank, rank), f32),
            pltpu.SemaphoreType.DMA((count,)),
        ],
        compiler_params=params(4),
        name="upward",
    )(*inputs[:4], *[stay(array) for array in inputs[4:]])

    payload = pl.pallas_call(
        mark_kernel,
        out_shape=like(payload),
        in_specs=[anywhere],
        out_specs=anywhere,
        input_output_aliases={0: 0},
        compiler_params=params(1),
        cost_estimate=pl.CostEstimate(
            flops=64 * near_blocks.size * rows,
            bytes_accessed=64 * near_blocks.size,
            transcendentals=0,
        ),
        name="mark",
    )(payload)

    other_payload = exchange(payload, "leaf", 1)
    direct = [distance for distance in range(1, list_count) if distance & (distance - 1) == 0]
    arrived = {distance: list_exchange(payload, distance) for distance in direct}

    terms = pl.pallas_call(
        terms_kernel,
        out_shape=shape(rows, 2 * rank, dtype=f32),
        in_specs=[whole] * 2,
        out_specs=whole,
        compiler_params=params(2),
        name="terms",
    )(payload, other_payload)

    far_terms = [
        spread(terms, direct[0], distance)
        for distance in range(1, list_count)
        if distance not in direct
    ]

    weights = pl.pallas_call(
        weights_kernel,
        out_shape=shape(leaves, 3 * rank, panels),
        in_specs=[whole] * 2 + [anywhere],
        out_specs=whole,
        compiler_params=params(4),
        name="weights",
    )(transfer, basis, terms)


    depth = leaf_count.bit_length() - 2
    fetched = [tree_transfer, device_transfer[0, 0], leaf_basis, far_coupling]
    near, tree_matrices, device_matrix, basis, coupling, couplings = pl.pallas_call(
        functools.partial(near_kernel, leaf_count),
        out_shape=[
            shape(leaves, rows, panels, dtype=f32),
            *[like(array) for array in fetched],
            shape(depth, *level_coupling.shape[1:], dtype=f32),
        ],
        in_specs=[anywhere, whole, whole] + [anywhere] * (2 + len(fetched)),
        out_specs=[whole] * (2 + len(fetched)),
        scratch_shapes=[
            pltpu.SMEM(near_list.shape, jnp.int32),
            pltpu.SemaphoreType.DMA((1 + len(fetched) + depth,)),
        ],
        compiler_params=params(12),
        cost_estimate=pl.CostEstimate(
            flops=2 * near_blocks.size * rows,
            bytes_accessed=2 * near_blocks.size,
            transcendentals=0,
        ),
        name="near",
    )(
        near_list,
        charges,
        near_blocks,
        weights,
        *[stay(array) for array in fetched],
        stay(level_coupling),
    )

    sums = pl.pallas_call(
        functools.partial(sum_kernel, 1 + len(direct)),
        out_shape=shape(2, rows, 2 * rank, dtype=f32),
        in_specs=[whole] * (1 + len(direct) + len(far_terms)) + [anywhere],
        out_specs=whole,
        compiler_params=params(4),
        name="group_sum",
    )(payload, *[arrived[distance] for distance in direct], *far_terms, near)
    other_sums = exchange(sums, "leaf", 1)

    bases = direct[:-1]
    forward = {}
    for base in bases:
        forward[base] = pl.pallas_call(
            forward_kernel,
            out_shape=shape(leaves // 2, rows, 2 * rank),
            in_specs=[whole, anywhere],
            out_specs=whole,
            compiler_params=params(2),
            name="forward",
        )(arrived[base], sums)

    passed = pl.pallas_call(
        pause_kernel,
        out_shape=shape(8, 128, dtype=f32),
        in_specs=[anywhere],
        out_specs=whole,
        compiler_params=params(1),
        cost_estimate=pl.CostEstimate(
            flops=64 * near_blocks.size * rows,
            bytes_accessed=64 * near_blocks.size,
            transcendentals=0,
        ),
        name="pause",
    )(sums)

    own_pair, rounded_pair = pl.pallas_call(
        pair_kernel,
        out_shape=[shape(rows, 2 * rank, dtype=f32), shape(rows, 2 * rank)],
        in_specs=[whole] * 2 + [anywhere],
        out_specs=[whole] * 2,
        compiler_params=params(2),
        name="pair",
    )(sums, other_sums, passed)

    down_high, down_low = pl.pallas_call(
        functools.partial(tree_kernel, leaf_count),
        out_shape=[
            shape(leaf_count, rank, rank),
            shape(leaf_count, rank, rank),
        ],
        in_specs=[whole] * 3 + [anywhere],
        out_specs=[whole] * 2,
        scratch_shapes=[pltpu.VMEM((2 * leaf_count, rank, rank), f32)],
        compiler_params=params(4),
        cost_estimate=pl.CostEstimate(
            flops=64 * near_blocks.size * rows,
            bytes_accessed=64 * near_blocks.size,
            transcendentals=0,
        ),
        name="tree",
    )(tree_matrices, couplings, device_matrix, own_pair)

    steps = (chip_count - 2) // 2
    received = [
        lax.ppermute(
            rounded_pair,
            "leaf",
            [(i, i ^ 2 * (2 + step + steps * (i % 2))) for i in range(leaf_count)],
        )
        for step in range(steps)
    ]
    beside = exchange(own_pair, "leaf", 2)

    skeletons = {distance: arrived[distance] for distance in direct}
    for distance in range(1, list_count):
        if distance not in direct:
            top = 1 << (distance.bit_length() - 1)
            forward[distance] = list_exchange(forward[distance ^ top], top)
            skeletons[distance] = forward[distance]

    relayed = pl.pallas_call(
        functools.partial(relay_kernel, steps),
        out_shape=shape(steps, rows, 2 * rank),
        in_specs=[whole] * steps + [anywhere],
        out_specs=whole,
        compiler_params=params(2),
        name="relay",
    )(*received, down_high)
    swapped = exchange(relayed, "leaf", 1)

    coupled = pl.pallas_call(
        functools.partial(far_kernel, list_count - 1),
        out_shape=shape(leaves // 2, rows, 2 * rank, dtype=f32),
        in_specs=[anywhere] * 2 + [whole] * list_count + [anywhere],
        out_specs=whole,
        scratch_shapes=[
            pltpu.VMEM(((list_count - 1) * leaves + 1, rows, 2 * rank), bf16),
            pltpu.SMEM(far_list.shape, jnp.int32),
            pltpu.SMEM(far_count.shape, jnp.int32),
            pltpu.SemaphoreType.DMA((2,)),
        ],
        compiler_params=params(8),
        cost_estimate=pl.CostEstimate(
            flops=2 * far_coupling.size * rows * 4,
            bytes_accessed=4 * far_coupling.size,
            transcendentals=0,
        ),
        name="far",
    )(
        far_list,
        far_count,
        *[skeletons[distance] for distance in range(1, list_count)],
        coupling,
        relayed,
    )


    base, part = pl.pallas_call(
        base_kernel,
        out_shape=[
            shape(leaves, rows, panels, dtype=f32),
            shape(rows, rank, dtype=f32),
        ],
        in_specs=[whole] * (7 + steps),
        out_specs=[whole] * 2,
        compiler_params=params(4),
        name="base",
    )(coupled, basis, near, down_high, down_low, own_pair, beside, *received)

    return pl.pallas_call(
        down_kernel,
        out_shape=shape(leaves, rows, panels),
        in_specs=[whole] * 6,
        out_specs=anywhere,
        scratch_shapes=[
            pltpu.VMEM((leaves, rows, panels), bf16),
            pltpu.SemaphoreType.DMA((leaves // 2,)),
        ],
        compiler_params=params(4),
        name="down",
    )(part, swapped, down_high, down_low, weights, base)


def solution(mesh):
    in_specs = (
        P(("leaf", "list"), None, None),
        P(("leaf", "list"), None, None),
        P(("leaf", "list"), None, None, None),
        P(("leaf", "list"), None),
        P(("leaf", "list"), None),
        P(("leaf", "list")),
        P(("leaf", "list"), None, None, None),
        P(("leaf", "list"), None, None),
        P("leaf", "list", None, None),
        P(),
        P(),
    )
    out_specs = P(("leaf", "list"), None, None)
    return jax.shard_map(
        on_device, mesh=mesh, in_specs=in_specs, out_specs=out_specs, check_vma=False
    )
```

```python
import functools

import jax
import jax.numpy as jnp
from jax import lax
from jax.experimental import pallas as pl
from jax.experimental.pallas import tpu as pltpu
from jax.sharding import PartitionSpec as P

offsets = (-3, -2, 2, 3)
f32 = jnp.float32
bf16 = jnp.bfloat16
whole = pl.BlockSpec(memory_space=pltpu.VMEM)
anywhere = pl.BlockSpec(memory_space=pl.ANY)


def params(mebibytes):
    return pltpu.CompilerParams(vmem_limit_bytes=mebibytes << 20)


def times(left, right):
    return lax.dot_general(left, right, (((1,), (0,)), ((), ())), preferred_element_type=f32)


def times_transposed(left, right):
    return lax.dot_general(left, right, (((1,), (1,)), ((), ())), preferred_element_type=f32)


def split(array):
    high = array.astype(bf16)
    return high, (array - high.astype(f32)).astype(bf16)


def exact(product, left, right):
    left_high, left_low = split(left)
    right_high, right_low = split(right)
    return product(left_high, right_high) + (
        product(left_low, right_high) + product(left_high, right_low)
    )


def mirrored(distance, count):
    bits = count.bit_length() - 1
    return sum(((distance >> i) & 1) << (bits - 1 - i) for i in range(bits))


def upward_kernel(count, *refs):
    sources = refs[:count]
    payload = refs[count]
    charges, basis, transfer, *lists, matrix, sem = refs[count + 1 :]
    targets = [charges, basis, transfer, matrix] + lists
    copies = [
        pltpu.make_async_copy(source, target, sem.at[i])
        for i, (source, target) in enumerate(zip(sources, targets))
    ]
    for copy in copies:
        copy.start()
    for copy in copies[:2]:
        copy.wait()
    pair_count = charges.shape[0] // 2
    rank = basis.shape[1]
    skeletons = []
    for pair in range(pair_count):
        halves = [
            times_transposed(charges[leaf], basis[leaf]).astype(bf16)
            for leaf in (2 * pair, 2 * pair + 1)
        ]
        skeletons.append(jnp.concatenate(halves, axis=1))
        payload[pair] = skeletons[pair]
    for copy in copies[2:]:
        copy.wait()
    high, low = split(transfer[...].reshape(2 * pair_count * rank, rank))
    row = jnp.concatenate(skeletons, axis=1)
    node = times(row, high) + times(row, low)
    term = exact(times, node, matrix[...])
    payload[pair_count] = jnp.concatenate(split(term), axis=1)


def mark_kernel(*refs):
    pass


def pause_kernel(after, out):
    out[...] = jnp.zeros_like(out)


def near_leaf(near_list, charges, blocks, row, leaf):
    total = None
    for slot in range(blocks.shape[1]):
        part = times_transposed(charges[near_list[slot, leaf]], blocks[row, slot])
        total = part if total is None else total + part
    return total


def near_kernel(leaf_count, list_in, charges, blocks, after, transfer, basis_ready, *refs):
    sources, couplings_in = refs[:4], refs[4]
    near, targets, couplings = refs[5], refs[6:10], refs[10]
    weights, near_list, sem = refs[11:]
    listed = pltpu.make_async_copy(list_in, near_list, sem.at[0])
    listed.start()
    place = lax.axis_index("leaf")
    moves = list(zip(sources, targets))
    for height in range(couplings.shape[0]):
        begin = 2 * leaf_count - 2 * (leaf_count >> height)
        moves.append((couplings_in.at[begin + (place >> height)], couplings.at[height]))
    copies = [
        pltpu.make_async_copy(source, target, sem.at[1 + i])
        for i, (source, target) in enumerate(moves)
    ]
    for copy in copies:
        copy.start()
    weigh(transfer, basis_ready, weights)
    listed.wait()
    for leaf in range(near.shape[0]):
        near[leaf] = near_leaf(near_list, charges, blocks, leaf, leaf)
    for copy in copies:
        copy.wait()


def joined(both):
    both = both.astype(f32)
    rank = both.shape[1] // 2
    return both[:, :rank] + both[:, rank:]


def terms_kernel(own, other, terms):
    last = own.shape[0] - 1
    both = jnp.concatenate([joined(own[last]), joined(other[last])], axis=1)
    terms[...] = both.astype(bf16)


def pair_kernel(mine, theirs, *refs):
    pair, rounded = refs[-2:]
    rank = pair.shape[1] // 2
    odd = lax.axis_index("leaf") % 2 == 1
    far = jnp.where(odd, mine[1], theirs[1])
    flipped = jnp.concatenate([far[:, rank:], far[:, :rank]], axis=1)
    near = jnp.concatenate([mine[0][:, :rank], theirs[0][:, :rank]], axis=1)
    total = near + jnp.where(odd, far, flipped)
    pair[...] = total
    rounded[...] = total.astype(bf16)


def forward_kernel(payload, near, copy):
    copy[...] = payload[pl.ds(0, copy.shape[0])]


def sum_kernel(count, *refs):
    arrays, pairs, sums = refs[:count], refs[count:-2], refs[-1]
    total = None
    for array in arrays:
        part = joined(array[array.shape[0] - 1])
        total = part if total is None else total + part
    sums[0] = jnp.concatenate([total, jnp.zeros_like(total)], axis=1)
    total = jnp.zeros(sums.shape[1:], f32)
    for pair in pairs:
        total = total + pair[...]
    sums[1] = total


def tree_kernel(
    leaf_count, tree, couplings, matrix, sums, down_high, down_low, down
):
    rank = matrix.shape[0]
    depth = leaf_count.bit_length() - 2
    place = lax.axis_index("leaf")
    begins = [2 * leaf_count - 2 * (leaf_count >> height) for height in range(depth)]
    down[...] = jnp.zeros_like(down)
    back = matrix[...]
    for height in range(depth):
        members = leaf_count >> height
        spot = place >> height
        for slot, offset in enumerate(offsets):
            source = spot + offset
            usable = jnp.logical_and(source >= 0, source < members)
            if abs(offset) == 3:
                usable = jnp.logical_and(usable, spot % 2 == (0 if offset > 0 else 1))
            entry = begins[height] + jnp.clip(source, 0, members - 1)
            part = exact(times, back, couplings[height, slot])
            down[entry] += jnp.where(usable, part, jnp.zeros_like(part))
        if height < depth - 1:
            back = exact(times, back, tree[begins[height] + spot])
    for height in reversed(range(depth - 1)):
        for parent in range(leaf_count >> (height + 1)):
            for child in (2 * parent, 2 * parent + 1):
                down[begins[height] + child] += exact(
                    times_transposed, down[begins[height + 1] + parent], tree[begins[height] + child]
                )
    for node in range(leaf_count):
        high, low = split(down[node])
        down_high[node] = high
        down_low[node] = low


def weigh(transfer, basis, weights):
    for leaf in range(transfer.shape[0]):
        high, low = split(transfer[leaf])
        full = times(high.T, basis[leaf]) + times(low.T, basis[leaf])
        full_high, full_low = split(full)
        weights[leaf] = jnp.concatenate([full_high, full_high, full_low], axis=0)


def base_kernel(coupled, basis, near, down_high, down_low, own, beside, *refs):
    pairs, base, part = refs[:-2], refs[-2], refs[-1]
    rank = basis.shape[1]
    for pair in range(coupled.shape[0]):
        both = coupled[pair].astype(bf16)
        for half in range(2):
            leaf = 2 * pair + half
            far = times(both[:, half * rank : (half + 1) * rank], basis[leaf])
            base[leaf] = far + near[leaf]
    place = lax.axis_index("leaf")
    chip, core = place // 2, place % 2
    total = down_product(down_high, down_low, own[...], chip, core)
    total = total + down_product(down_high, down_low, beside[...], chip ^ 1, core)
    for step, pair in enumerate(pairs):
        at = chip ^ (2 + step + len(pairs) * core)
        total = total + down_product(down_high, down_low, pair[...], at, core)
    part[...] = total


def relay_kernel(count, *refs):
    out = refs[-1]
    for i in range(count):
        out[i] = refs[i][...]


def far_kernel(peer_count, list_in, count_in, *refs):
    peers = refs[:peer_count]
    coupling, after, coupled, table, rights, far_list, far_count, sem = refs[peer_count:]
    copies = [
        pltpu.make_async_copy(list_in, far_list, sem.at[0]),
        pltpu.make_async_copy(count_in, far_count, sem.at[1]),
    ]
    for copy in copies:
        copy.start()
    leaves, slots, rank = coupling.shape[0], coupling.shape[1], coupling.shape[2]
    rows = table.shape[1]
    empty = peer_count * leaves
    table[empty] = jnp.zeros(table.shape[1:], bf16)
    odd = lax.axis_index("leaf") % 2 == 1
    for peer in range(peer_count):
        begin = jnp.where(odd, mirrored(peer + 1, peer_count + 1) - 1, peer) * leaves
        for pair in range(leaves // 2):
            block = peers[peer][pair]
            first, second = block[:, :rank], block[:, rank:]
            table[begin + 2 * pair] = jnp.concatenate([first, first], axis=1)
            table[begin + 2 * pair + 1] = jnp.concatenate([second, second], axis=1)
    for leaf in range(leaves // 2):
        for slot in range(0, slots, 2):
            rights[leaf, :, rank * slot : rank * (slot + 2)] = jnp.concatenate(
                [coupling[leaf, slot], coupling[leaf, slot + 1]], axis=1
            )
    own = lax.axis_index("list")
    lower = lax.broadcasted_iota(jnp.int32, (rows, 2 * rank), 1) < rank
    for copy in copies:
        copy.wait()

    def entry(leaf, slot):
        source = far_list[slot, leaf]
        device = source // leaves
        place = ((device ^ own) - 1) * leaves + (source - device * leaves)
        return jnp.where(slot < far_count[0, leaf], place, empty)

    def one(leaf):
        lefts = [
            jnp.where(lower, table[entry(leaf, slot)], table[entry(leaf, slot + 1)])
            for slot in range(0, slots, 2)
        ]
        if leaf < leaves // 2:
            right = rights[leaf]
        else:
            right = jnp.concatenate(
                [
                    jnp.concatenate([coupling[leaf, slot], coupling[leaf, slot + 1]], axis=1)
                    for slot in range(0, slots, 2)
                ],
                axis=1,
            )
        return times_transposed(jnp.concatenate(lefts, axis=1), right)

    for pair in range(leaves // 2):
        coupled[pair] = jnp.concatenate([one(2 * pair), one(2 * pair + 1)], axis=1)


def down_product(down_high, down_low, both, chip_at, core):
    first, second = 2 * chip_at + core, 2 * chip_at + 1 - core
    high = jnp.concatenate([down_high[first], down_high[second]], axis=1)
    low = jnp.concatenate([down_low[first], down_low[second]], axis=1)
    if both.dtype == bf16:
        return times_transposed(
            jnp.concatenate([both, both], axis=1), jnp.concatenate([high, low], axis=1)
        )
    both_high, both_low = split(both)
    return times_transposed(
        jnp.concatenate([both_high, both_low, both_high], axis=1),
        jnp.concatenate([high, high, low], axis=1),
    )


def down_kernel(part, swapped, down_high, down_low, weights, base, out, buffer, sem):
    place = lax.axis_index("leaf")
    chip, other = place // 2, 1 - place % 2
    total = part[...]
    steps = swapped.shape[0]
    for step in range(steps):
        at = chip ^ (2 + step + steps * other)
        total = total + down_product(down_high, down_low, swapped[step], at, other)
    high, low = split(total)
    wide = jnp.concatenate([high, low, high], axis=1)
    copies = []
    group = 2
    for begin in range(0, base.shape[0], group):
        for leaf in range(begin, begin + group):
            buffer[leaf] = (base[leaf] + times(wide, weights[leaf])).astype(bf16)
        rows = pl.ds(begin, group)
        copy = pltpu.make_async_copy(buffer.at[rows], out.at[rows], sem.at[begin // group])
        copy.start()
        copies.append(copy)
    for copy in copies:
        copy.wait()


def on_device(
    panel_charges,
    leaf_basis,
    near_blocks,
    near_list,
    far_list,
    far_count,
    far_coupling,
    leaf_transfer,
    device_transfer,
    tree_transfer,
    level_coupling,
):
    leaves, rows, panels = panel_charges.shape
    rank = leaf_basis.shape[1]
    list_count, leaf_count = lax.axis_size("list"), lax.axis_size("leaf")
    chip_count = leaf_count // 2

    def like(array, dtype=None):
        return jax.ShapeDtypeStruct(array.shape, dtype or array.dtype)

    def shape(*dims, dtype=bf16):
        return jax.ShapeDtypeStruct(dims, dtype)

    def stay(array):
        return pltpu.with_memory_space_constraint(array, pltpu.HBM)

    def exchange(array, axis, distance):
        pairs = [(i, i ^ distance) for i in range(lax.axis_size(axis))]
        return lax.ppermute(array, axis, pairs)

    def spread(array, first, second):
        places = [(l, j) for l in range(leaf_count) for j in range(list_count)]
        ends = [l * list_count + (j ^ (second if l % 2 else first)) for l, j in places]
        return lax.ppermute(array, ("leaf", "list"), list(enumerate(ends)))

    def list_exchange(array, distance):
        return spread(array, distance, mirrored(distance, list_count))

    inputs = [stay(panel_charges), stay(leaf_basis), stay(leaf_transfer)]
    inputs += [stay(device_transfer[0, 0]), near_list.T, far_list.T, far_count[None]]
    count = len(inputs)
    payload, charges, basis, transfer, near_list, far_list, far_count = pl.pallas_call(
        functools.partial(upward_kernel, count),
        out_shape=[
            shape(leaves // 2 + 1, rows, 2 * rank),
            like(panel_charges),
            like(leaf_basis),
            like(leaf_transfer),
            *[like(array) for array in inputs[4:]],
        ],
        in_specs=[anywhere] * count,
        out_specs=[whole] * 7,
        scratch_shapes=[
            pltpu.VMEM((rank, rank), f32),
            pltpu.SemaphoreType.DMA((count,)),
        ],
        compiler_params=params(4),
        name="upward",
    )(*inputs[:4], *[stay(array) for array in inputs[4:]])

    payload = pl.pallas_call(
        mark_kernel,
        out_shape=like(payload),
        in_specs=[anywhere],
        out_specs=anywhere,
        input_output_aliases={0: 0},
        compiler_params=params(1),
        cost_estimate=pl.CostEstimate(
            flops=64 * near_blocks.size * rows,
            bytes_accessed=64 * near_blocks.size,
            transcendentals=0,
        ),
        name="mark",
    )(payload)

    other_payload = exchange(payload, "leaf", 1)
    direct = [distance for distance in range(1, list_count) if distance & (distance - 1) == 0]
    arrived = {distance: list_exchange(payload, distance) for distance in direct}

    terms = pl.pallas_call(
        terms_kernel,
        out_shape=shape(rows, 2 * rank),
        in_specs=[whole] * 2,
        out_specs=whole,
        compiler_params=params(2),
        name="terms",
    )(payload, other_payload)

    far_terms = [
        spread(terms, direct[0], distance)
        for distance in range(1, list_count)
        if distance not in direct
    ]

    depth = leaf_count.bit_length() - 2
    fetched = [tree_transfer, device_transfer[0, 0], leaf_basis, far_coupling]
    near, tree_matrices, device_matrix, basis_later, coupling, couplings, weights = pl.pallas_call(
        functools.partial(near_kernel, leaf_count),
        out_shape=[
            shape(leaves, rows, panels, dtype=f32),
            *[like(array) for array in fetched],
            shape(depth, *level_coupling.shape[1:], dtype=f32),
            shape(leaves, 3 * rank, panels),
        ],
        in_specs=[anywhere, whole, whole, anywhere, whole, whole] + [anywhere] * (1 + len(fetched)),
        out_specs=[whole] * (3 + len(fetched)),
        scratch_shapes=[
            pltpu.SMEM(near_list.shape, jnp.int32),
            pltpu.SemaphoreType.DMA((1 + len(fetched) + depth,)),
        ],
        compiler_params=params(12),
        cost_estimate=pl.CostEstimate(
            flops=2 * near_blocks.size * rows,
            bytes_accessed=2 * near_blocks.size,
            transcendentals=0,
        ),
        name="near",
    )(
        near_list,
        charges,
        near_blocks,
        terms,
        transfer,
        basis,
        *[stay(array) for array in fetched],
        stay(level_coupling),
    )

    sums = pl.pallas_call(
        functools.partial(sum_kernel, 1 + len(direct)),
        out_shape=shape(2, rows, 2 * rank, dtype=f32),
        in_specs=[whole] * (1 + len(direct) + len(far_terms)) + [anywhere],
        out_specs=whole,
        compiler_params=params(4),
        name="group_sum",
    )(payload, *[arrived[distance] for distance in direct], *far_terms, near)
    other_sums = exchange(sums, "leaf", 1)

    bases = direct[:-1]
    forward = {}
    for base in bases:
        forward[base] = pl.pallas_call(
            forward_kernel,
            out_shape=shape(leaves // 2, rows, 2 * rank),
            in_specs=[whole, anywhere],
            out_specs=whole,
            compiler_params=params(2),
            name="forward",
        )(arrived[base], sums)

    passed = pl.pallas_call(
        pause_kernel,
        out_shape=shape(8, 128, dtype=f32),
        in_specs=[anywhere],
        out_specs=whole,
        compiler_params=params(1),
        cost_estimate=pl.CostEstimate(
            flops=64 * near_blocks.size * rows,
            bytes_accessed=64 * near_blocks.size,
            transcendentals=0,
        ),
        name="pause",
    )(sums)

    own_pair, rounded_pair = pl.pallas_call(
        pair_kernel,
        out_shape=[shape(rows, 2 * rank, dtype=f32), shape(rows, 2 * rank)],
        in_specs=[whole] * 2 + [anywhere],
        out_specs=[whole] * 2,
        compiler_params=params(2),
        name="pair",
    )(sums, other_sums, passed)

    down_high, down_low = pl.pallas_call(
        functools.partial(tree_kernel, leaf_count),
        out_shape=[
            shape(leaf_count, rank, rank),
            shape(leaf_count, rank, rank),
        ],
        in_specs=[whole] * 3 + [anywhere],
        out_specs=[whole] * 2,
        scratch_shapes=[pltpu.VMEM((2 * leaf_count, rank, rank), f32)],
        compiler_params=params(4),
        cost_estimate=pl.CostEstimate(
            flops=64 * near_blocks.size * rows,
            bytes_accessed=64 * near_blocks.size,
            transcendentals=0,
        ),
        name="tree",
    )(tree_matrices, couplings, device_matrix, own_pair)

    steps = (chip_count - 2) // 2
    received = [
        lax.ppermute(
            rounded_pair,
            "leaf",
            [(i, i ^ 2 * (2 + step + steps * (i % 2))) for i in range(leaf_count)],
        )
        for step in range(steps)
    ]
    beside = exchange(own_pair, "leaf", 2)

    skeletons = {distance: arrived[distance] for distance in direct}
    for distance in range(1, list_count):
        if distance not in direct:
            top = 1 << (distance.bit_length() - 1)
            forward[distance] = list_exchange(forward[distance ^ top], top)
            skeletons[distance] = forward[distance]

    relayed = pl.pallas_call(
        functools.partial(relay_kernel, steps),
        out_shape=shape(steps, rows, 2 * rank),
        in_specs=[whole] * steps + [anywhere],
        out_specs=whole,
        compiler_params=params(2),
        name="relay",
    )(*received, down_high)
    swapped = exchange(relayed, "leaf", 1)

    coupled = pl.pallas_call(
        functools.partial(far_kernel, list_count - 1),
        out_shape=shape(leaves // 2, rows, 2 * rank, dtype=f32),
        in_specs=[anywhere] * 2 + [whole] * list_count + [anywhere],
        out_specs=whole,
        scratch_shapes=[
            pltpu.VMEM(((list_count - 1) * leaves + 1, rows, 2 * rank), bf16),
            pltpu.VMEM((leaves, rank, far_list.shape[0] * rank), bf16),
            pltpu.SMEM(far_list.shape, jnp.int32),
            pltpu.SMEM(far_count.shape, jnp.int32),
            pltpu.SemaphoreType.DMA((2,)),
        ],
        compiler_params=params(8),
        cost_estimate=pl.CostEstimate(
            flops=2 * far_coupling.size * rows * 4,
            bytes_accessed=4 * far_coupling.size,
            transcendentals=0,
        ),
        name="far",
    )(
        far_list,
        far_count,
        *[skeletons[distance] for distance in range(1, list_count)],
        coupling,
        relayed,
    )


    base, part = pl.pallas_call(
        base_kernel,
        out_shape=[
            shape(leaves, rows, panels, dtype=f32),
            shape(rows, rank, dtype=f32),
        ],
        in_specs=[whole] * (7 + steps),
        out_specs=[whole] * 2,
        compiler_params=params(4),
        name="base",
    )(coupled, basis_later, near, down_high, down_low, own_pair, beside, *received)

    return pl.pallas_call(
        down_kernel,
        out_shape=shape(leaves, rows, panels),
        in_specs=[whole] * 6,
        out_specs=anywhere,
        scratch_shapes=[
            pltpu.VMEM((leaves, rows, panels), bf16),
            pltpu.SemaphoreType.DMA((leaves // 2,)),
        ],
        compiler_params=params(4),
        name="down",
    )(part, swapped, down_high, down_low, weights, base)


def solution(mesh):
    in_specs = (
        P(("leaf", "list"), None, None),
        P(("leaf", "list"), None, None),
        P(("leaf", "list"), None, None, None),
        P(("leaf", "list"), None),
        P(("leaf", "list"), None),
        P(("leaf", "list")),
        P(("leaf", "list"), None, None, None),
        P(("leaf", "list"), None, None),
        P("leaf", "list", None, None),
        P(),
        P(),
    )
    out_specs = P(("leaf", "list"), None, None)
    return jax.shard_map(
        on_device, mesh=mesh, in_specs=in_specs, out_specs=out_specs, check_vma=False
    )
```

```python
import functools

import jax
import jax.numpy as jnp
from jax import lax
from jax.experimental import pallas as pl
from jax.experimental.pallas import tpu as pltpu
from jax.sharding import PartitionSpec as P

offsets = (-3, -2, 2, 3)
f32 = jnp.float32
bf16 = jnp.bfloat16
whole = pl.BlockSpec(memory_space=pltpu.VMEM)
anywhere = pl.BlockSpec(memory_space=pl.ANY)


def params(mebibytes):
    return pltpu.CompilerParams(vmem_limit_bytes=mebibytes << 20)


def times(left, right):
    return lax.dot_general(left, right, (((1,), (0,)), ((), ())), preferred_element_type=f32)


def times_transposed(left, right):
    return lax.dot_general(left, right, (((1,), (1,)), ((), ())), preferred_element_type=f32)


def split(array):
    high = array.astype(bf16)
    return high, (array - high.astype(f32)).astype(bf16)


def exact(product, left, right):
    left_high, left_low = split(left)
    right_high, right_low = split(right)
    return product(left_high, right_high) + (
        product(left_low, right_high) + product(left_high, right_low)
    )


def mirrored(distance, count):
    bits = count.bit_length() - 1
    return sum(((distance >> i) & 1) << (bits - 1 - i) for i in range(bits))


def upward_kernel(count, *refs):
    sources = refs[:count]
    payload = refs[count]
    charges, basis, transfer, *lists, matrix, sem = refs[count + 1 :]
    targets = [charges, basis, transfer, matrix] + lists
    copies = [
        pltpu.make_async_copy(source, target, sem.at[i])
        for i, (source, target) in enumerate(zip(sources, targets))
    ]
    for copy in copies:
        copy.start()
    for copy in copies[:2]:
        copy.wait()
    pair_count = charges.shape[0] // 2
    rank = basis.shape[1]
    skeletons = []
    for pair in range(pair_count):
        halves = [
            times_transposed(charges[leaf], basis[leaf]).astype(bf16)
            for leaf in (2 * pair, 2 * pair + 1)
        ]
        skeletons.append(jnp.concatenate(halves, axis=1))
        payload[pair] = skeletons[pair]
    for copy in copies[2:]:
        copy.wait()
    high, low = split(transfer[...].reshape(2 * pair_count * rank, rank))
    row = jnp.concatenate(skeletons, axis=1)
    node = times(row, high) + times(row, low)
    term = exact(times, node, matrix[...])
    payload[pair_count] = jnp.concatenate(split(term), axis=1)


def mark_kernel(*refs):
    pass


def pause_kernel(after, out):
    out[...] = jnp.zeros_like(out)


def near_leaf(near_list, charges, blocks, row, leaf):
    total = None
    for slot in range(blocks.shape[1]):
        part = times_transposed(charges[near_list[slot, leaf]], blocks[row, slot])
        total = part if total is None else total + part
    return total


def near_kernel(leaf_count, list_in, charges, blocks, after, transfer, basis_ready, *refs):
    sources, couplings_in = refs[:4], refs[4]
    near, targets, couplings = refs[5], refs[6:10], refs[10]
    weights, near_list, sem = refs[11:]
    listed = pltpu.make_async_copy(list_in, near_list, sem.at[0])
    listed.start()
    place = lax.axis_index("leaf")
    moves = list(zip(sources, targets))
    for height in range(couplings.shape[0]):
        begin = 2 * leaf_count - 2 * (leaf_count >> height)
        moves.append((couplings_in.at[begin + (place >> height)], couplings.at[height]))
    copies = [
        pltpu.make_async_copy(source, target, sem.at[1 + i])
        for i, (source, target) in enumerate(moves)
    ]
    for copy in copies:
        copy.start()
    weigh(transfer, basis_ready, weights)
    listed.wait()
    for leaf in range(near.shape[0]):
        near[leaf] = near_leaf(near_list, charges, blocks, leaf, leaf)
    for copy in copies:
        copy.wait()


def joined(both):
    both = both.astype(f32)
    rank = both.shape[1] // 2
    return both[:, :rank] + both[:, rank:]


def terms_kernel(own, other, terms):
    last = own.shape[0] - 1
    both = jnp.concatenate([joined(own[last]), joined(other[last])], axis=1)
    terms[...] = both.astype(bf16)


def pair_kernel(mine, theirs, *refs):
    pair, rounded = refs[-2:]
    rank = pair.shape[1] // 2
    odd = lax.axis_index("leaf") % 2 == 1
    far = jnp.where(odd, mine[1], theirs[1])
    flipped = jnp.concatenate([far[:, rank:], far[:, :rank]], axis=1)
    near = jnp.concatenate([mine[0][:, :rank], theirs[0][:, :rank]], axis=1)
    total = near + jnp.where(odd, far, flipped)
    pair[...] = total
    rounded[...] = total.astype(bf16)


def forward_kernel(payload, near, copy):
    copy[...] = payload[pl.ds(0, copy.shape[0])]


def sum_kernel(count, *refs):
    arrays, pairs, sums = refs[:count], refs[count:-2], refs[-1]
    total = None
    for array in arrays:
        part = joined(array[array.shape[0] - 1])
        total = part if total is None else total + part
    sums[0] = jnp.concatenate([total, jnp.zeros_like(total)], axis=1)
    total = jnp.zeros(sums.shape[1:], f32)
    for pair in pairs:
        total = total + pair[...]
    sums[1] = total


def tree_kernel(
    leaf_count, tree, couplings, matrix, sums, down_high, down_low, down
):
    rank = matrix.shape[0]
    depth = leaf_count.bit_length() - 2
    place = lax.axis_index("leaf")
    begins = [2 * leaf_count - 2 * (leaf_count >> height) for height in range(depth)]
    down[...] = jnp.zeros_like(down)
    back = matrix[...]
    for height in range(depth):
        members = leaf_count >> height
        spot = place >> height
        for slot, offset in enumerate(offsets):
            source = spot + offset
            usable = jnp.logical_and(source >= 0, source < members)
            if abs(offset) == 3:
                usable = jnp.logical_and(usable, spot % 2 == (0 if offset > 0 else 1))
            entry = begins[height] + jnp.clip(source, 0, members - 1)
            part = exact(times, back, couplings[height, slot])
            down[entry] += jnp.where(usable, part, jnp.zeros_like(part))
        if height < depth - 1:
            back = exact(times, back, tree[begins[height] + spot])
    for height in reversed(range(depth - 1)):
        for parent in range(leaf_count >> (height + 1)):
            for child in (2 * parent, 2 * parent + 1):
                down[begins[height] + child] += exact(
                    times_transposed, down[begins[height + 1] + parent], tree[begins[height] + child]
                )
    for node in range(leaf_count):
        high, low = split(down[node])
        down_high[node] = high
        down_low[node] = low


def weigh(transfer, basis, weights):
    for leaf in range(transfer.shape[0]):
        high, low = split(transfer[leaf])
        full = times(high.T, basis[leaf]) + times(low.T, basis[leaf])
        weights[leaf] = full.astype(bf16)


def base_kernel(coupled, basis, near, down_high, down_low, own, *refs):
    pairs, base, part = refs[:-2], refs[-2], refs[-1]
    rank = basis.shape[1]
    for pair in range(coupled.shape[0]):
        both = coupled[pair].astype(bf16)
        for half in range(2):
            leaf = 2 * pair + half
            far = times(both[:, half * rank : (half + 1) * rank], basis[leaf])
            base[leaf] = far + near[leaf]
    place = lax.axis_index("leaf")
    chip, core = place // 2, place % 2
    total = down_product(down_high, down_low, own[...], chip, core)
    for step, pair in enumerate(pairs):
        at = chip ^ (2 + step + len(pairs) * core)
        total = total + down_product(down_high, down_low, pair[...], at, core)
    part[...] = total


def relay_kernel(count, *refs):
    out = refs[-1]
    for i in range(count):
        out[i] = refs[i][...]


def far_kernel(peer_count, list_in, count_in, *refs):
    peers = refs[:peer_count]
    coupling, after, coupled, table = refs[peer_count:]
    far_list, far_count = list_in[...], count_in[...]
    leaves, slots, rank = coupling.shape[0], coupling.shape[1], coupling.shape[2]
    rows = table.shape[1]
    empty = peer_count * leaves
    table[empty] = jnp.zeros(table.shape[1:], bf16)
    odd = lax.axis_index("leaf") % 2 == 1
    for peer in range(peer_count):
        begin = jnp.where(odd, mirrored(peer + 1, peer_count + 1) - 1, peer) * leaves
        for pair in range(leaves // 2):
            block = peers[peer][pair]
            first, second = block[:, :rank], block[:, rank:]
            table[begin + 2 * pair] = jnp.concatenate([first, first], axis=1)
            table[begin + 2 * pair + 1] = jnp.concatenate([second, second], axis=1)
    own = lax.axis_index("list")
    lower = lax.broadcasted_iota(jnp.int32, (rows, 2 * rank), 1) < rank

    def entry(leaf, slot):
        source = far_list[slot, leaf]
        device = source // leaves
        place = ((device ^ own) - 1) * leaves + (source - device * leaves)
        return jnp.where(slot < far_count[0, leaf], place, empty)

    def one(leaf):
        lefts = [
            jnp.where(lower, table[entry(leaf, slot)], table[entry(leaf, slot + 1)])
            for slot in range(0, slots, 2)
        ]
        right = jnp.concatenate(
            [
                jnp.concatenate([coupling[leaf, slot], coupling[leaf, slot + 1]], axis=1)
                for slot in range(0, slots, 2)
            ],
            axis=1,
        )
        return times_transposed(jnp.concatenate(lefts, axis=1), right)

    for pair in range(leaves // 2):
        coupled[pair] = jnp.concatenate([one(2 * pair), one(2 * pair + 1)], axis=1)


def down_product(down_high, down_low, both, chip_at, core):
    first, second = 2 * chip_at + core, 2 * chip_at + 1 - core
    high = jnp.concatenate([down_high[first], down_high[second]], axis=1)
    low = jnp.concatenate([down_low[first], down_low[second]], axis=1)
    if both.dtype == bf16:
        return times_transposed(
            jnp.concatenate([both, both], axis=1), jnp.concatenate([high, low], axis=1)
        )
    both_high, both_low = split(both)
    return times_transposed(
        jnp.concatenate([both_high, both_low, both_high], axis=1),
        jnp.concatenate([high, high, low], axis=1),
    )


def down_kernel(part, beside, swapped, down_high, down_low, weights, base, out, buffer, sem):
    place = lax.axis_index("leaf")
    chip, other = place // 2, 1 - place % 2
    total = part[...]
    total = total + down_product(down_high, down_low, beside[...], chip ^ 1, 1 - other)
    steps = swapped.shape[0]
    for step in range(steps):
        at = chip ^ (2 + step + steps * other)
        total = total + down_product(down_high, down_low, swapped[step], at, other)
    wide = total.astype(bf16)
    copies = []
    group = 2
    for begin in range(0, base.shape[0], group):
        for leaf in range(begin, begin + group):
            buffer[leaf] = (base[leaf] + times(wide, weights[leaf])).astype(bf16)
        rows = pl.ds(begin, group)
        copy = pltpu.make_async_copy(buffer.at[rows], out.at[rows], sem.at[begin // group])
        copy.start()
        copies.append(copy)
    for copy in copies:
        copy.wait()


def on_device(
    panel_charges,
    leaf_basis,
    near_blocks,
    near_list,
    far_list,
    far_count,
    far_coupling,
    leaf_transfer,
    device_transfer,
    tree_transfer,
    level_coupling,
):
    leaves, rows, panels = panel_charges.shape
    rank = leaf_basis.shape[1]
    list_count, leaf_count = lax.axis_size("list"), lax.axis_size("leaf")
    chip_count = leaf_count // 2

    def like(array, dtype=None):
        return jax.ShapeDtypeStruct(array.shape, dtype or array.dtype)

    def shape(*dims, dtype=bf16):
        return jax.ShapeDtypeStruct(dims, dtype)

    def stay(array):
        return pltpu.with_memory_space_constraint(array, pltpu.HBM)

    def exchange(array, axis, distance):
        pairs = [(i, i ^ distance) for i in range(lax.axis_size(axis))]
        return lax.ppermute(array, axis, pairs)

    def spread(array, first, second):
        places = [(l, j) for l in range(leaf_count) for j in range(list_count)]
        ends = [l * list_count + (j ^ (second if l % 2 else first)) for l, j in places]
        return lax.ppermute(array, ("leaf", "list"), list(enumerate(ends)))

    def list_exchange(array, distance):
        return spread(array, distance, mirrored(distance, list_count))

    inputs = [stay(panel_charges), stay(leaf_basis), stay(leaf_transfer)]
    inputs += [stay(device_transfer[0, 0]), near_list.T, far_list.T, far_count[None]]
    count = len(inputs)
    payload, charges, basis, transfer, near_list, far_list, far_count = pl.pallas_call(
        functools.partial(upward_kernel, count),
        out_shape=[
            shape(leaves // 2 + 1, rows, 2 * rank),
            like(panel_charges),
            like(leaf_basis),
            like(leaf_transfer),
            *[like(array) for array in inputs[4:]],
        ],
        in_specs=[anywhere] * count,
        out_specs=[whole] * 7,
        scratch_shapes=[
            pltpu.VMEM((rank, rank), f32),
            pltpu.SemaphoreType.DMA((count,)),
        ],
        compiler_params=params(4),
        name="upward",
    )(*inputs[:4], *[stay(array) for array in inputs[4:]])

    payload = pl.pallas_call(
        mark_kernel,
        out_shape=like(payload),
        in_specs=[anywhere],
        out_specs=anywhere,
        input_output_aliases={0: 0},
        compiler_params=params(1),
        cost_estimate=pl.CostEstimate(
            flops=64 * near_blocks.size * rows,
            bytes_accessed=64 * near_blocks.size,
            transcendentals=0,
        ),
        name="mark",
    )(payload)

    other_payload = exchange(payload, "leaf", 1)
    direct = [distance for distance in range(1, list_count) if distance & (distance - 1) == 0]
    arrived = {distance: list_exchange(payload, distance) for distance in direct}

    terms = pl.pallas_call(
        terms_kernel,
        out_shape=shape(rows, 2 * rank),
        in_specs=[whole] * 2,
        out_specs=whole,
        compiler_params=params(2),
        name="terms",
    )(payload, other_payload)

    far_terms = [
        spread(terms, direct[0], distance)
        for distance in range(1, list_count)
        if distance not in direct
    ]

    depth = leaf_count.bit_length() - 2
    fetched = [tree_transfer, device_transfer[0, 0], leaf_basis, far_coupling]
    near, tree_matrices, device_matrix, basis_later, coupling, couplings, weights = pl.pallas_call(
        functools.partial(near_kernel, leaf_count),
        out_shape=[
            shape(leaves, rows, panels, dtype=f32),
            *[like(array) for array in fetched],
            shape(depth, *level_coupling.shape[1:], dtype=f32),
            shape(leaves, rank, panels),
        ],
        in_specs=[anywhere, whole, whole, anywhere, whole, whole] + [anywhere] * (1 + len(fetched)),
        out_specs=[whole] * (3 + len(fetched)),
        scratch_shapes=[
            pltpu.SMEM(near_list.shape, jnp.int32),
            pltpu.SemaphoreType.DMA((1 + len(fetched) + depth,)),
        ],
        compiler_params=params(12),
        cost_estimate=pl.CostEstimate(
            flops=2 * near_blocks.size * rows,
            bytes_accessed=2 * near_blocks.size,
            transcendentals=0,
        ),
        name="near",
    )(
        near_list,
        charges,
        near_blocks,
        terms,
        transfer,
        basis,
        *[stay(array) for array in fetched],
        stay(level_coupling),
    )

    sums = pl.pallas_call(
        functools.partial(sum_kernel, 1 + len(direct)),
        out_shape=shape(2, rows, 2 * rank, dtype=f32),
        in_specs=[whole] * (1 + len(direct) + len(far_terms)) + [anywhere],
        out_specs=whole,
        compiler_params=params(4),
        name="group_sum",
    )(payload, *[arrived[distance] for distance in direct], *far_terms, near)
    other_sums = exchange(sums, "leaf", 1)

    bases = direct[:-1]
    forward = {}
    for base in bases:
        forward[base] = pl.pallas_call(
            forward_kernel,
            out_shape=shape(leaves // 2, rows, 2 * rank),
            in_specs=[whole, anywhere],
            out_specs=whole,
            compiler_params=params(2),
            name="forward",
        )(arrived[base], sums)

    passed = pl.pallas_call(
        pause_kernel,
        out_shape=shape(8, 128, dtype=f32),
        in_specs=[anywhere],
        out_specs=whole,
        compiler_params=params(1),
        cost_estimate=pl.CostEstimate(
            flops=64 * near_blocks.size * rows,
            bytes_accessed=64 * near_blocks.size,
            transcendentals=0,
        ),
        name="pause",
    )(sums)

    own_pair, rounded_pair = pl.pallas_call(
        pair_kernel,
        out_shape=[shape(rows, 2 * rank, dtype=f32), shape(rows, 2 * rank)],
        in_specs=[whole] * 2 + [anywhere],
        out_specs=[whole] * 2,
        compiler_params=params(2),
        name="pair",
    )(sums, other_sums, passed)

    down_high, down_low = pl.pallas_call(
        functools.partial(tree_kernel, leaf_count),
        out_shape=[
            shape(leaf_count, rank, rank),
            shape(leaf_count, rank, rank),
        ],
        in_specs=[whole] * 3 + [anywhere],
        out_specs=[whole] * 2,
        scratch_shapes=[pltpu.VMEM((2 * leaf_count, rank, rank), f32)],
        compiler_params=params(4),
        cost_estimate=pl.CostEstimate(
            flops=64 * near_blocks.size * rows,
            bytes_accessed=64 * near_blocks.size,
            transcendentals=0,
        ),
        name="tree",
    )(tree_matrices, couplings, device_matrix, own_pair)

    steps = (chip_count - 2) // 2
    received = [
        lax.ppermute(
            rounded_pair,
            "leaf",
            [(i, i ^ 2 * (2 + step + steps * (i % 2))) for i in range(leaf_count)],
        )
        for step in range(steps)
    ]
    beside = exchange(own_pair, "leaf", 2)

    skeletons = {distance: arrived[distance] for distance in direct}
    for distance in range(1, list_count):
        if distance not in direct:
            top = 1 << (distance.bit_length() - 1)
            forward[distance] = list_exchange(forward[distance ^ top], top)
            skeletons[distance] = forward[distance]

    relayed = pl.pallas_call(
        functools.partial(relay_kernel, steps),
        out_shape=shape(steps, rows, 2 * rank),
        in_specs=[whole] * steps + [anywhere],
        out_specs=whole,
        compiler_params=params(2),
        name="relay",
    )(*received, down_high)
    swapped = exchange(relayed, "leaf", 1)

    coupled = pl.pallas_call(
        functools.partial(far_kernel, list_count - 1),
        out_shape=shape(leaves // 2, rows, 2 * rank, dtype=f32),
        in_specs=[whole] * 2 + [whole] * list_count + [anywhere],
        out_specs=whole,
        scratch_shapes=[
            pltpu.VMEM(((list_count - 1) * leaves + 1, rows, 2 * rank), bf16),
        ],
        compiler_params=params(8),
        cost_estimate=pl.CostEstimate(
            flops=2 * far_coupling.size * rows * 4,
            bytes_accessed=4 * far_coupling.size,
            transcendentals=0,
        ),
        name="far",
    )(
        far_list,
        far_count,
        *[skeletons[distance] for distance in range(1, list_count)],
        coupling,
        relayed,
    )


    base, part = pl.pallas_call(
        base_kernel,
        out_shape=[
            shape(leaves, rows, panels, dtype=f32),
            shape(rows, rank, dtype=f32),
        ],
        in_specs=[whole] * (6 + steps),
        out_specs=[whole] * 2,
        compiler_params=params(4),
        name="base",
    )(coupled, basis_later, near, down_high, down_low, own_pair, *received)

    return pl.pallas_call(
        down_kernel,
        out_shape=shape(leaves, rows, panels),
        in_specs=[whole] * 7,
        out_specs=anywhere,
        scratch_shapes=[
            pltpu.VMEM((leaves, rows, panels), bf16),
            pltpu.SemaphoreType.DMA((leaves // 2,)),
        ],
        compiler_params=params(4),
        name="down",
    )(part, beside, swapped, down_high, down_low, weights, base)


def solution(mesh):
    in_specs = (
        P(("leaf", "list"), None, None),
        P(("leaf", "list"), None, None),
        P(("leaf", "list"), None, None, None),
        P(("leaf", "list"), None),
        P(("leaf", "list"), None),
        P(("leaf", "list")),
        P(("leaf", "list"), None, None, None),
        P(("leaf", "list"), None, None),
        P("leaf", "list", None, None),
        P(),
        P(),
    )
    out_specs = P(("leaf", "list"), None, None)
    return jax.shard_map(
        on_device, mesh=mesh, in_specs=in_specs, out_specs=out_specs, check_vma=False
    )
```

```python
import functools

import jax
import jax.numpy as jnp
from jax import lax
from jax.experimental import pallas as pl
from jax.experimental.pallas import tpu as pltpu
from jax.sharding import PartitionSpec as P

f32 = jnp.float32
bf16 = jnp.bfloat16
whole = pl.BlockSpec(memory_space=pltpu.VMEM)
anywhere = pl.BlockSpec(memory_space=pl.ANY)


def params(mebibytes):
    return pltpu.CompilerParams(vmem_limit_bytes=mebibytes << 20)


def times(left, right):
    return lax.dot_general(left, right, (((1,), (0,)), ((), ())), preferred_element_type=f32)


def times_transposed(left, right):
    return lax.dot_general(left, right, (((1,), (1,)), ((), ())), preferred_element_type=f32)


def split(array):
    high = array.astype(bf16)
    return high, (array - high.astype(f32)).astype(bf16)


def exact(product, left, right):
    left_high, left_low = split(left)
    right_high, right_low = split(right)
    return product(left_high, right_high) + (
        product(left_low, right_high) + product(left_high, right_low)
    )


def mirrored(distance, count):
    bits = count.bit_length() - 1
    return sum(((distance >> i) & 1) << (bits - 1 - i) for i in range(bits))


def upward_kernel(count, *refs):
    sources = refs[:count]
    payload = refs[count]
    charges, basis, transfer, *lists, matrix, sem = refs[count + 1 :]
    targets = [charges, basis, transfer, matrix] + lists
    copies = [
        pltpu.make_async_copy(source, target, sem.at[i])
        for i, (source, target) in enumerate(zip(sources, targets))
    ]
    for copy in copies:
        copy.start()
    for copy in copies[:2]:
        copy.wait()
    pair_count = charges.shape[0] // 2
    rank = basis.shape[1]
    skeletons = []
    for pair in range(pair_count):
        halves = [
            times_transposed(charges[leaf], basis[leaf]).astype(bf16)
            for leaf in (2 * pair, 2 * pair + 1)
        ]
        skeletons.append(jnp.concatenate(halves, axis=1))
        payload[pair] = skeletons[pair]
    for copy in copies[2:]:
        copy.wait()
    high, low = split(transfer[...].reshape(2 * pair_count * rank, rank))
    row = jnp.concatenate(skeletons, axis=1)
    node = times(row, high) + times(row, low)
    term = exact(times, node, matrix[...])
    payload[pair_count] = jnp.concatenate(split(term), axis=1)


def mark_kernel(*refs):
    pass


def pause_kernel(after, out):
    out[...] = jnp.zeros_like(out)


def near_leaf(near_list, charges, blocks, row, leaf):
    total = None
    for slot in range(blocks.shape[1]):
        part = times_transposed(charges[near_list[slot, leaf]], blocks[row, slot])
        total = part if total is None else total + part
    return total


def near_kernel(leaf_count, list_in, charges, blocks, after, transfer, basis_ready, *refs):
    sources, couplings_in = refs[:4], refs[4]
    near, targets, couplings = refs[5], refs[6:10], refs[10]
    weights, near_list, sem = refs[11:]
    listed = pltpu.make_async_copy(list_in, near_list, sem.at[0])
    listed.start()
    place = lax.axis_index("leaf")
    moves = list(zip(sources, targets))
    for height in range(couplings.shape[0]):
        begin = 2 * leaf_count - 2 * (leaf_count >> height)
        moves.append((couplings_in.at[begin + (place >> height)], couplings.at[height]))
    copies = [
        pltpu.make_async_copy(source, target, sem.at[1 + i])
        for i, (source, target) in enumerate(moves)
    ]
    for copy in copies:
        copy.start()
    weigh(transfer, basis_ready, weights)
    listed.wait()
    for leaf in range(near.shape[0]):
        near[leaf] = near_leaf(near_list, charges, blocks, leaf, leaf)
    for copy in copies:
        copy.wait()


def joined(both):
    both = both.astype(f32)
    rank = both.shape[1] // 2
    return both[:, :rank] + both[:, rank:]


def terms_kernel(own, other, terms):
    last = own.shape[0] - 1
    both = jnp.concatenate([joined(own[last]), joined(other[last])], axis=1)
    terms[...] = both.astype(bf16)


def pair_kernel(mine, theirs, *refs):
    pair, rounded = refs[-2:]
    rank = pair.shape[1] // 2
    odd = lax.axis_index("leaf") % 2 == 1
    far = jnp.where(odd, mine[1], theirs[1])
    flipped = jnp.concatenate([far[:, rank:], far[:, :rank]], axis=1)
    near = jnp.concatenate([mine[0][:, :rank], theirs[0][:, :rank]], axis=1)
    total = near + jnp.where(odd, far, flipped)
    pair[...] = total
    rounded[...] = total.astype(bf16)


def forward_kernel(payload, near, copy):
    copy[...] = payload[pl.ds(0, copy.shape[0])]


def sum_kernel(count, *refs):
    arrays, pairs, sums = refs[:count], refs[count:-2], refs[-1]
    total = None
    for array in arrays:
        part = joined(array[array.shape[0] - 1])
        total = part if total is None else total + part
    sums[0] = jnp.concatenate([total, jnp.zeros_like(total)], axis=1)
    total = jnp.zeros(sums.shape[1:], f32)
    for pair in pairs:
        total = total + pair[...]
    sums[1] = total


def tree_kernel(leaf_count, tree, couplings, matrix, sums, down_high, down_low):
    depth = leaf_count.bit_length() - 2
    place = lax.axis_index("leaf")
    begins = [2 * leaf_count - 2 * (leaf_count >> height) for height in range(depth)]
    back = matrix[...]
    added = []
    for height in range(depth):
        spot = place >> height
        even = spot % 2 == 0
        picks = [(jnp.where(even, 3, 0), spot + jnp.where(even, 3, -3))]
        if height == depth - 1:
            picks.append((jnp.where(spot < 2, 2, 1), spot ^ 2))
        else:
            picks += [(1, spot - 2), (2, spot + 2)]
        added.append([(at, exact(times, back, couplings[height, slot])) for slot, at in picks])
        if height < depth - 1:
            back = exact(times, back, tree[begins[height] + spot])
    nodes = added[-1]
    for height in reversed(range(depth - 1)):
        members = leaf_count >> height
        parts = list(added[height])
        for parent, value in nodes:
            for child in (2 * parent, 2 * parent + 1):
                safe = child if isinstance(child, int) else jnp.clip(child, 0, members - 1)
                product = exact(times_transposed, value, tree[begins[height] + safe])
                parts.append((child, product))
        nodes = []
        for node in range(members):
            total = jnp.zeros(matrix.shape, f32)
            for at, value in parts:
                if isinstance(at, int):
                    total = total + value if at == node else total
                else:
                    total = total + jnp.where(at == node, value, jnp.zeros_like(value))
            nodes.append((node, total))
    for node, value in nodes:
        high, low = split(value)
        down_high[node] = high
        down_low[node] = low


def weigh(transfer, basis, weights):
    for leaf in range(transfer.shape[0]):
        high, low = split(transfer[leaf])
        full = times(high.T, basis[leaf]) + times(low.T, basis[leaf])
        weights[leaf] = full.astype(bf16)


def base_kernel(coupled, basis, near, down_high, down_low, own, *refs):
    pairs, base, part = refs[:-2], refs[-2], refs[-1]
    rank = basis.shape[1]
    for pair in range(coupled.shape[0]):
        both = coupled[pair].astype(bf16)
        for half in range(2):
            leaf = 2 * pair + half
            far = times(both[:, half * rank : (half + 1) * rank], basis[leaf])
            base[leaf] = far + near[leaf]
    place = lax.axis_index("leaf")
    chip, core = place // 2, place % 2
    total = down_product(down_high, down_low, own[...], chip, core)
    for step, pair in enumerate(pairs):
        at = chip ^ (2 + step + len(pairs) * core)
        total = total + down_product(down_high, down_low, pair[...], at, core)
    part[...] = total


def relay_kernel(count, *refs):
    out = refs[-1]
    for i in range(count):
        out[i] = refs[i][...]


def far_kernel(peer_count, list_in, count_in, *refs):
    peers = refs[:peer_count]
    coupling, after, coupled, table = refs[peer_count:]
    far_list, far_count = list_in[...], count_in[...]
    leaves, slots, rank = coupling.shape[0], coupling.shape[1], coupling.shape[2]
    rows = table.shape[1]
    empty = peer_count * leaves
    table[empty] = jnp.zeros(table.shape[1:], bf16)
    odd = lax.axis_index("leaf") % 2 == 1
    for peer in range(peer_count):
        begin = jnp.where(odd, mirrored(peer + 1, peer_count + 1) - 1, peer) * leaves
        for pair in range(leaves // 2):
            block = peers[peer][pair]
            first, second = block[:, :rank], block[:, rank:]
            table[begin + 2 * pair] = jnp.concatenate([first, first], axis=1)
            table[begin + 2 * pair + 1] = jnp.concatenate([second, second], axis=1)
    own = lax.axis_index("list")
    lower = lax.broadcasted_iota(jnp.int32, (rows, 2 * rank), 1) < rank

    def entry(leaf, slot):
        source = far_list[slot, leaf]
        device = source // leaves
        place = ((device ^ own) - 1) * leaves + (source - device * leaves)
        return jnp.where(slot < far_count[0, leaf], place, empty)

    def one(leaf):
        lefts = [
            jnp.where(lower, table[entry(leaf, slot)], table[entry(leaf, slot + 1)])
            for slot in range(0, slots, 2)
        ]
        right = jnp.concatenate(
            [
                jnp.concatenate([coupling[leaf, slot], coupling[leaf, slot + 1]], axis=1)
                for slot in range(0, slots, 2)
            ],
            axis=1,
        )
        return times_transposed(jnp.concatenate(lefts, axis=1), right)

    for pair in range(leaves // 2):
        coupled[pair] = jnp.concatenate([one(2 * pair), one(2 * pair + 1)], axis=1)


def down_product(down_high, down_low, both, chip_at, core):
    first, second = 2 * chip_at + core, 2 * chip_at + 1 - core
    high = jnp.concatenate([down_high[first], down_high[second]], axis=1)
    low = jnp.concatenate([down_low[first], down_low[second]], axis=1)
    if both.dtype == bf16:
        return times_transposed(
            jnp.concatenate([both, both], axis=1), jnp.concatenate([high, low], axis=1)
        )
    both_high, both_low = split(both)
    return times_transposed(
        jnp.concatenate([both_high, both_low, both_high], axis=1),
        jnp.concatenate([high, high, low], axis=1),
    )


def down_kernel(part, beside, swapped, down_high, down_low, weights, base, out, buffer, sem):
    place = lax.axis_index("leaf")
    chip, other = place // 2, 1 - place % 2
    total = part[...]
    total = total + down_product(down_high, down_low, beside[...], chip ^ 1, 1 - other)
    steps = swapped.shape[0]
    for step in range(steps):
        at = chip ^ (2 + step + steps * other)
        total = total + down_product(down_high, down_low, swapped[step], at, other)
    wide = total.astype(bf16)
    copies = []
    group = 2
    for begin in range(0, base.shape[0], group):
        for leaf in range(begin, begin + group):
            buffer[leaf] = (base[leaf] + times(wide, weights[leaf])).astype(bf16)
        rows = pl.ds(begin, group)
        copy = pltpu.make_async_copy(buffer.at[rows], out.at[rows], sem.at[begin // group])
        copy.start()
        copies.append(copy)
    for copy in copies:
        copy.wait()


def on_device(
    panel_charges,
    leaf_basis,
    near_blocks,
    near_list,
    far_list,
    far_count,
    far_coupling,
    leaf_transfer,
    device_transfer,
    tree_transfer,
    level_coupling,
):
    leaves, rows, panels = panel_charges.shape
    rank = leaf_basis.shape[1]
    list_count, leaf_count = lax.axis_size("list"), lax.axis_size("leaf")
    chip_count = leaf_count // 2

    def like(array, dtype=None):
        return jax.ShapeDtypeStruct(array.shape, dtype or array.dtype)

    def shape(*dims, dtype=bf16):
        return jax.ShapeDtypeStruct(dims, dtype)

    def stay(array):
        return pltpu.with_memory_space_constraint(array, pltpu.HBM)

    def exchange(array, axis, distance):
        pairs = [(i, i ^ distance) for i in range(lax.axis_size(axis))]
        return lax.ppermute(array, axis, pairs)

    def spread(array, first, second):
        places = [(l, j) for l in range(leaf_count) for j in range(list_count)]
        ends = [l * list_count + (j ^ (second if l % 2 else first)) for l, j in places]
        return lax.ppermute(array, ("leaf", "list"), list(enumerate(ends)))

    def list_exchange(array, distance):
        return spread(array, distance, mirrored(distance, list_count))

    inputs = [stay(panel_charges), stay(leaf_basis), stay(leaf_transfer)]
    inputs += [stay(device_transfer[0, 0]), near_list.T, far_list.T, far_count[None]]
    count = len(inputs)
    payload, charges, basis, transfer, near_list, far_list, far_count = pl.pallas_call(
        functools.partial(upward_kernel, count),
        out_shape=[
            shape(leaves // 2 + 1, rows, 2 * rank),
            like(panel_charges),
            like(leaf_basis),
            like(leaf_transfer),
            *[like(array) for array in inputs[4:]],
        ],
        in_specs=[anywhere] * count,
        out_specs=[whole] * 7,
        scratch_shapes=[
            pltpu.VMEM((rank, rank), f32),
            pltpu.SemaphoreType.DMA((count,)),
        ],
        compiler_params=params(4),
        name="upward",
    )(*inputs[:4], *[stay(array) for array in inputs[4:]])

    payload = pl.pallas_call(
        mark_kernel,
        out_shape=like(payload),
        in_specs=[anywhere],
        out_specs=anywhere,
        input_output_aliases={0: 0},
        compiler_params=params(1),
        cost_estimate=pl.CostEstimate(
            flops=64 * near_blocks.size * rows,
            bytes_accessed=64 * near_blocks.size,
            transcendentals=0,
        ),
        name="mark",
    )(payload)

    other_payload = exchange(payload, "leaf", 1)
    direct = [distance for distance in range(1, list_count) if distance & (distance - 1) == 0]
    arrived = {distance: list_exchange(payload, distance) for distance in direct}

    terms = pl.pallas_call(
        terms_kernel,
        out_shape=shape(rows, 2 * rank),
        in_specs=[whole] * 2,
        out_specs=whole,
        compiler_params=params(2),
        name="terms",
    )(payload, other_payload)

    far_terms = [
        spread(terms, direct[0], distance)
        for distance in range(1, list_count)
        if distance not in direct
    ]

    depth = leaf_count.bit_length() - 2
    fetched = [tree_transfer, device_transfer[0, 0], leaf_basis, far_coupling]
    near, tree_matrices, device_matrix, basis_later, coupling, couplings, weights = pl.pallas_call(
        functools.partial(near_kernel, leaf_count),
        out_shape=[
            shape(leaves, rows, panels, dtype=f32),
            *[like(array) for array in fetched],
            shape(depth, *level_coupling.shape[1:], dtype=f32),
            shape(leaves, rank, panels),
        ],
        in_specs=[anywhere, whole, whole, anywhere, whole, whole] + [anywhere] * (1 + len(fetched)),
        out_specs=[whole] * (3 + len(fetched)),
        scratch_shapes=[
            pltpu.SMEM(near_list.shape, jnp.int32),
            pltpu.SemaphoreType.DMA((1 + len(fetched) + depth,)),
        ],
        compiler_params=params(12),
        cost_estimate=pl.CostEstimate(
            flops=2 * near_blocks.size * rows,
            bytes_accessed=2 * near_blocks.size,
            transcendentals=0,
        ),
        name="near",
    )(
        near_list,
        charges,
        near_blocks,
        terms,
        transfer,
        basis,
        *[stay(array) for array in fetched],
        stay(level_coupling),
    )

    sums = pl.pallas_call(
        functools.partial(sum_kernel, 1 + len(direct)),
        out_shape=shape(2, rows, 2 * rank, dtype=f32),
        in_specs=[whole] * (1 + len(direct) + len(far_terms)) + [anywhere],
        out_specs=whole,
        compiler_params=params(4),
        name="group_sum",
    )(payload, *[arrived[distance] for distance in direct], *far_terms, near)
    other_sums = exchange(sums, "leaf", 1)

    bases = direct[:-1]
    forward = {}
    for base in bases:
        forward[base] = pl.pallas_call(
            forward_kernel,
            out_shape=shape(leaves // 2, rows, 2 * rank),
            in_specs=[whole, anywhere],
            out_specs=whole,
            compiler_params=params(2),
            name="forward",
        )(arrived[base], sums)

    passed = pl.pallas_call(
        pause_kernel,
        out_shape=shape(8, 128, dtype=f32),
        in_specs=[anywhere],
        out_specs=whole,
        compiler_params=params(1),
        cost_estimate=pl.CostEstimate(
            flops=64 * near_blocks.size * rows,
            bytes_accessed=64 * near_blocks.size,
            transcendentals=0,
        ),
        name="pause",
    )(sums)

    own_pair, rounded_pair = pl.pallas_call(
        pair_kernel,
        out_shape=[shape(rows, 2 * rank, dtype=f32), shape(rows, 2 * rank)],
        in_specs=[whole] * 2 + [anywhere],
        out_specs=[whole] * 2,
        compiler_params=params(2),
        name="pair",
    )(sums, other_sums, passed)

    down_high, down_low = pl.pallas_call(
        functools.partial(tree_kernel, leaf_count),
        out_shape=[
            shape(leaf_count, rank, rank),
            shape(leaf_count, rank, rank),
        ],
        in_specs=[whole] * 3 + [anywhere],
        out_specs=[whole] * 2,
        compiler_params=params(4),
        cost_estimate=pl.CostEstimate(
            flops=64 * near_blocks.size * rows,
            bytes_accessed=64 * near_blocks.size,
            transcendentals=0,
        ),
        name="tree",
    )(tree_matrices, couplings, device_matrix, own_pair)

    steps = (chip_count - 2) // 2
    received = [
        lax.ppermute(
            rounded_pair,
            "leaf",
            [(i, i ^ 2 * (2 + step + steps * (i % 2))) for i in range(leaf_count)],
        )
        for step in range(steps)
    ]
    beside = exchange(own_pair, "leaf", 2)

    skeletons = {distance: arrived[distance] for distance in direct}
    for distance in range(1, list_count):
        if distance not in direct:
            top = 1 << (distance.bit_length() - 1)
            forward[distance] = list_exchange(forward[distance ^ top], top)
            skeletons[distance] = forward[distance]

    relayed = pl.pallas_call(
        functools.partial(relay_kernel, steps),
        out_shape=shape(steps, rows, 2 * rank),
        in_specs=[whole] * steps + [anywhere],
        out_specs=whole,
        compiler_params=params(2),
        name="relay",
    )(*received, down_high)
    swapped = exchange(relayed, "leaf", 1)

    coupled = pl.pallas_call(
        functools.partial(far_kernel, list_count - 1),
        out_shape=shape(leaves // 2, rows, 2 * rank, dtype=f32),
        in_specs=[whole] * 2 + [whole] * list_count + [anywhere],
        out_specs=whole,
        scratch_shapes=[
            pltpu.VMEM(((list_count - 1) * leaves + 1, rows, 2 * rank), bf16),
        ],
        compiler_params=params(8),
        cost_estimate=pl.CostEstimate(
            flops=2 * far_coupling.size * rows * 4,
            bytes_accessed=4 * far_coupling.size,
            transcendentals=0,
        ),
        name="far",
    )(
        far_list,
        far_count,
        *[skeletons[distance] for distance in range(1, list_count)],
        coupling,
        relayed,
    )


    base, part = pl.pallas_call(
        base_kernel,
        out_shape=[
            shape(leaves, rows, panels, dtype=f32),
            shape(rows, rank, dtype=f32),
        ],
        in_specs=[whole] * (6 + steps),
        out_specs=[whole] * 2,
        compiler_params=params(4),
        name="base",
    )(coupled, basis_later, near, down_high, down_low, own_pair, *received)

    return pl.pallas_call(
        down_kernel,
        out_shape=shape(leaves, rows, panels),
        in_specs=[whole] * 7,
        out_specs=anywhere,
        scratch_shapes=[
            pltpu.VMEM((leaves, rows, panels), bf16),
            pltpu.SemaphoreType.DMA((leaves // 2,)),
        ],
        compiler_params=params(4),
        name="down",
    )(part, beside, swapped, down_high, down_low, weights, base)


def solution(mesh):
    in_specs = (
        P(("leaf", "list"), None, None),
        P(("leaf", "list"), None, None),
        P(("leaf", "list"), None, None, None),
        P(("leaf", "list"), None),
        P(("leaf", "list"), None),
        P(("leaf", "list")),
        P(("leaf", "list"), None, None, None),
        P(("leaf", "list"), None, None),
        P("leaf", "list", None, None),
        P(),
        P(),
    )
    out_specs = P(("leaf", "list"), None, None)
    return jax.shard_map(
        on_device, mesh=mesh, in_specs=in_specs, out_specs=out_specs, check_vma=False
    )
```

```python
import functools

import jax
import jax.numpy as jnp
from jax import lax
from jax.experimental import pallas as pl
from jax.experimental.pallas import tpu as pltpu
from jax.sharding import PartitionSpec as P

f32 = jnp.float32
bf16 = jnp.bfloat16
whole = pl.BlockSpec(memory_space=pltpu.VMEM)
anywhere = pl.BlockSpec(memory_space=pl.ANY)


def params(mebibytes):
    return pltpu.CompilerParams(vmem_limit_bytes=mebibytes << 20)


def times(left, right):
    return lax.dot_general(left, right, (((1,), (0,)), ((), ())), preferred_element_type=f32)


def times_transposed(left, right):
    return lax.dot_general(left, right, (((1,), (1,)), ((), ())), preferred_element_type=f32)


def split(array):
    high = array.astype(bf16)
    return high, (array - high.astype(f32)).astype(bf16)


def exact(product, left, right):
    left_high, left_low = split(left)
    right_high, right_low = split(right)
    return product(left_high, right_high) + (
        product(left_low, right_high) + product(left_high, right_low)
    )


def mirrored(distance, count):
    bits = count.bit_length() - 1
    return sum(((distance >> i) & 1) << (bits - 1 - i) for i in range(bits))


def upward_kernel(count, *refs):
    sources = refs[:count]
    payload = refs[count]
    charges, basis, transfer, *lists, matrix, sem = refs[count + 1 :]
    targets = [charges, basis, transfer, matrix] + lists
    copies = [
        pltpu.make_async_copy(source, target, sem.at[i])
        for i, (source, target) in enumerate(zip(sources, targets))
    ]
    for copy in copies:
        copy.start()
    for copy in copies[:2]:
        copy.wait()
    pair_count = charges.shape[0] // 2
    rank = basis.shape[1]
    skeletons = []
    for pair in range(pair_count):
        halves = [
            times_transposed(charges[leaf], basis[leaf]).astype(bf16)
            for leaf in (2 * pair, 2 * pair + 1)
        ]
        skeletons.append(jnp.concatenate(halves, axis=1))
        payload[pair] = skeletons[pair]
    for copy in copies[2:]:
        copy.wait()
    high, low = split(transfer[...].reshape(2 * pair_count * rank, rank))
    row = jnp.concatenate(skeletons, axis=1)
    node = times(row, high) + times(row, low)
    term = exact(times, node, matrix[...])
    payload[pair_count] = jnp.concatenate(split(term), axis=1)


def mark_kernel(*refs):
    pass


def pause_kernel(after, out):
    out[...] = jnp.zeros_like(out)


def near_leaf(near_list, charges, blocks, row, leaf):
    total = None
    for slot in range(blocks.shape[1]):
        part = times_transposed(charges[near_list[slot, leaf]], blocks[row, slot])
        total = part if total is None else total + part
    return total


def near_kernel(leaf_count, list_in, charges, blocks, after, transfer, basis_ready, *refs):
    sources, couplings_in = refs[:4], refs[4]
    near, targets, couplings = refs[5], refs[6:10], refs[10]
    weights, near_list, sem = refs[11:]
    listed = pltpu.make_async_copy(list_in, near_list, sem.at[0])
    listed.start()
    place = lax.axis_index("leaf")
    moves = list(zip(sources, targets))
    for height in range(couplings.shape[0]):
        begin = 2 * leaf_count - 2 * (leaf_count >> height)
        moves.append((couplings_in.at[begin + (place >> height)], couplings.at[height]))
    copies = [
        pltpu.make_async_copy(source, target, sem.at[1 + i])
        for i, (source, target) in enumerate(moves)
    ]
    for copy in copies:
        copy.start()
    weigh(transfer, basis_ready, weights)
    listed.wait()
    for leaf in range(near.shape[0]):
        near[leaf] = near_leaf(near_list, charges, blocks, leaf, leaf)
    for copy in copies:
        copy.wait()


def joined(both):
    both = both.astype(f32)
    rank = both.shape[1] // 2
    return both[:, :rank] + both[:, rank:]


def terms_kernel(own, other, terms):
    last = own.shape[0] - 1
    both = jnp.concatenate([joined(own[last]), joined(other[last])], axis=1)
    terms[...] = both.astype(bf16)


def pair_kernel(mine, theirs, *refs):
    pair, rounded = refs[-2:]
    rank = pair.shape[1] // 2
    odd = lax.axis_index("leaf") % 2 == 1
    far = jnp.where(odd, mine[1], theirs[1])
    flipped = jnp.concatenate([far[:, rank:], far[:, :rank]], axis=1)
    near = jnp.concatenate([mine[0][:, :rank], theirs[0][:, :rank]], axis=1)
    total = near + jnp.where(odd, far, flipped)
    pair[...] = total
    rounded[...] = total.astype(bf16)


def forward_kernel(payload, near, copy):
    copy[...] = payload[pl.ds(0, copy.shape[0])]


def sum_kernel(count, *refs):
    arrays, pairs, sums = refs[:count], refs[count:-2], refs[-1]
    total = None
    for array in arrays:
        part = joined(array[array.shape[0] - 1])
        total = part if total is None else total + part
    sums[0] = jnp.concatenate([total, jnp.zeros_like(total)], axis=1)
    total = jnp.zeros(sums.shape[1:], f32)
    for pair in pairs:
        total = total + pair[...]
    sums[1] = total


def tree_kernel(leaf_count, tree, couplings, matrix, sums, down_high, down_low):
    depth = leaf_count.bit_length() - 2
    place = lax.axis_index("leaf")
    begins = [2 * leaf_count - 2 * (leaf_count >> height) for height in range(depth)]
    back = matrix[...]
    added = []
    for height in range(depth):
        spot = place >> height
        even = spot % 2 == 0
        picks = [(jnp.where(even, 3, 0), spot + jnp.where(even, 3, -3))]
        if height == depth - 1:
            picks.append((jnp.where(spot < 2, 2, 1), spot ^ 2))
        else:
            picks += [(1, spot - 2), (2, spot + 2)]
        added.append([(at, exact(times, back, couplings[height, slot])) for slot, at in picks])
        if height < depth - 1:
            back = exact(times, back, tree[begins[height] + spot])
    nodes = added[-1]
    for height in reversed(range(depth - 1)):
        members = leaf_count >> height
        parts = list(added[height])
        for parent, value in nodes:
            for child in (2 * parent, 2 * parent + 1):
                safe = child if isinstance(child, int) else jnp.clip(child, 0, members - 1)
                product = exact(times_transposed, value, tree[begins[height] + safe])
                parts.append((child, product))
        nodes = []
        for node in range(members):
            total = jnp.zeros(matrix.shape, f32)
            for at, value in parts:
                if isinstance(at, int):
                    total = total + value if at == node else total
                else:
                    total = total + jnp.where(at == node, value, jnp.zeros_like(value))
            nodes.append((node, total))
    for node, value in nodes:
        high, low = split(value)
        down_high[node] = high
        down_low[node] = low


def weigh(transfer, basis, weights):
    for leaf in range(transfer.shape[0]):
        high, low = split(transfer[leaf])
        full = times(high.T, basis[leaf]) + times(low.T, basis[leaf])
        weights[leaf] = full.astype(bf16)


def base_kernel(coupled, basis, near, down_high, down_low, own, *refs):
    pairs, base, part = refs[:-2], refs[-2], refs[-1]
    rank = basis.shape[1]
    for pair in range(coupled.shape[0]):
        both = coupled[pair].astype(bf16)
        for half in range(2):
            leaf = 2 * pair + half
            far = times(both[:, half * rank : (half + 1) * rank], basis[leaf])
            base[leaf] = far + near[leaf]
    place = lax.axis_index("leaf")
    chip, core = place // 2, place % 2
    total = down_product(down_high, down_low, own[...], chip, core)
    for step, pair in enumerate(pairs):
        at = chip ^ (2 + step + len(pairs) * core)
        total = total + down_product(down_high, down_low, pair[...], at, core)
    part[...] = total


def relay_kernel(count, *refs):
    out = refs[-1]
    for i in range(count):
        out[i] = refs[i][...]


def far_kernel(peer_count, list_in, count_in, *refs):
    peers = refs[:peer_count]
    coupling, after, coupled, table = refs[peer_count:]
    far_list, far_count = list_in[...], count_in[...]
    leaves, slots, rank = coupling.shape[0], coupling.shape[1], coupling.shape[2]
    rows = table.shape[1]
    empty = peer_count * leaves
    table[empty] = jnp.zeros(table.shape[1:], bf16)
    odd = lax.axis_index("leaf") % 2 == 1
    for peer in range(peer_count):
        begin = jnp.where(odd, mirrored(peer + 1, peer_count + 1) - 1, peer) * leaves
        for pair in range(leaves // 2):
            block = peers[peer][pair]
            first, second = block[:, :rank], block[:, rank:]
            table[begin + 2 * pair] = jnp.concatenate([first, first], axis=1)
            table[begin + 2 * pair + 1] = jnp.concatenate([second, second], axis=1)
    own = lax.axis_index("list")
    lower = lax.broadcasted_iota(jnp.int32, (rows, 2 * rank), 1) < rank

    def entry(leaf, slot):
        source = far_list[slot, leaf]
        device = source // leaves
        place = ((device ^ own) - 1) * leaves + (source - device * leaves)
        return jnp.where(slot < far_count[0, leaf], place, empty)

    def one(leaf):
        lefts = [
            jnp.where(lower, table[entry(leaf, slot)], table[entry(leaf, slot + 1)])
            for slot in range(0, slots, 2)
        ]
        right = jnp.concatenate(
            [
                jnp.concatenate([coupling[leaf, slot], coupling[leaf, slot + 1]], axis=1)
                for slot in range(0, slots, 2)
            ],
            axis=1,
        )
        return times_transposed(jnp.concatenate(lefts, axis=1), right)

    for pair in range(leaves // 2):
        coupled[pair] = jnp.concatenate([one(2 * pair), one(2 * pair + 1)], axis=1)


def down_product(down_high, down_low, both, chip_at, core):
    first, second = 2 * chip_at + core, 2 * chip_at + 1 - core
    high = jnp.concatenate([down_high[first], down_high[second]], axis=1)
    low = jnp.concatenate([down_low[first], down_low[second]], axis=1)
    if both.dtype == bf16:
        return times_transposed(
            jnp.concatenate([both, both], axis=1), jnp.concatenate([high, low], axis=1)
        )
    both_high, both_low = split(both)
    return times_transposed(
        jnp.concatenate([both_high, both_low, both_high], axis=1),
        jnp.concatenate([high, high, low], axis=1),
    )


def down_kernel(part, beside, swapped, down_high, down_low, weights, base, out, buffer, sem):
    place = lax.axis_index("leaf")
    chip, other = place // 2, 1 - place % 2
    total = part[...]
    total = total + down_product(down_high, down_low, beside[...], chip ^ 1, 1 - other)
    steps = swapped.shape[0]
    for step in range(steps):
        at = chip ^ (2 + step + steps * other)
        total = total + down_product(down_high, down_low, swapped[step], at, other)
    wide = total.astype(bf16)
    copies = []
    group = 8
    for begin in range(0, base.shape[0], group):
        for leaf in range(begin, begin + group):
            buffer[leaf] = (base[leaf] + times(wide, weights[leaf])).astype(bf16)
        rows = pl.ds(begin, group)
        copy = pltpu.make_async_copy(buffer.at[rows], out.at[rows], sem.at[begin // group])
        copy.start()
        copies.append(copy)
    for copy in copies:
        copy.wait()


def on_device(
    panel_charges,
    leaf_basis,
    near_blocks,
    near_list,
    far_list,
    far_count,
    far_coupling,
    leaf_transfer,
    device_transfer,
    tree_transfer,
    level_coupling,
):
    leaves, rows, panels = panel_charges.shape
    rank = leaf_basis.shape[1]
    list_count, leaf_count = lax.axis_size("list"), lax.axis_size("leaf")
    chip_count = leaf_count // 2

    def like(array, dtype=None):
        return jax.ShapeDtypeStruct(array.shape, dtype or array.dtype)

    def shape(*dims, dtype=bf16):
        return jax.ShapeDtypeStruct(dims, dtype)

    def stay(array):
        return pltpu.with_memory_space_constraint(array, pltpu.HBM)

    def exchange(array, axis, distance):
        pairs = [(i, i ^ distance) for i in range(lax.axis_size(axis))]
        return lax.ppermute(array, axis, pairs)

    def spread(array, first, second):
        places = [(l, j) for l in range(leaf_count) for j in range(list_count)]
        ends = [l * list_count + (j ^ (second if l % 2 else first)) for l, j in places]
        return lax.ppermute(array, ("leaf", "list"), list(enumerate(ends)))

    def list_exchange(array, distance):
        return spread(array, distance, mirrored(distance, list_count))

    inputs = [stay(panel_charges), stay(leaf_basis), stay(leaf_transfer)]
    inputs += [stay(device_transfer[0, 0]), near_list.T, far_list.T, far_count[None]]
    count = len(inputs)
    payload, charges, basis, transfer, near_list, far_list, far_count = pl.pallas_call(
        functools.partial(upward_kernel, count),
        out_shape=[
            shape(leaves // 2 + 1, rows, 2 * rank),
            like(panel_charges),
            like(leaf_basis),
            like(leaf_transfer),
            *[like(array) for array in inputs[4:]],
        ],
        in_specs=[anywhere] * count,
        out_specs=[whole] * 7,
        scratch_shapes=[
            pltpu.VMEM((rank, rank), f32),
            pltpu.SemaphoreType.DMA((count,)),
        ],
        compiler_params=params(4),
        name="upward",
    )(*inputs[:4], *[stay(array) for array in inputs[4:]])

    payload = pl.pallas_call(
        mark_kernel,
        out_shape=like(payload),
        in_specs=[anywhere],
        out_specs=anywhere,
        input_output_aliases={0: 0},
        compiler_params=params(1),
        cost_estimate=pl.CostEstimate(
            flops=64 * near_blocks.size * rows,
            bytes_accessed=64 * near_blocks.size,
            transcendentals=0,
        ),
        name="mark",
    )(payload)

    other_payload = exchange(payload, "leaf", 1)
    direct = [distance for distance in range(1, list_count) if distance & (distance - 1) == 0]
    arrived = {distance: list_exchange(payload, distance) for distance in direct}

    terms = pl.pallas_call(
        terms_kernel,
        out_shape=shape(rows, 2 * rank),
        in_specs=[whole] * 2,
        out_specs=whole,
        compiler_params=params(2),
        name="terms",
    )(payload, other_payload)

    far_terms = [
        spread(terms, direct[0], distance)
        for distance in range(1, list_count)
        if distance not in direct
    ]

    depth = leaf_count.bit_length() - 2
    fetched = [tree_transfer, device_transfer[0, 0], leaf_basis, far_coupling]
    near, tree_matrices, device_matrix, basis_later, coupling, couplings, weights = pl.pallas_call(
        functools.partial(near_kernel, leaf_count),
        out_shape=[
            shape(leaves, rows, panels, dtype=f32),
            *[like(array) for array in fetched],
            shape(depth, *level_coupling.shape[1:], dtype=f32),
            shape(leaves, rank, panels),
        ],
        in_specs=[anywhere, whole, whole, anywhere, whole, whole] + [anywhere] * (1 + len(fetched)),
        out_specs=[whole] * (3 + len(fetched)),
        scratch_shapes=[
            pltpu.SMEM(near_list.shape, jnp.int32),
            pltpu.SemaphoreType.DMA((1 + len(fetched) + depth,)),
        ],
        compiler_params=params(12),
        cost_estimate=pl.CostEstimate(
            flops=2 * near_blocks.size * rows,
            bytes_accessed=2 * near_blocks.size,
            transcendentals=0,
        ),
        name="near",
    )(
        near_list,
        charges,
        near_blocks,
        terms,
        transfer,
        basis,
        *[stay(array) for array in fetched],
        stay(level_coupling),
    )

    sums = pl.pallas_call(
        functools.partial(sum_kernel, 1 + len(direct)),
        out_shape=shape(2, rows, 2 * rank, dtype=f32),
        in_specs=[whole] * (1 + len(direct) + len(far_terms)) + [anywhere],
        out_specs=whole,
        compiler_params=params(4),
        name="group_sum",
    )(payload, *[arrived[distance] for distance in direct], *far_terms, near)
    other_sums = exchange(sums, "leaf", 1)

    bases = direct[:-1]
    forward = {}
    for base in bases:
        forward[base] = pl.pallas_call(
            forward_kernel,
            out_shape=shape(leaves // 2, rows, 2 * rank),
            in_specs=[whole, anywhere],
            out_specs=whole,
            compiler_params=params(2),
            name="forward",
        )(arrived[base], sums)

    passed = pl.pallas_call(
        pause_kernel,
        out_shape=shape(8, 128, dtype=f32),
        in_specs=[anywhere],
        out_specs=whole,
        compiler_params=params(1),
        cost_estimate=pl.CostEstimate(
            flops=64 * near_blocks.size * rows,
            bytes_accessed=64 * near_blocks.size,
            transcendentals=0,
        ),
        name="pause",
    )(sums)

    own_pair, rounded_pair = pl.pallas_call(
        pair_kernel,
        out_shape=[shape(rows, 2 * rank, dtype=f32), shape(rows, 2 * rank)],
        in_specs=[whole] * 2 + [anywhere],
        out_specs=[whole] * 2,
        compiler_params=params(2),
        name="pair",
    )(sums, other_sums, passed)

    down_high, down_low = pl.pallas_call(
        functools.partial(tree_kernel, leaf_count),
        out_shape=[
            shape(leaf_count, rank, rank),
            shape(leaf_count, rank, rank),
        ],
        in_specs=[whole] * 3 + [anywhere],
        out_specs=[whole] * 2,
        compiler_params=params(4),
        cost_estimate=pl.CostEstimate(
            flops=64 * near_blocks.size * rows,
            bytes_accessed=64 * near_blocks.size,
            transcendentals=0,
        ),
        name="tree",
    )(tree_matrices, couplings, device_matrix, own_pair)

    steps = (chip_count - 2) // 2
    received = [
        lax.ppermute(
            rounded_pair,
            "leaf",
            [(i, i ^ 2 * (2 + step + steps * (i % 2))) for i in range(leaf_count)],
        )
        for step in range(steps)
    ]
    beside = exchange(rounded_pair, "leaf", 2)

    skeletons = {distance: arrived[distance] for distance in direct}
    for distance in range(1, list_count):
        if distance not in direct:
            top = 1 << (distance.bit_length() - 1)
            forward[distance] = list_exchange(forward[distance ^ top], top)
            skeletons[distance] = forward[distance]

    relayed = pl.pallas_call(
        functools.partial(relay_kernel, steps),
        out_shape=shape(steps, rows, 2 * rank),
        in_specs=[whole] * steps + [anywhere],
        out_specs=whole,
        compiler_params=params(2),
        name="relay",
    )(*received, down_high)
    swapped = exchange(relayed, "leaf", 1)

    coupled = pl.pallas_call(
        functools.partial(far_kernel, list_count - 1),
        out_shape=shape(leaves // 2, rows, 2 * rank, dtype=f32),
        in_specs=[whole] * 2 + [whole] * list_count + [anywhere],
        out_specs=whole,
        scratch_shapes=[
            pltpu.VMEM(((list_count - 1) * leaves + 1, rows, 2 * rank), bf16),
        ],
        compiler_params=params(8),
        cost_estimate=pl.CostEstimate(
            flops=2 * far_coupling.size * rows * 4,
            bytes_accessed=4 * far_coupling.size,
            transcendentals=0,
        ),
        name="far",
    )(
        far_list,
        far_count,
        *[skeletons[distance] for distance in range(1, list_count)],
        coupling,
        relayed,
    )


    base, part = pl.pallas_call(
        base_kernel,
        out_shape=[
            shape(leaves, rows, panels, dtype=f32),
            shape(rows, rank, dtype=f32),
        ],
        in_specs=[whole] * (6 + steps),
        out_specs=[whole] * 2,
        compiler_params=params(4),
        name="base",
    )(coupled, basis_later, near, down_high, down_low, own_pair, *received)

    return pl.pallas_call(
        down_kernel,
        out_shape=shape(leaves, rows, panels),
        in_specs=[whole] * 7,
        out_specs=anywhere,
        scratch_shapes=[
            pltpu.VMEM((leaves, rows, panels), bf16),
            pltpu.SemaphoreType.DMA((leaves // 8,)),
        ],
        compiler_params=params(4),
        name="down",
    )(part, beside, swapped, down_high, down_low, weights, base)


def solution(mesh):
    in_specs = (
        P(("leaf", "list"), None, None),
        P(("leaf", "list"), None, None),
        P(("leaf", "list"), None, None, None),
        P(("leaf", "list"), None),
        P(("leaf", "list"), None),
        P(("leaf", "list")),
        P(("leaf", "list"), None, None, None),
        P(("leaf", "list"), None, None),
        P("leaf", "list", None, None),
        P(),
        P(),
    )
    out_specs = P(("leaf", "list"), None, None)
    return jax.shard_map(
        on_device, mesh=mesh, in_specs=in_specs, out_specs=out_specs, check_vma=False
    )
```

```python
import functools

import jax
import jax.numpy as jnp
from jax import lax
from jax.experimental import pallas as pl
from jax.experimental.pallas import tpu as pltpu
from jax.sharding import PartitionSpec as P

f32 = jnp.float32
bf16 = jnp.bfloat16
whole = pl.BlockSpec(memory_space=pltpu.VMEM)
anywhere = pl.BlockSpec(memory_space=pl.ANY)


def params(mebibytes):
    return pltpu.CompilerParams(vmem_limit_bytes=mebibytes << 20)


def times(left, right):
    return lax.dot_general(left, right, (((1,), (0,)), ((), ())), preferred_element_type=f32)


def times_transposed(left, right):
    return lax.dot_general(left, right, (((1,), (1,)), ((), ())), preferred_element_type=f32)


def split(array):
    high = array.astype(bf16)
    return high, (array - high.astype(f32)).astype(bf16)


def exact(product, left, right):
    left_high, left_low = split(left)
    right_high, right_low = split(right)
    return product(left_high, right_high) + (
        product(left_low, right_high) + product(left_high, right_low)
    )


def mirrored(distance, count):
    bits = count.bit_length() - 1
    return sum(((distance >> i) & 1) << (bits - 1 - i) for i in range(bits))


def upward_kernel(count, *refs):
    sources = refs[:count]
    payload = refs[count]
    charges, basis, transfer, *lists, matrix, sem = refs[count + 1 :]
    targets = [charges, basis, transfer, matrix] + lists
    copies = [
        pltpu.make_async_copy(source, target, sem.at[i])
        for i, (source, target) in enumerate(zip(sources, targets))
    ]
    for copy in copies:
        copy.start()
    for copy in copies[:2]:
        copy.wait()
    pair_count = charges.shape[0] // 2
    rank = basis.shape[1]
    skeletons = []
    for pair in range(pair_count):
        halves = [
            times_transposed(charges[leaf], basis[leaf]).astype(bf16)
            for leaf in (2 * pair, 2 * pair + 1)
        ]
        skeletons.append(jnp.concatenate(halves, axis=1))
        payload[pair] = skeletons[pair]
    for copy in copies[2:]:
        copy.wait()
    high, low = split(transfer[...].reshape(2 * pair_count * rank, rank))
    row = jnp.concatenate(skeletons, axis=1)
    node = times(row, high) + times(row, low)
    term = exact(times, node, matrix[...])
    payload[pair_count] = jnp.concatenate(split(term), axis=1)


def mark_kernel(*refs):
    pass


def pause_kernel(after, out):
    out[...] = jnp.zeros_like(out)


def near_leaf(near_list, charges, blocks, row, leaf):
    total = None
    for slot in range(blocks.shape[1]):
        part = times_transposed(charges[near_list[slot, leaf]], blocks[row, slot])
        total = part if total is None else total + part
    return total


def near_kernel(leaf_count, list_in, charges, blocks, after, transfer, basis_ready, *refs):
    sources, couplings_in = refs[:4], refs[4]
    near, targets, couplings = refs[5], refs[6:10], refs[10]
    weights, near_list, sem = refs[11:]
    listed = pltpu.make_async_copy(list_in, near_list, sem.at[0])
    listed.start()
    place = lax.axis_index("leaf")
    moves = list(zip(sources, targets))
    for height in range(couplings.shape[0]):
        begin = 2 * leaf_count - 2 * (leaf_count >> height)
        moves.append((couplings_in.at[begin + (place >> height)], couplings.at[height]))
    copies = [
        pltpu.make_async_copy(source, target, sem.at[1 + i])
        for i, (source, target) in enumerate(moves)
    ]
    for copy in copies:
        copy.start()
    weigh(transfer, basis_ready, weights)
    listed.wait()
    for leaf in range(near.shape[0]):
        near[leaf] = near_leaf(near_list, charges, blocks, leaf, leaf)
    for copy in copies:
        copy.wait()


def joined(both):
    both = both.astype(f32)
    rank = both.shape[1] // 2
    return both[:, :rank] + both[:, rank:]


def terms_kernel(own, other, terms):
    last = own.shape[0] - 1
    rank = terms.shape[1] // 2
    terms[...] = jnp.concatenate([own[last][:, :rank], other[last][:, :rank]], axis=1)


def pair_kernel(mine, theirs, *refs):
    pair, rounded = refs[-2:]
    rank = pair.shape[1] // 2
    odd = lax.axis_index("leaf") % 2 == 1
    far = jnp.where(odd, mine[1], theirs[1])
    flipped = jnp.concatenate([far[:, rank:], far[:, :rank]], axis=1)
    near = jnp.concatenate([mine[0][:, :rank], theirs[0][:, :rank]], axis=1)
    total = near + jnp.where(odd, far, flipped)
    pair[...] = total
    rounded[...] = total.astype(bf16)


def forward_kernel(payload, near, copy):
    copy[...] = payload[pl.ds(0, copy.shape[0])]


def sum_kernel(count, *refs):
    arrays, pairs, sums = refs[:count], refs[count:-2], refs[-1]
    total = None
    for array in arrays:
        part = joined(array[array.shape[0] - 1])
        total = part if total is None else total + part
    sums[0] = jnp.concatenate([total, jnp.zeros_like(total)], axis=1)
    total = jnp.zeros(sums.shape[1:], f32)
    for pair in pairs:
        total = total + pair[...]
    sums[1] = total


def tree_kernel(leaf_count, tree, couplings, matrix, sums, down_high, down_low):
    depth = leaf_count.bit_length() - 2
    place = lax.axis_index("leaf")
    begins = [2 * leaf_count - 2 * (leaf_count >> height) for height in range(depth)]
    back = matrix[...]
    added = []
    for height in range(depth):
        spot = place >> height
        even = spot % 2 == 0
        picks = [(jnp.where(even, 3, 0), spot + jnp.where(even, 3, -3))]
        if height == depth - 1:
            picks.append((jnp.where(spot < 2, 2, 1), spot ^ 2))
        else:
            picks += [(1, spot - 2), (2, spot + 2)]
        added.append([(at, exact(times, back, couplings[height, slot])) for slot, at in picks])
        if height < depth - 1:
            back = exact(times, back, tree[begins[height] + spot])
    nodes = added[-1]
    for height in reversed(range(depth - 1)):
        members = leaf_count >> height
        parts = list(added[height])
        for parent, value in nodes:
            for child in (2 * parent, 2 * parent + 1):
                safe = child if isinstance(child, int) else jnp.clip(child, 0, members - 1)
                product = exact(times_transposed, value, tree[begins[height] + safe])
                parts.append((child, product))
        nodes = []
        for node in range(members):
            total = jnp.zeros(matrix.shape, f32)
            for at, value in parts:
                if isinstance(at, int):
                    total = total + value if at == node else total
                else:
                    total = total + jnp.where(at == node, value, jnp.zeros_like(value))
            nodes.append((node, total))
    for node, value in nodes:
        high, low = split(value)
        down_high[node] = high
        down_low[node] = low


def weigh(transfer, basis, weights):
    for leaf in range(transfer.shape[0]):
        high, low = split(transfer[leaf])
        full = times(high.T, basis[leaf]) + times(low.T, basis[leaf])
        weights[leaf] = full.astype(bf16)


def base_kernel(coupled, basis, near, down_high, down_low, own, *refs):
    pairs, base, part = refs[:-2], refs[-2], refs[-1]
    rank = basis.shape[1]
    for pair in range(coupled.shape[0]):
        both = coupled[pair].astype(bf16)
        for half in range(2):
            leaf = 2 * pair + half
            far = times(both[:, half * rank : (half + 1) * rank], basis[leaf])
            base[leaf] = far + near[leaf]
    place = lax.axis_index("leaf")
    chip, core = place // 2, place % 2
    total = down_product(down_high, down_low, own[...], chip, core)
    for step, pair in enumerate(pairs):
        at = chip ^ (2 + step + len(pairs) * core)
        total = total + down_product(down_high, down_low, pair[...], at, core)
    part[...] = total


def relay_kernel(count, *refs):
    out = refs[-1]
    for i in range(count):
        out[i] = refs[i][...]


def far_kernel(peer_count, list_in, count_in, *refs):
    peers = refs[:peer_count]
    coupling, after, coupled, table = refs[peer_count:]
    far_list, far_count = list_in[...], count_in[...]
    leaves, slots, rank = coupling.shape[0], coupling.shape[1], coupling.shape[2]
    rows = table.shape[1]
    empty = peer_count * leaves
    table[empty] = jnp.zeros(table.shape[1:], bf16)
    odd = lax.axis_index("leaf") % 2 == 1
    for peer in range(peer_count):
        begin = jnp.where(odd, mirrored(peer + 1, peer_count + 1) - 1, peer) * leaves
        for pair in range(leaves // 2):
            block = peers[peer][pair]
            first, second = block[:, :rank], block[:, rank:]
            table[begin + 2 * pair] = jnp.concatenate([first, first], axis=1)
            table[begin + 2 * pair + 1] = jnp.concatenate([second, second], axis=1)
    own = lax.axis_index("list")
    lower = lax.broadcasted_iota(jnp.int32, (rows, 2 * rank), 1) < rank

    def entry(leaf, slot):
        source = far_list[slot, leaf]
        device = source // leaves
        place = ((device ^ own) - 1) * leaves + (source - device * leaves)
        return jnp.where(slot < far_count[0, leaf], place, empty)

    def one(leaf):
        lefts = [
            jnp.where(lower, table[entry(leaf, slot)], table[entry(leaf, slot + 1)])
            for slot in range(0, slots, 2)
        ]
        right = jnp.concatenate(
            [
                jnp.concatenate([coupling[leaf, slot], coupling[leaf, slot + 1]], axis=1)
                for slot in range(0, slots, 2)
            ],
            axis=1,
        )
        return times_transposed(jnp.concatenate(lefts, axis=1), right)

    for pair in range(leaves // 2):
        coupled[pair] = jnp.concatenate([one(2 * pair), one(2 * pair + 1)], axis=1)


def down_product(down_high, down_low, both, chip_at, core):
    first, second = 2 * chip_at + core, 2 * chip_at + 1 - core
    high = jnp.concatenate([down_high[first], down_high[second]], axis=1)
    low = jnp.concatenate([down_low[first], down_low[second]], axis=1)
    if both.dtype == bf16:
        return times_transposed(
            jnp.concatenate([both, both], axis=1), jnp.concatenate([high, low], axis=1)
        )
    both_high, both_low = split(both)
    return times_transposed(
        jnp.concatenate([both_high, both_low, both_high], axis=1),
        jnp.concatenate([high, high, low], axis=1),
    )


def down_kernel(part, beside, swapped, down_high, down_low, weights, base, out, buffer, sem):
    place = lax.axis_index("leaf")
    chip, other = place // 2, 1 - place % 2
    total = part[...]
    total = total + down_product(down_high, down_low, beside[...], chip ^ 1, 1 - other)
    steps = swapped.shape[0]
    for step in range(steps):
        at = chip ^ (2 + step + steps * other)
        total = total + down_product(down_high, down_low, swapped[step], at, other)
    wide = total.astype(bf16)
    copies = []
    group = 8
    for begin in range(0, base.shape[0], group):
        for leaf in range(begin, begin + group):
            buffer[leaf] = (base[leaf] + times(wide, weights[leaf])).astype(bf16)
        rows = pl.ds(begin, group)
        copy = pltpu.make_async_copy(buffer.at[rows], out.at[rows], sem.at[begin // group])
        copy.start()
        copies.append(copy)
    for copy in copies:
        copy.wait()


def on_device(
    panel_charges,
    leaf_basis,
    near_blocks,
    near_list,
    far_list,
    far_count,
    far_coupling,
    leaf_transfer,
    device_transfer,
    tree_transfer,
    level_coupling,
):
    leaves, rows, panels = panel_charges.shape
    rank = leaf_basis.shape[1]
    list_count, leaf_count = lax.axis_size("list"), lax.axis_size("leaf")
    chip_count = leaf_count // 2

    def like(array, dtype=None):
        return jax.ShapeDtypeStruct(array.shape, dtype or array.dtype)

    def shape(*dims, dtype=bf16):
        return jax.ShapeDtypeStruct(dims, dtype)

    def stay(array):
        return pltpu.with_memory_space_constraint(array, pltpu.HBM)

    def exchange(array, axis, distance):
        pairs = [(i, i ^ distance) for i in range(lax.axis_size(axis))]
        return lax.ppermute(array, axis, pairs)

    def spread(array, first, second):
        places = [(l, j) for l in range(leaf_count) for j in range(list_count)]
        ends = [l * list_count + (j ^ (second if l % 2 else first)) for l, j in places]
        return lax.ppermute(array, ("leaf", "list"), list(enumerate(ends)))

    def list_exchange(array, distance):
        return spread(array, distance, mirrored(distance, list_count))

    inputs = [stay(panel_charges), stay(leaf_basis), stay(leaf_transfer)]
    inputs += [stay(device_transfer[0, 0]), near_list.T, far_list.T, far_count[None]]
    count = len(inputs)
    payload, charges, basis, transfer, near_list, far_list, far_count = pl.pallas_call(
        functools.partial(upward_kernel, count),
        out_shape=[
            shape(leaves // 2 + 1, rows, 2 * rank),
            like(panel_charges),
            like(leaf_basis),
            like(leaf_transfer),
            *[like(array) for array in inputs[4:]],
        ],
        in_specs=[anywhere] * count,
        out_specs=[whole] * 7,
        scratch_shapes=[
            pltpu.VMEM((rank, rank), f32),
            pltpu.SemaphoreType.DMA((count,)),
        ],
        compiler_params=params(4),
        name="upward",
    )(*inputs[:4], *[stay(array) for array in inputs[4:]])

    payload = pl.pallas_call(
        mark_kernel,
        out_shape=like(payload),
        in_specs=[anywhere],
        out_specs=anywhere,
        input_output_aliases={0: 0},
        compiler_params=params(1),
        cost_estimate=pl.CostEstimate(
            flops=64 * near_blocks.size * rows,
            bytes_accessed=64 * near_blocks.size,
            transcendentals=0,
        ),
        name="mark",
    )(payload)

    other_payload = exchange(payload, "leaf", 1)
    direct = [distance for distance in range(1, list_count) if distance & (distance - 1) == 0]
    arrived = {distance: list_exchange(payload, distance) for distance in direct}

    terms = pl.pallas_call(
        terms_kernel,
        out_shape=shape(rows, 2 * rank),
        in_specs=[whole] * 2,
        out_specs=whole,
        compiler_params=params(2),
        name="terms",
    )(payload, other_payload)

    far_terms = [
        spread(terms, direct[0], distance)
        for distance in range(1, list_count)
        if distance not in direct
    ]

    depth = leaf_count.bit_length() - 2
    fetched = [tree_transfer, device_transfer[0, 0], leaf_basis, far_coupling]
    near, tree_matrices, device_matrix, basis_later, coupling, couplings, weights = pl.pallas_call(
        functools.partial(near_kernel, leaf_count),
        out_shape=[
            shape(leaves, rows, panels, dtype=f32),
            *[like(array) for array in fetched],
            shape(depth, *level_coupling.shape[1:], dtype=f32),
            shape(leaves, rank, panels),
        ],
        in_specs=[anywhere, whole, whole, anywhere, whole, whole] + [anywhere] * (1 + len(fetched)),
        out_specs=[whole] * (3 + len(fetched)),
        scratch_shapes=[
            pltpu.SMEM(near_list.shape, jnp.int32),
            pltpu.SemaphoreType.DMA((1 + len(fetched) + depth,)),
        ],
        compiler_params=params(12),
        cost_estimate=pl.CostEstimate(
            flops=2 * near_blocks.size * rows,
            bytes_accessed=2 * near_blocks.size,
            transcendentals=0,
        ),
        name="near",
    )(
        near_list,
        charges,
        near_blocks,
        terms,
        transfer,
        basis,
        *[stay(array) for array in fetched],
        stay(level_coupling),
    )

    sums = pl.pallas_call(
        functools.partial(sum_kernel, 1 + len(direct)),
        out_shape=shape(2, rows, 2 * rank, dtype=f32),
        in_specs=[whole] * (1 + len(direct) + len(far_terms)) + [anywhere],
        out_specs=whole,
        compiler_params=params(4),
        name="group_sum",
    )(payload, *[arrived[distance] for distance in direct], *far_terms, near)
    other_sums = exchange(sums, "leaf", 1)

    bases = direct[:-1]
    forward = {}
    for base in bases:
        forward[base] = pl.pallas_call(
            forward_kernel,
            out_shape=shape(leaves // 2, rows, 2 * rank),
            in_specs=[whole, anywhere],
            out_specs=whole,
            compiler_params=params(2),
            name="forward",
        )(arrived[base], sums)

    passed = pl.pallas_call(
        pause_kernel,
        out_shape=shape(8, 128, dtype=f32),
        in_specs=[anywhere],
        out_specs=whole,
        compiler_params=params(1),
        cost_estimate=pl.CostEstimate(
            flops=64 * near_blocks.size * rows,
            bytes_accessed=64 * near_blocks.size,
            transcendentals=0,
        ),
        name="pause",
    )(sums)

    own_pair, rounded_pair = pl.pallas_call(
        pair_kernel,
        out_shape=[shape(rows, 2 * rank, dtype=f32), shape(rows, 2 * rank)],
        in_specs=[whole] * 2 + [anywhere],
        out_specs=[whole] * 2,
        compiler_params=params(2),
        name="pair",
    )(sums, other_sums, passed)

    down_high, down_low = pl.pallas_call(
        functools.partial(tree_kernel, leaf_count),
        out_shape=[
            shape(leaf_count, rank, rank),
            shape(leaf_count, rank, rank),
        ],
        in_specs=[whole] * 3 + [anywhere],
        out_specs=[whole] * 2,
        compiler_params=params(4),
        cost_estimate=pl.CostEstimate(
            flops=64 * near_blocks.size * rows,
            bytes_accessed=64 * near_blocks.size,
            transcendentals=0,
        ),
        name="tree",
    )(tree_matrices, couplings, device_matrix, own_pair)

    steps = (chip_count - 2) // 2
    received = [
        lax.ppermute(
            rounded_pair,
            "leaf",
            [(i, i ^ 2 * (2 + step + steps * (i % 2))) for i in range(leaf_count)],
        )
        for step in range(steps)
    ]
    beside = exchange(own_pair, "leaf", 2)

    skeletons = {distance: arrived[distance] for distance in direct}
    for distance in range(1, list_count):
        if distance not in direct:
            top = 1 << (distance.bit_length() - 1)
            forward[distance] = list_exchange(forward[distance ^ top], top)
            skeletons[distance] = forward[distance]

    relayed = pl.pallas_call(
        functools.partial(relay_kernel, steps),
        out_shape=shape(steps, rows, 2 * rank),
        in_specs=[whole] * steps + [anywhere],
        out_specs=whole,
        compiler_params=params(2),
        name="relay",
    )(*received, down_high)
    swapped = exchange(relayed, "leaf", 1)

    coupled = pl.pallas_call(
        functools.partial(far_kernel, list_count - 1),
        out_shape=shape(leaves // 2, rows, 2 * rank, dtype=f32),
        in_specs=[whole] * 2 + [whole] * list_count + [anywhere],
        out_specs=whole,
        scratch_shapes=[
            pltpu.VMEM(((list_count - 1) * leaves + 1, rows, 2 * rank), bf16),
        ],
        compiler_params=params(8),
        cost_estimate=pl.CostEstimate(
            flops=2 * far_coupling.size * rows * 4,
            bytes_accessed=4 * far_coupling.size,
            transcendentals=0,
        ),
        name="far",
    )(
        far_list,
        far_count,
        *[skeletons[distance] for distance in range(1, list_count)],
        coupling,
        relayed,
    )


    base, part = pl.pallas_call(
        base_kernel,
        out_shape=[
            shape(leaves, rows, panels, dtype=f32),
            shape(rows, rank, dtype=f32),
        ],
        in_specs=[whole] * (6 + steps),
        out_specs=[whole] * 2,
        compiler_params=params(4),
        name="base",
    )(coupled, basis_later, near, down_high, down_low, own_pair, *received)

    return pl.pallas_call(
        down_kernel,
        out_shape=shape(leaves, rows, panels),
        in_specs=[whole] * 7,
        out_specs=anywhere,
        scratch_shapes=[
            pltpu.VMEM((leaves, rows, panels), bf16),
            pltpu.SemaphoreType.DMA((leaves // 8,)),
        ],
        compiler_params=params(4),
        name="down",
    )(part, beside, swapped, down_high, down_low, weights, base)


def solution(mesh):
    in_specs = (
        P(("leaf", "list"), None, None),
        P(("leaf", "list"), None, None),
        P(("leaf", "list"), None, None, None),
        P(("leaf", "list"), None),
        P(("leaf", "list"), None),
        P(("leaf", "list")),
        P(("leaf", "list"), None, None, None),
        P(("leaf", "list"), None, None),
        P("leaf", "list", None, None),
        P(),
        P(),
    )
    out_specs = P(("leaf", "list"), None, None)
    return jax.shard_map(
        on_device, mesh=mesh, in_specs=in_specs, out_specs=out_specs, check_vma=False
    )
```
